32 devices in a mesh: section: 2 (over y), dp: 16 (over z, x, core).
Axes of the slice: x: 2, y: 2, z: 4, core: 2. Of those that a mesh axis runs over, the one named last changes fastest.
Arguments:
- stream_in: bfloat16 [32, 1024, 767], P('dp')
- cotangent: bfloat16 [32, 1024, 767], P('dp'), may hold values from -6 to 6
- weights_first: bfloat16 [2, 768, 3072], P('section')
- down_weight: bfloat16 [3072, 768], replicated, may hold values from -0.1875 to 0.1875
- segments: int32 [32, 1024], P('dp'), may hold values from 0 to 4, as said below
Outputs:
- stream_out: bfloat16 [2, 32, 1024, 767], P('section', 'dp')
- stream_grad: bfloat16 [2, 32, 1024, 767], P('section', 'dp')
- grad_first: float32 [2, 768, 3072], P('section')
- grad_down: float32 [3072, 768], P('section')
- residual_rms: float32 [2], P('section')
- token_count: int32 [2], P('section')
The draws below stay inside these ranges and needn't reach their ends.
Inputs may be any that keep to these rules, and one draw needn't show every extreme that they name: `segments`: each row holds documents numbered in order up to 4, the last of them present in every row, over its first 512 positions or more; the rest of the row is padding with id 0.
All inputs are finite; a program needn't handle non-finite values.
Results may differ from the reference program's by a relative error of at most 0.013.
Values may be sent and summed in bfloat16 or wider, within the bound.
No kernel may reach another device: no remote copies, remote signals or barrier semaphores. Data moves between devices by JAX's collectives and lax.ppermute only.
A program may use at most 320 MiB of HBM per device.

```python
import math
import jax
import jax.numpy as jnp
from jax import lax

D = 768
HEADS = 12
HEAD_DIM = 64
FF = 3072
SEQ = 1024
DOCS = 4
NROWS = 32


def draw_stream_in(key, part):
    key = jax.random.fold_in(key, 11)
    subkeys = jax.random.split(key, 3)
    shape_full = (NROWS, SEQ, D - 1)
    rising = jnp.power(3.0, jnp.arange(NROWS, dtype=jnp.float32) / max(NROWS - 1, 1)).reshape(NROWS, 1, 1)
    token_scale = jnp.exp(jax.random.uniform(subkeys[1], (NROWS, SEQ, 1), minval=math.log(0.3), maxval=math.log(3.0)))
    feature_scale = jnp.exp(jax.random.uniform(subkeys[2], (1, 1, D - 1), minval=math.log(0.3), maxval=math.log(3.0)))
    base = jax.random.normal(subkeys[0], shape_full)
    return (0.6 * base * token_scale * feature_scale * rising).astype(jnp.bfloat16)


def draw_weights_first(key, part):
    key = jax.random.fold_in(key, 7)
    base = jax.random.normal(key, (2, D, 4 * D))
    columns = jnp.arange(4 * D)
    attention_scale = jnp.where(columns < 2 * D, 1.3, jnp.where(columns < 3 * D, 1.0, 2.5))
    column_scale = jnp.stack([attention_scale, jnp.ones_like(attention_scale)])[:, None, :]
    return (base * column_scale * D ** (-0.5)).astype(jnp.bfloat16)


def draw_segments(key, part):
    key = jax.random.fold_in(key, 23)
    subkeys = jax.random.split(key, 2)
    filled = jax.random.randint(subkeys[0], (NROWS, 1), SEQ // 2, SEQ + 1)
    shares = jax.random.randint(subkeys[1], (NROWS, DOCS), 20, 101)
    running = jnp.cumsum(shares, axis=1)
    bounds = filled * running[:, :DOCS - 1] // running[:, DOCS - 1:]
    positions = jnp.arange(SEQ)
    labels = 1 + jnp.sum((positions[None, :, None] >= bounds[:, None, :]).astype(jnp.int32), axis=-1)
    return jnp.where(positions[None, :] < filled, labels, 0).astype(jnp.int32)


def block_levels(stream_key, extent, cuts, least, top_value):
    factor_of, own = 1.0, jax.random.fold_in(stream_key, 6)
    for axis_at, shards_of in cuts:
        heights = jnp.exp(jax.random.uniform(jax.random.fold_in(own, axis_at), (shards_of,), jnp.float32, least / len(cuts), top_value / len(cuts)))
        factor_of = factor_of * jnp.repeat(heights, extent[axis_at] // shards_of).reshape([-1 if axis == axis_at else 1 for axis in range(len(extent))])
    return factor_of


def scatter_about(rng, extent, spread, limit, shards=(), kind=jnp.bfloat16):
    array = spread * jax.random.normal(rng, extent, jnp.float32)
    if shards:
        array = array * block_levels(rng, extent, shards, -0.22, 0.18)
    return jnp.clip(array, -limit, limit).astype(kind)


def setup_inputs(seed: int = 0) -> dict:
    keys = jax.random.split(jax.random.key(seed), 6)
    stream_in = draw_stream_in(jax.random.fold_in(keys[5], 71), 0)
    cotangent = scatter_about(keys[1], (NROWS, SEQ, D - 1), 1.0, 6.0, ((0, 16),))
    weights_first = draw_weights_first(jax.random.fold_in(keys[5], 71), 0)
    down_weight = scatter_about(keys[3], (FF, D), (FF // 3) ** -0.5, 0.1875)
    segments = draw_segments(jax.random.fold_in(keys[5], 71), 0)
    return {"stream_in": stream_in, "cotangent": cotangent, "weights_first": weights_first, "down_weight": down_weight, "segments": segments}


EPSILON = 1e-06
MASKED = -1e+30

@jax.custom_vjp
def low(v):
    return lax.optimization_barrier(v.astype(jnp.bfloat16)).astype(jnp.float32)

@jax.custom_vjp
def low_back(v):
    return v

def low_keep(v):
    return (low(v), None)

def low_pass(kept, grad):
    return (grad,)

def back_keep(v):
    return (v, None)

def back_low(kept, grad):
    return (low(grad),)
low.defvjp(low_keep, low_pass)
low_back.defvjp(back_keep, back_low)

def widen(compact):
    return jnp.concatenate([compact, -lax.optimization_barrier(jnp.sum(compact, axis=-1, keepdims=True))], axis=-1)

def normalize(values):
    return values * lax.rsqrt(lax.optimization_barrier(jnp.mean(values * values, axis=-1, keepdims=True)) + EPSILON)

def compress(branch):
    return (branch - lax.optimization_barrier(jnp.mean(branch, axis=-1, keepdims=True)))[..., :-1]

def matmul_high(left, right):
    return jnp.matmul(left, right, precision=lax.Precision.HIGHEST)

def row_attention(operands):
    queries, key_rows, values, segment_row = operands
    length = segment_row.shape[0]
    positions = jnp.arange(length)
    allowed = (segment_row[:, None] == segment_row[None, :]) & (positions[None, :] <= positions[:, None])
    scores = jnp.einsum('qhd,khd->hqk', queries, key_rows, precision=lax.Precision.HIGHEST) * HEAD_DIM ** (-0.5)
    scores = low_back(scores)
    scores = jnp.where(allowed[None], scores, MASKED)
    highest = lax.optimization_barrier(jnp.max(scores, axis=-1, keepdims=True))
    exponent = jnp.exp(scores - highest)
    probs = low(exponent / lax.optimization_barrier(jnp.sum(exponent, axis=-1, keepdims=True)))
    return jnp.einsum('hqk,khd->qhd', probs, values, precision=lax.Precision.HIGHEST)

def forward(compact, attn_weights, up_weights, down_weights, probe, segment_rows):
    group_rows = compact.shape[0]
    normed = normalize(widen(compact))
    packed = low_back(low(matmul_high(low(normed), attn_weights[:, :3 * D])))
    heads = [packed[..., member * D:(member + 1) * D].reshape(group_rows, SEQ, HEADS, HEAD_DIM) for member in range(3)]
    mixed = lax.map(jax.checkpoint(row_attention), (heads[0], heads[1], heads[2], segment_rows))
    mixed = low_back(low(mixed.reshape(group_rows, SEQ, D)))
    branch = low_back(matmul_high(mixed, attn_weights[:, 3 * D:]))
    middle = low(compact + compress(branch))
    middle = low_back(middle + probe)
    normed_mid = normalize(widen(middle))
    hidden = low_back(matmul_high(low(normed_mid), up_weights))
    activated = low(jax.nn.gelu(hidden, approximate=True))
    branch_mlp = low_back(matmul_high(activated, down_weights))
    return (middle, middle + compress(branch_mlp))

def square_total(rows, valid):
    totals = lax.optimization_barrier(jnp.sum(rows * rows, axis=-1)) + jnp.square(lax.optimization_barrier(jnp.sum(rows, axis=-1)))
    return jnp.sum(jnp.where(valid, totals, 0.0))

def reference(stream_in, cotangent, weights_first, down_weight, segments):
    per_group = math.gcd(NROWS, max(1, 4096 // SEQ))
    steps_count = NROWS // per_group
    attn_weights = weights_first[0].astype(jnp.float32)
    up_weights = weights_first[1].astype(jnp.float32)
    down_weights = down_weight.astype(jnp.float32)
    compact_all = stream_in.astype(jnp.float32).reshape(steps_count, per_group, SEQ, D - 1)
    cot_all = cotangent.astype(jnp.float32).reshape(steps_count, per_group, SEQ, D - 1)
    segment_all = segments.reshape(steps_count, per_group, SEQ)

    def accumulate(carried, item):
        compact, grad_out, segment_rows = item

        def run(comp, attn, upper, lower, probe):
            return forward(comp, attn, upper, lower, probe, segment_rows)
        (middle, output), pullback = jax.vjp(run, compact, attn_weights, up_weights, down_weights, jnp.zeros_like(compact))
        grad_in, grad_attn, grad_up, grad_lower, grad_mid = pullback((jnp.zeros_like(middle), grad_out))
        output_low = output.astype(jnp.bfloat16)
        valid = segment_rows > 0
        first_sq = square_total(middle, valid)
        second_sq = square_total(output_low.astype(jnp.float32), valid)
        counted = jnp.sum(valid.astype(jnp.float32))
        updated = (carried[0] + grad_attn, carried[1] + grad_up, carried[2] + grad_lower, carried[3] + first_sq, carried[4] + second_sq, carried[5] + counted)
        return (updated, (middle.astype(jnp.bfloat16), output_low, grad_in.astype(jnp.bfloat16), grad_mid.astype(jnp.bfloat16)))
    initial = (jnp.zeros((D, 4 * D), jnp.float32), jnp.zeros((D, FF), jnp.float32), jnp.zeros((FF, D), jnp.float32), jnp.zeros((), jnp.float32), jnp.zeros((), jnp.float32), jnp.zeros((), jnp.float32))
    totals, stacked = lax.scan(accumulate, initial, (compact_all, cot_all, segment_all))
    shaped = [member.reshape(NROWS, SEQ, D - 1) for member in stacked]
    stream_out = jnp.stack([shaped[0], shaped[1]])
    stream_grad = jnp.stack([shaped[2], shaped[3]])
    grad_first = jnp.stack([totals[0], totals[1]])
    grad_down = totals[2]
    residual_rms = jnp.sqrt(jnp.stack([totals[3], totals[4]]) / (totals[5] * D))
    slots = jnp.float32(NROWS * SEQ)
    token_count = jnp.stack([totals[5], slots - totals[5]]).astype(jnp.int32)
    return (stream_out, stream_grad, grad_first, grad_down, residual_rms, token_count)
```

```python
import functools

import jax
import jax.numpy as jnp
from jax import lax
from jax.experimental import pallas as pl
from jax.experimental.pallas import tpu as pltpu
from jax.sharding import PartitionSpec as P

HEADS = 12
HEAD_DIM = 64
GROUPS = 3
EPSILON = 1e-06
MASKED = -1e30
SCALE = HEAD_DIM ** (-0.5)
LOG2E = 1.4426950408889634
LOW = jnp.bfloat16
FULL = jnp.float32
VMEM = 58 * 2**20


def dot(left, right, left_dim=1, right_dim=0):
    return lax.dot_general(
        left, right, (((left_dim,), (right_dim,)), ((), ())), preferred_element_type=FULL
    )


def kernel_call(body, name, grid_spec, out_shape, flops, moved, exps=0, aliases=None):
    return pl.pallas_call(
        body,
        grid_spec=grid_spec,
        out_shape=out_shape,
        input_output_aliases=aliases or {},
        compiler_params=pltpu.CompilerParams(vmem_limit_bytes=VMEM),
        cost_estimate=pl.CostEstimate(flops=int(flops), bytes_accessed=int(moved), transcendentals=int(exps)),
        name=name,
    )


def widened(block):
    lane = lax.broadcasted_iota(jnp.int32, block.shape, 1)
    last = block.shape[1] - 1
    values = jnp.where(lane == last, 0.0, block.astype(FULL))
    return jnp.where(lane == last, -jnp.sum(values, axis=1, keepdims=True), values)


def crms(values):
    inverse = lax.rsqrt(jnp.mean(values * values, axis=1, keepdims=True) + EPSILON)
    return values * inverse, inverse


def crms_back(normed, inverse, grad):
    return inverse * (grad - normed * jnp.mean(grad * normed, axis=1, keepdims=True))


def compressed(branch):
    return branch - jnp.mean(branch, axis=1, keepdims=True)


def widened_back(grad):
    last = grad.shape[1] - 1
    return grad - grad[:, last:]


def compressed_back(block):
    lane = lax.broadcasted_iota(jnp.int32, block.shape, 1)
    values = jnp.where(lane == block.shape[1] - 1, 0.0, block.astype(FULL))
    return values - jnp.mean(values, axis=1, keepdims=True)


def square_sum(rounded, valid_row):
    wide = widened(rounded)
    per_token = jnp.sum(wide * wide, axis=1, keepdims=True)
    tokens = valid_row.shape[1]
    valid = jnp.transpose(jnp.broadcast_to(valid_row, (128, tokens)))[:, :1]
    return jnp.sum(jnp.where(valid > 0.5, per_token, 0.0), axis=0, keepdims=True)


def prep_kernel(where_ref, x_ref, cot_ref, nt_ref, g_ref):
    normed, _ = crms(widened(x_ref[0]))
    nt_ref[...] = jnp.transpose(normed.astype(LOW))
    g_ref[...] = compressed_back(cot_ref[0]).astype(LOW)


def prep(where, stream_in, cotangent):
    length, width = stream_in.shape[1], stream_in.shape[2] + 1
    block = length // 4
    return kernel_call(
        prep_kernel,
        "prep",
        pltpu.PrefetchScalarGridSpec(
            num_scalar_prefetch=1,
            grid=(4,),
            in_specs=[
                pl.BlockSpec((1, block, width), lambda t, w: (w[0], t, 0)),
                pl.BlockSpec((1, block, width), lambda t, w: (w[0], t, 0)),
            ],
            out_specs=[
                pl.BlockSpec((width, block), lambda t, w: (0, t)),
                pl.BlockSpec((block, width), lambda t, w: (t, 0)),
            ],
        ),
        [jax.ShapeDtypeStruct((width, length), LOW), jax.ShapeDtypeStruct((length, width), LOW)],
        0,
        8 * length * width,
    )(where, stream_in, cotangent)


def branch_grad_kernel(g_ref, w_ref, out_ref):
    out_ref[0] = dot(g_ref[...], w_ref[...], 1, 1).astype(LOW)


def branch_grad(g, down_weight):
    length, width = g.shape
    blocks = down_weight.shape[0] // width
    return kernel_call(
        branch_grad_kernel,
        "branch_grad",
        pltpu.PrefetchScalarGridSpec(
            num_scalar_prefetch=0,
            grid=(blocks,),
            in_specs=[
                pl.BlockSpec((length, width), lambda b: (0, 0)),
                pl.BlockSpec((width, width), lambda b: (b, 0)),
            ],
            out_specs=pl.BlockSpec((1, length, width), lambda b: (b, 0, 0)),
        ),
        jax.ShapeDtypeStruct((blocks, length, width), LOW),
        2 * length * width * width * blocks,
        2 * length * width * (blocks + 1),
    )(g, down_weight)


def own_column(group, piece, section):
    attention = jnp.where(group < GROUPS, group + GROUPS * piece, 3 * GROUPS + piece)
    return jnp.where(section == 0, attention, 3 * group + piece)


def own_column_static(group, piece, section):
    if section == 1 or group == GROUPS:
        return 3 * group + piece
    return group + GROUPS * piece


def piece_kernel(where_ref, w_ref, out_ref):
    out_ref[0] = w_ref[0]


def weight_piece(where, weights):
    rows, columns = weights.shape[1:]
    part = columns // 12
    return kernel_call(
        piece_kernel,
        "weight_piece",
        pltpu.PrefetchScalarGridSpec(
            num_scalar_prefetch=1,
            grid=(4, 3),
            in_specs=[pl.BlockSpec((1, rows // 4, part), lambda g, j, w: (0, w[1], own_column(g, j, w[0])))],
            out_specs=pl.BlockSpec((1, rows // 4, part), lambda g, j, w: (g, 0, j)),
        ),
        jax.ShapeDtypeStruct((4, rows // 4, 3 * part), LOW),
        0,
        rows * columns,
    )(where, weights)


def weight_copies(group, wanted, where_ref, own_ref, near_ref, beside_ref, core_ref, target, sem, act):
    quarter = target.shape[0] // 4
    part = target.shape[1] // 3

    @pl.when(where_ref[0] == wanted)
    def _():
        for piece in range(3):
            column = own_column_static(group, piece, wanted) * part
            act(pltpu.make_async_copy(own_ref.at[0, :, pl.ds(column, part)], target.at[:, pl.ds(piece * part, part)], sem.at[piece]))

    @pl.when(where_ref[0] != wanted)
    def _():
        sources = (near_ref, beside_ref, core_ref.at[0], core_ref.at[1])
        for place, source in enumerate(sources):
            index = where_ref[1] ^ (0, 2, 1, 3)[place]
            act(pltpu.make_async_copy(source, target.at[pl.ds(index * quarter, quarter), :], sem.at[place]))


def segment_rows(segment):
    tokens = segment.shape[1]
    ids = lax.broadcasted_iota(jnp.int32, (16, tokens), 0)
    same = segment == ids
    real = ids < 5
    queries = jnp.where(real & jnp.logical_not(same), MASKED, 0.0).astype(LOW)
    keys = jnp.where(real & same, 1.0, 0.0).astype(LOW)
    return queries, keys


def two_parts(values):
    high = values.astype(LOW)
    return high, (values - high.astype(FULL)).astype(LOW)


def minus_rows(values):
    high = values.astype(LOW)
    rest = values - high.astype(FULL)
    middle = rest.astype(LOW)
    low = rest - middle.astype(FULL)
    row = lax.broadcasted_iota(jnp.int32, (16, values.shape[1]), 0)
    parts = jnp.where(
        row == 0, high.astype(FULL), jnp.where(row == 1, middle.astype(FULL), jnp.where(row == 2, low, 0.0))
    )
    return (-parts).astype(LOW)


def three_ones(tokens):
    return jnp.where(lax.broadcasted_iota(jnp.int32, (16, tokens), 0) < 3, 1.0, 0.0).astype(LOW)


def head_tasks(heads, blocks, block):
    return [
        (head, slice(i * block, (i + 1) * block), slice(0, (i + 1) * block), i * block)
        for head in range(heads)
        for i in range(blocks)
    ]


def in_stages(tasks, stages):
    for step in range(len(tasks) + len(stages) - 1):
        for late, stage in enumerate(stages):
            if 0 <= step - late < len(tasks):
                stage(tasks[step - late])


def attend_kernel(group, where_ref, own_ref, near_ref, beside_ref, core_ref, nt_ref, seg_ref, qkv_ref, mixed_ref, total_ref, w_ref, sem):
    copies = functools.partial(
        weight_copies, group, 0, where_ref, own_ref, near_ref, beside_ref, core_ref, w_ref, sem
    )
    copies(lambda c: c.start())
    copies(lambda c: c.wait())
    length = nt_ref.shape[1]
    width = qkv_ref.shape[0] // 3
    heads, blocks = width // HEAD_DIM, 4
    block = length // blocks
    for part in range(3):
        qkv_ref[part * width : (part + 1) * width, :] = dot(
            w_ref[:, part * width : (part + 1) * width], nt_ref[...], 0, 0
        ).astype(LOW)
    seg_queries, seg_keys = segment_rows(seg_ref[0])
    causal = lax.broadcasted_iota(jnp.int32, (block, block), 0) <= lax.broadcasted_iota(jnp.int32, (block, block), 1)
    ones = three_ones(length)
    scored, weighed = {}, {}

    def score(task):
        head, queries, keys, _ = task
        high, low = two_parts(qkv_ref[head * HEAD_DIM : (head + 1) * HEAD_DIM, queries].astype(FULL) * (SCALE * LOG2E))
        key_rows = qkv_ref[width + head * HEAD_DIM : width + (head + 1) * HEAD_DIM, keys]
        scored[task] = dot(
            jnp.concatenate([key_rows, key_rows, seg_keys[:, keys]], axis=0),
            jnp.concatenate([high, low, seg_queries[:, queries]], axis=0),
            0,
            0,
        )

    def weigh(task):
        before = task[3]
        scores = scored.pop(task)
        last = jnp.where(causal, scores[before:], MASKED)
        highest = jnp.max(last, axis=0, keepdims=True)
        if before:
            highest = jnp.maximum(highest, jnp.max(scores[:before], axis=0, keepdims=True))
        exponents = jnp.exp2(last - highest).astype(LOW)
        if before:
            exponents = jnp.concatenate([jnp.exp2(scores[:before] - highest).astype(LOW), exponents], axis=0)
        weighed[task] = (exponents, highest)

    def mix(task):
        head, queries, keys, _ = task
        exponents, highest = weighed.pop(task)
        values = qkv_ref[2 * width + head * HEAD_DIM : 2 * width + (head + 1) * HEAD_DIM, keys]
        mixed = dot(jnp.concatenate([values, ones[:, keys]], axis=0), exponents)
        total = mixed[HEAD_DIM : HEAD_DIM + 1]
        mixed_ref[head * HEAD_DIM : (head + 1) * HEAD_DIM, queries] = (mixed[:HEAD_DIM] / total).astype(LOW)
        total_ref[head : head + 1, queries] = highest + jnp.log2(total)

    in_stages(head_tasks(heads, blocks, block), (score, weigh, mix))


def attend(group, where, own, received, nt, segments):
    width, length = nt.shape
    part = width // GROUPS
    anywhere = pl.BlockSpec(memory_space=pl.ANY)
    return kernel_call(
        functools.partial(attend_kernel, group),
        "attend",
        pltpu.PrefetchScalarGridSpec(
            num_scalar_prefetch=1,
            grid=(1,),
            in_specs=[anywhere] * 4
            + [
                pl.BlockSpec((width, length), lambda i, w: (0, 0)),
                pl.BlockSpec((1, 1, length), lambda i, w: (w[0], 0, 0)),
            ],
            out_specs=[
                pl.BlockSpec((3 * part, length), lambda i, w: (0, 0)),
                pl.BlockSpec((part, length), lambda i, w: (0, 0)),
                pl.BlockSpec((part // HEAD_DIM, length), lambda i, w: (0, 0)),
                pl.BlockSpec((width, 3 * part), lambda i, w: (0, 0)),
            ],
            scratch_shapes=[pltpu.SemaphoreType.DMA((4,))],
        ),
        [
            jax.ShapeDtypeStruct((3 * part, length), LOW),
            jax.ShapeDtypeStruct((part, length), LOW),
            jax.ShapeDtypeStruct((part // HEAD_DIM, length), FULL),
            jax.ShapeDtypeStruct((width, 3 * part), LOW),
        ],
        4.5e9,
        8 * width * length,
    )(where, own, *received, nt, segments)


def attend_back_kernel(qkv_ref, gm_ref, total_ref, delta_ref, seg_ref, w_ref, nt_ref, *rest):
    before_refs, (gw_ref, gn_ref, acc) = rest[:-3], rest[-3:]
    length = nt_ref.shape[1]
    width = gm_ref.shape[0]
    heads, blocks = width // HEAD_DIM, 4
    block = length // blocks
    seg_queries, seg_keys = segment_rows(seg_ref[0])
    ones = three_ones(length)
    causal = lax.broadcasted_iota(jnp.int32, (block, block), 1) <= lax.broadcasted_iota(jnp.int32, (block, block), 0)
    acc[...] = jnp.zeros_like(acc)
    scored, weighed = {}, {}

    def rows(part, head):
        return slice(part * width + head * HEAD_DIM, part * width + (head + 1) * HEAD_DIM)

    def score(task):
        head, queries, keys, _ = task
        high, low = two_parts(qkv_ref[rows(0, head), queries].astype(FULL) * (SCALE * LOG2E))
        key_rows = qkv_ref[rows(1, head), keys]
        scores = dot(
            jnp.concatenate([high, low, seg_queries[:, queries], minus_rows(total_ref[head : head + 1, queries])], axis=0),
            jnp.concatenate([key_rows, key_rows, seg_keys[:, keys], ones[:, keys]], axis=0),
            0,
            0,
        )
        grads = dot(
            jnp.concatenate([gm_ref[rows(0, head), queries], minus_rows(delta_ref[head : head + 1, queries])], axis=0),
            jnp.concatenate([qkv_ref[rows(2, head), keys], ones[:, keys]], axis=0),
            0,
            0,
        )
        scored[task] = (scores, grads)

    def weigh(task):
        before = task[3]
        scores, grads = scored.pop(task)
        last = jnp.where(causal, scores[:, before:], MASKED)
        if before:
            last = jnp.concatenate([scores[:, :before], last], axis=1)
        probs = jnp.exp2(last)
        weighed[task] = (probs.astype(LOW), (probs * grads).astype(LOW))

    def collect(task):
        head, queries, keys, _ = task
        probs, grads = weighed.pop(task)
        acc[rows(2, head), keys] += dot(gm_ref[rows(0, head), queries], probs)
        acc[rows(1, head), keys] += dot(qkv_ref[rows(0, head), queries] * LOW(SCALE), grads)
        acc[rows(0, head), queries] = dot(qkv_ref[rows(1, head), keys], grads, 1, 1) * SCALE

    in_stages(head_tasks(heads, blocks, block), (score, weigh, collect))
    grads = acc[...].astype(LOW)
    gw_ref[...] = dot(nt_ref[...], grads, 1, 1).astype(LOW)
    grad_normed = dot(w_ref[...], grads)
    if before_refs:
        grad_normed = grad_normed + before_refs[0][...]
    gn_ref[...] = grad_normed


def attend_back(where, qkv, gm, total, delta, segments, w, nt, before=None):
    width, length = nt.shape
    part = gm.shape[0]
    whole = lambda a: pl.BlockSpec(a.shape, lambda i, w: (0,) * a.ndim)
    arrays = [qkv, gm, total, delta]
    extra = [] if before is None else [before]

    def body(where_ref, *refs):
        attend_back_kernel(*refs)

    return kernel_call(
        body,
        "attend_back",
        pltpu.PrefetchScalarGridSpec(
            num_scalar_prefetch=1,
            grid=(1,),
            in_specs=[whole(a) for a in arrays]
            + [pl.BlockSpec((1, 1, length), lambda i, w: (w[0], 0, 0)), whole(w), whole(nt)]
            + [whole(a) for a in extra],
            out_specs=[
                pl.BlockSpec((width, 3 * part), lambda i, w: (0, 0)),
                pl.BlockSpec((width, length), lambda i, w: (0, 0)),
            ],
            scratch_shapes=[pltpu.VMEM((3 * part, length), FULL)],
        ),
        [jax.ShapeDtypeStruct((width, 3 * part), LOW), jax.ShapeDtypeStruct((width, length), FULL)],
        9e9,
        8 * width * length,
    )(where, *arrays, segments, w, nt, *extra)


def middle_kernel(where_ref, own_ref, near_ref, beside_ref, core_ref, *refs):
    mixed_refs, (x_ref, seg_ref, mid_ref, nm_ref, nmt_ref, sums_ref, w_ref, sem) = refs[:GROUPS], refs[GROUPS:]
    step = pl.program_id(0)

    @pl.when(step == 0)
    def _():
        copies = functools.partial(
            weight_copies, GROUPS, 0, where_ref, own_ref, near_ref, beside_ref, core_ref, w_ref, sem
        )
        copies(lambda c: c.start())
        copies(lambda c: c.wait())
        sums_ref[...] = jnp.zeros_like(sums_ref)

    mixed = jnp.concatenate([ref[...] for ref in mixed_refs], axis=0)
    branch = dot(mixed, w_ref[...], 0, 0)
    middle = (x_ref[0].astype(FULL) + compressed(branch)).astype(LOW)
    mid_ref[...] = middle
    normed, _ = crms(widened(middle))
    low = normed.astype(LOW)
    nm_ref[...] = low
    nmt_ref[...] = jnp.transpose(low)
    valid = (seg_ref[0] > 0).astype(FULL)
    lane = lax.broadcasted_iota(jnp.int32, sums_ref.shape, 1)
    count = jnp.sum(valid, axis=1, keepdims=True)
    sums_ref[...] += jnp.where(lane == 0, square_sum(middle, valid), 0.0) + jnp.where(lane == 2, count, 0.0)


def middle_of(where, own, received, mixed, stream_in, segments):
    length, width = stream_in.shape[1], stream_in.shape[2] + 1
    block = length // 4
    anywhere = pl.BlockSpec(memory_space=pl.ANY)
    return kernel_call(
        middle_kernel,
        "middle",
        pltpu.PrefetchScalarGridSpec(
            num_scalar_prefetch=1,
            grid=(4,),
            in_specs=[anywhere] * 4
            + [pl.BlockSpec((width // GROUPS, block), lambda t, w: (0, t))] * GROUPS
            + [
                pl.BlockSpec((1, block, width), lambda t, w: (w[0], t, 0)),
                pl.BlockSpec((1, 1, block), lambda t, w: (w[0], 0, t)),
            ],
            out_specs=[
                pl.BlockSpec((block, width), lambda t, w: (t, 0)),
                pl.BlockSpec((block, width), lambda t, w: (t, 0)),
                pl.BlockSpec((width, block), lambda t, w: (0, t)),
                pl.BlockSpec((8, 128), lambda t, w: (0, 0)),
                pl.BlockSpec((width, width), lambda t, w: (0, 0)),
            ],
            scratch_shapes=[pltpu.SemaphoreType.DMA((4,))],
        ),
        [
            jax.ShapeDtypeStruct((length, width - 1), LOW),
            jax.ShapeDtypeStruct((length, width), LOW),
            jax.ShapeDtypeStruct((width, length), LOW),
            jax.ShapeDtypeStruct((8, 128), FULL),
            jax.ShapeDtypeStruct((width, width), LOW),
        ],
        2 * length * width * width,
        12 * length * width,
    )(where, own, *received, *mixed, stream_in, segments)


def gelu_both(hidden):
    rate = 0.7978845608028654
    square = hidden * hidden
    tanh = jnp.tanh(rate * hidden * (1.0 + 0.044715 * square))
    half = 0.5 + 0.5 * tanh
    slope = half + (0.5 * rate) * hidden * (1.0 - tanh * tanh) * (1.0 + (3 * 0.044715) * square)
    return hidden * half, slope


def feed_kernel(where_ref, own_ref, *refs):
    received, refs = refs[:12], refs[12:]
    (nm_ref, nmt_ref, g_ref, ga_ref, down_ref, mid_ref, cot_ref, seg_ref) = refs[:8]
    (keep_dn, send_dn, keep_up, send_up, keep_out, send_out, gmid_ref, gab_ref, sums_ref) = refs[8:17]
    (weights, act, slope_grad, out_acc, gn_acc, sem) = refs[17:]
    step, steps = pl.program_id(0), pl.num_programs(0)
    length, width = nm_ref.shape
    blocks = 4
    block = length // blocks

    def copies(group, do):
        weight_copies(
            group, 1, where_ref, own_ref, *received[3 * group : 3 * group + 3], weights.at[group], sem.at[group], do
        )

    @pl.when(step == 0)
    def _():
        for group in range(4):
            copies(group, lambda c: c.start())
        out_acc[...] = jnp.zeros_like(out_acc)
        gn_acc[...] = jnp.zeros_like(gn_acc)

    for group in range(4):

        @pl.when(step == group)
        def _(group=group):
            copies(group, lambda c: c.wait())

    up = weights.at[step]
    hidden, waiting = {}, {}

    def enter(rows):
        hidden[rows] = dot(nm_ref[rows, :], up[...])

    def bend(rows):
        value, slope = gelu_both(hidden.pop(rows))
        act[rows, :] = value.astype(LOW)
        slope_grad[rows, :] = (ga_ref[0, rows, :].astype(FULL) * slope).astype(LOW)

    def leave(rows):
        out_acc[rows, :] += dot(act[rows, :], down_ref[...])
        gn_acc[rows, :] += dot(slope_grad[rows, :], up[...], 1, 1)

    in_stages([slice(i * block, (i + 1) * block) for i in range(blocks)], (enter, bend, leave))
    half = width // 2
    mine = pl.multiple_of(where_ref[2] * half, half)
    theirs = pl.multiple_of((1 - where_ref[2]) * half, half)
    keep_dn[0] = dot(act[:, pl.ds(mine, half)], g_ref[...], 0, 0).astype(LOW)
    send_dn[0] = dot(act[:, pl.ds(theirs, half)], g_ref[...], 0, 0).astype(LOW)
    keep_up[0] = dot(nmt_ref[pl.ds(mine, half), :], slope_grad[...]).astype(LOW)
    send_up[0] = dot(nmt_ref[pl.ds(theirs, half), :], slope_grad[...]).astype(LOW)

    @pl.when(step == steps - 1)
    def _():
        on_attention = where_ref[0] == 0
        sums = jnp.zeros((1, 1), FULL)
        for i in range(blocks):
            rows = slice(i * block, (i + 1) * block)
            middle = mid_ref[rows, :]
            wide = widened(middle)
            output = (wide + compressed(out_acc[rows, :])).astype(LOW)
            sums = sums + square_sum(output, (seg_ref[0][:, rows] > 0).astype(FULL))
            keep_out[rows, :] = jnp.where(on_attention, middle, output)
            send_out[rows, :] = jnp.where(on_attention, output, middle)
            normed, inverse = crms(wide)
            grad = (
                cot_ref[0, rows, :].astype(FULL) + widened_back(crms_back(normed, inverse, gn_acc[rows, :]))
            ).astype(LOW)
            gmid_ref[rows, :] = grad
            gab_ref[rows, :] = compressed_back(grad).astype(LOW)
        lane = lax.broadcasted_iota(jnp.int32, sums_ref.shape, 1)
        sums_ref[...] = jnp.where(lane == 1, sums, 0.0)


def feed(where, own, received, nm, nmt, g, ga, down_weight, middle, cotangent, segments):
    length, width = nm.shape
    groups = down_weight.shape[0] // width
    half = width // 2
    anywhere = pl.BlockSpec(memory_space=pl.ANY)
    once = pl.Buffered(1)
    fixed = lambda shape: pl.BlockSpec(shape, lambda b, w: (0,) * len(shape), pipeline_mode=once)
    per_group = lambda *shape: pl.BlockSpec((1, *shape), lambda b, w: (b, 0, 0))
    row = pl.BlockSpec((1, length, width), lambda b, w: (w[0], 0, 0), pipeline_mode=once)
    return kernel_call(
        feed_kernel,
        "feed",
        pltpu.PrefetchScalarGridSpec(
            num_scalar_prefetch=1,
            grid=(groups,),
            in_specs=[anywhere] * 13
            + [
                fixed((length, width)),
                fixed((width, length)),
                fixed((length, width)),
                per_group(length, width),
                pl.BlockSpec((width, width), lambda b, w: (b, 0)),
                fixed((length, width)),
                row,
                pl.BlockSpec((1, 1, length), lambda b, w: (w[0], 0, 0)),
            ],
            out_specs=[per_group(half, width)] * 4
            + [
                fixed((length, width)),
                fixed((length, width)),
                fixed((length, width)),
                fixed((length, width)),
                pl.BlockSpec((8, 128), lambda b, w: (0, 0)),
            ],
            scratch_shapes=[
                pltpu.VMEM((groups, width, width), LOW),
                pltpu.VMEM((length, width), LOW),
                pltpu.VMEM((length, width), LOW),
                pltpu.VMEM((length, width), FULL),
                pltpu.VMEM((length, width), FULL),
                pltpu.SemaphoreType.DMA((groups, 4)),
            ],
        ),
        [jax.ShapeDtypeStruct((groups, half, width), LOW)] * 4
        + [jax.ShapeDtypeStruct((length, width - 1), LOW)] * 3
        + [jax.ShapeDtypeStruct((length, width), LOW), jax.ShapeDtypeStruct((8, 128), FULL)],
        32e9,
        30 * length * width,
    )(where, own, *[a for r in received for a in r], nm, nmt, g, ga, down_weight, middle, cotangent, segments)


def mixed_grad_kernel(gab_ref, w_ref, *refs):
    mixed_refs, (gm_refs, delta_ref, gw_ref) = refs[:GROUPS], (refs[GROUPS : 2 * GROUPS], *refs[2 * GROUPS :])
    gab = gab_ref[...]
    part = gm_refs[0].shape[0]
    heads = part // HEAD_DIM
    for group in range(GROUPS):
        grads = dot(w_ref[group * part : (group + 1) * part, :], gab, 1, 1).astype(LOW)
        gm_refs[group][...] = grads
        mixed = mixed_refs[group][...]
        product = grads.astype(FULL) * mixed.astype(FULL)
        for head in range(heads):
            at = group * heads + head
            delta_ref[at : at + 1, :] = jnp.sum(
                product[head * HEAD_DIM : (head + 1) * HEAD_DIM], axis=0, keepdims=True
            )
        gw_ref[group * part : (group + 1) * part, :] = dot(mixed, gab).astype(LOW)


def mixed_grad(gab, w, mixed):
    length, width = gab.shape
    part = width // GROUPS
    whole = lambda shape: pl.BlockSpec(shape, lambda i: (0,) * len(shape))
    outs = kernel_call(
        mixed_grad_kernel,
        "mixed_grad",
        pltpu.PrefetchScalarGridSpec(
            num_scalar_prefetch=0,
            grid=(1,),
            in_specs=[whole((length, width)), whole((width, width))] + [whole((part, length))] * GROUPS,
            out_specs=[whole((part, length))] * GROUPS + [whole((HEADS, length)), whole((width, width))],
        ),
        [jax.ShapeDtypeStruct((part, length), LOW)] * GROUPS
        + [jax.ShapeDtypeStruct((HEADS, length), FULL), jax.ShapeDtypeStruct((width, width), LOW)],
        4 * length * width * width,
        8 * length * width,
    )(gab, w, *mixed)
    return outs[:GROUPS], outs[GROUPS], outs[GROUPS + 1]


def input_grad_kernel(where_ref, x_ref, gmid_ref, gn_ref, keep_ref, send_ref):
    on_attention = where_ref[0] == 0
    normed, inverse = crms(widened(x_ref[0]))
    middle = gmid_ref[...]
    grad = (
        middle.astype(FULL) + widened_back(crms_back(normed, inverse, jnp.transpose(gn_ref[...])))
    ).astype(LOW)
    keep_ref[...] = jnp.where(on_attention, grad, middle)
    send_ref[...] = jnp.where(on_attention, middle, grad)


def input_grad(where, stream_in, grad_middle, grad_normed):
    length, width = stream_in.shape[1], stream_in.shape[2] + 1
    block = length // 4
    tokens = pl.BlockSpec((block, width), lambda t, w: (t, 0))
    return kernel_call(
        input_grad_kernel,
        "input_grad",
        pltpu.PrefetchScalarGridSpec(
            num_scalar_prefetch=1,
            grid=(4,),
            in_specs=[
                pl.BlockSpec((1, block, width), lambda t, w: (w[0], t, 0)),
                tokens,
                pl.BlockSpec((width, block), lambda t, w: (0, t)),
            ],
            out_specs=[tokens, tokens],
        ),
        [jax.ShapeDtypeStruct((length, width - 1), LOW)] * 2,
        0,
        12 * length * width,
    )(where, stream_in, grad_middle, grad_normed)


def partner(block, distance):
    size = lax.axis_size("dp")
    return lax.ppermute(block, "dp", [(i, i ^ distance) for i in range(size)])


def across(block):
    return lax.ppermute(block, "section", [(0, 1), (1, 0)])


def halve(held, distance):
    bit = (lax.axis_index("dp") & distance) // distance
    half = held.shape[1] // 2
    mine = lax.dynamic_slice_in_dim(held, bit * half, half, 1)
    theirs = lax.dynamic_slice_in_dim(held, (1 - bit) * half, half, 1)
    return add_low(mine, partner(theirs, distance))


def add_low(left, right):
    return (left.astype(FULL) + right.astype(FULL)).astype(LOW)


def scatter(held, order):
    for distance in order:
        held = halve(held, distance)
    return held


def gather(shard, order):
    held = shard[None]
    for distance in reversed(order):
        held = jnp.concatenate([held, partner(held, distance)], axis=0)
    return held


def places(order):
    me = lax.axis_index("dp")
    count = len(order)
    numbers = []
    for entry in range(1 << count):
        other = 0
        for place, distance in enumerate(reversed(order)):
            if entry >> place & 1:
                other |= distance
        device = me ^ other
        number = jnp.int32(0)
        for place, distance in enumerate(order):
            number = number + ((device // distance) & 1) * (1 << (count - 1 - place))
        numbers.append(number)
    return jnp.stack(numbers).astype(jnp.int32)


def down_sum_kernel(place_ref, in_ref, out_ref):
    rows = out_ref.shape[2]
    for block in range(out_ref.shape[0]):
        out_ref[block, 0] = in_ref[0, block * rows : (block + 1) * rows, :].astype(FULL)


def down_sum(place, gathered, width):
    entries, held = gathered.shape[:2]
    rows = width // entries
    blocks = 2
    out = kernel_call(
        down_sum_kernel,
        "down_sum",
        pltpu.PrefetchScalarGridSpec(
            num_scalar_prefetch=1,
            grid=(entries,),
            in_specs=[pl.BlockSpec((1, held, width), lambda e, p: (e, 0, 0))],
            out_specs=pl.BlockSpec((blocks, 1, rows, width), lambda e, p: (0, p[e], 0, 0)),
        ),
        jax.ShapeDtypeStruct((blocks, entries, rows, width), FULL),
        0,
        6 * blocks * width * width,
    )(place, gathered)
    return out.reshape(blocks * width, width)


def first_sum_kernel(place_ref, a_ref, b_ref, out_ref):
    rows, columns = out_ref.shape[1:]
    width = columns // 4
    part = width // 3

    def block(number):
        if number < 3:
            return a_ref[0, number * rows : (number + 1) * rows, :].astype(FULL)
        return b_ref[0].astype(FULL)

    @pl.when(place_ref[0] == 0)
    def _():
        out_ref[0, :, 3 * width :] = block(0)
        for group in range(GROUPS):
            values = block(group + 1)
            for piece in range(3):
                column = own_column_static(group, piece, 0) * part
                out_ref[0, :, column : column + part] = values[:, piece * part : (piece + 1) * part]

    @pl.when(place_ref[0] == 1)
    def _():
        for group in range(4):
            out_ref[0, :, group * width : (group + 1) * width] = block(group)


def first_sum(place, a, b, width):
    entries = a.shape[0]
    rows = width // entries
    out = kernel_call(
        first_sum_kernel,
        "first_sum",
        pltpu.PrefetchScalarGridSpec(
            num_scalar_prefetch=1,
            grid=(entries,),
            in_specs=[
                pl.BlockSpec((1, 3 * rows, width), lambda e, p: (e, 0, 0)),
                pl.BlockSpec((1, rows, width), lambda e, p: (e, 0, 0)),
            ],
            out_specs=pl.BlockSpec((1, rows, 4 * width), lambda e, p: (p[e + 1], 0, 0)),
        ),
        jax.ShapeDtypeStruct((entries, rows, 4 * width), FULL),
        0,
        24 * width * width,
    )(place, a, b)
    return out.reshape(width, 4 * width)


def on_device(stream_in, cotangent, weights_first, down_weight, segments):
    rows_dev, length, compact_width = stream_in.shape
    width = compact_width + 1
    section = lax.axis_index("section").astype(jnp.int32)
    index = lax.axis_index("dp").astype(jnp.int32)
    size = lax.axis_size("dp")
    on_attention = section == 0
    where = jnp.stack([section, index & 3, index & 1])
    segments3 = segments.reshape(rows_dev, 1, length)
    bits = [1 << i for i in range(1, size.bit_length() - 1)]
    orders = ([1] + bits, [1] + bits[1:] + bits[:1])

    piece = weight_piece(where, weights_first)
    received = []
    for group in range(4):
        near = across(piece[group])
        beside = partner(near, 2)
        received.append((near, beside, partner(jnp.stack([near, beside]), 1)))

    nt, g = prep(where, stream_in, cotangent)
    ga = branch_grad(g, down_weight)
    attended = [attend(group, where, weights_first, received[group], nt, segments3) for group in range(GROUPS)]
    mixed = [a[1] for a in attended]
    middle, nm, nmt, sums_mid, out_weights = middle_of(
        where, weights_first, received[GROUPS], mixed, stream_in, segments3
    )
    (keep_dn, send_dn, keep_up, send_up, keep_out, send_out, grad_mid, gab, sums_out) = feed(
        where, weights_first, received, nm, nmt, g, ga, down_weight, middle, cotangent, segments3
    )
    received_out = across(send_out)

    dn = scatter(add_low(keep_dn, partner(send_dn, 1)), orders[0][1:])
    up = scatter(add_low(keep_up, partner(send_up, 1)), orders[1][1:])

    gm, delta, gw_out = mixed_grad(gab, out_weights, mixed)
    heads = HEADS // GROUPS
    grad_normed = None
    grads = []
    for group in range(GROUPS):
        qkv, _, total, w = attended[group]
        gw, grad_normed = attend_back(
            where, qkv, gm[group], total, delta[group * heads : (group + 1) * heads], segments3, w, nt, grad_normed
        )
        grads.append(gw)
    keep_grad, send_grad = input_grad(where, stream_in, grad_mid, grad_normed)
    received_grad = across(send_grad)

    rows = dn.shape[1]
    flat = lambda a: a.reshape(-1, width)
    scalars = (sums_mid + sums_out)[0, :3]

    def scalar_rows(values):
        high = values.astype(LOW)
        rest = values - high.astype(FULL)
        middle_part = rest.astype(LOW)
        low = (rest - middle_part.astype(FULL)).astype(LOW)
        packed = jnp.concatenate([high, middle_part, low])
        return jnp.zeros((16, width), LOW).at[0, :9].set(packed)

    def scalars_of(block):
        parts = block[..., 0, :9].astype(FULL)
        return parts[..., :3] + parts[..., 3:6] + parts[..., 6:9]

    lower, upper = flat(dn[:2]), flat(dn[2:])
    mine = jnp.concatenate([jnp.where(on_attention, lower, upper), flat(up)])
    theirs = jnp.concatenate([jnp.where(on_attention, upper, lower), flat(up), scalar_rows(scalars)])
    swapped = across(theirs)
    shard = add_low(mine, swapped[:-16])
    pair = scalars + scalars_of(swapped[-16:])
    dn_rows = 2 * rows

    attn_a = scatter(jnp.stack([gw_out] + grads[:2]), orders[1])
    attn_b = scatter(jnp.stack(grads[2:]), orders[1])
    attn = jnp.concatenate([flat(attn_a), flat(attn_b)])
    attn = add_low(attn, across(attn))
    first_a = jnp.where(on_attention, attn[: 3 * rows], shard[dn_rows : dn_rows + 3 * rows])
    first_b = jnp.where(on_attention, attn[3 * rows :], shard[dn_rows + 3 * rows :])
    down_all = gather(jnp.concatenate([shard[:dn_rows], scalar_rows(pair)]), orders[0])
    grad_down = down_sum(places(orders[0]), down_all, width)
    grad_first = first_sum(
        jnp.concatenate([section[None], places(orders[1])]), gather(first_a, orders[1]), gather(first_b, orders[1]), width
    )
    totals = jnp.sum(scalars_of(down_all[:, dn_rows:]), axis=0)
    square = jnp.where(on_attention, totals[0], totals[1])
    residual_rms = jnp.sqrt(square / (totals[2] * width)).reshape(1)
    slots = jnp.float32(rows_dev * length * size)
    token_count = jnp.where(on_attention, totals[2], slots - totals[2]).astype(jnp.int32).reshape(1)

    def stacked(kept, other):
        return jnp.where(on_attention, jnp.stack([kept, other]), jnp.stack([other, kept]))[None]

    return (
        stacked(keep_out, received_out),
        stacked(keep_grad, received_grad),
        grad_first[None],
        grad_down,
        residual_rms,
        token_count,
    )


def solution(mesh):
    placed = (
        P("dp", None, None),
        P("dp", None, None),
        P("section", None, None),
        P(),
        P("dp", None),
    )
    return jax.shard_map(
        on_device,
        mesh=mesh,
        in_specs=placed,
        out_specs=(
            P("section", "dp", None, None),
            P("section", "dp", None, None),
            P("section", None, None),
            P("section", None),
            P("section"),
            P("section"),
        ),
        check_vma=False,
    )
```

```python
import functools

import jax
import jax.numpy as jnp
from jax import lax
from jax.experimental import pallas as pl
from jax.experimental.pallas import tpu as pltpu
from jax.sharding import PartitionSpec as P

HEADS = 12
HEAD_DIM = 64
GROUPS = 3
EPSILON = 1e-06
MASKED = -1e30
SCALE = HEAD_DIM ** (-0.5)
LOG2E = 1.4426950408889634
LOW = jnp.bfloat16
FULL = jnp.float32


def dot(left, right, left_dim=1, right_dim=0):
    return lax.dot_general(
        left, right, (((left_dim,), (right_dim,)), ((), ())), preferred_element_type=FULL
    )


def kernel_call(body, name, grid_spec, out_shape, flops, moved, vmem=32):
    return pl.pallas_call(
        body,
        grid_spec=grid_spec,
        out_shape=out_shape,
        compiler_params=pltpu.CompilerParams(vmem_limit_bytes=vmem * 2**20),
        cost_estimate=pl.CostEstimate(flops=int(flops * 3), bytes_accessed=int(moved * 3), transcendentals=0),
        name=name,
    )


def last_row(block):
    return lax.broadcasted_iota(jnp.int32, block.shape, 0) == block.shape[0] - 1


def widened(block):
    values = jnp.where(last_row(block), 0.0, block.astype(FULL))
    return jnp.where(last_row(block), -jnp.sum(values, axis=0, keepdims=True), values)


def crms(values):
    inverse = lax.rsqrt(jnp.mean(values * values, axis=0, keepdims=True) + EPSILON)
    return values * inverse, inverse


def crms_back(normed, inverse, grad):
    return inverse * (grad - normed * jnp.mean(grad * normed, axis=0, keepdims=True))


def compressed(branch):
    return branch - jnp.mean(branch, axis=0, keepdims=True)


def widened_back(grad):
    return grad - grad[grad.shape[0] - 1 :]


def compressed_back(block):
    values = jnp.where(last_row(block), 0.0, block.astype(FULL))
    return values - jnp.mean(values, axis=0, keepdims=True)


def square_sum(rounded, valid):
    wide = widened(rounded)
    per_token = jnp.sum(wide * wide, axis=0, keepdims=True)
    return jnp.sum(jnp.where(valid, per_token, 0.0), axis=1, keepdims=True)


def prep_kernel(where_ref, x_ref, cot_ref, nt_ref, g_ref):
    normed, _ = crms(widened(x_ref[0]))
    nt_ref[...] = normed.astype(LOW)
    g_ref[...] = compressed_back(cot_ref[0]).astype(LOW)


def tokens_spec(width, block):
    return pl.BlockSpec((width, block), lambda t, *_: (0, t))


def row_spec(width, block):
    return pl.BlockSpec((1, width, block), lambda t, w: (w[0], 0, t))


def prep(where, x, cot):
    width, length = x.shape[1] + 1, x.shape[2]
    spec = tokens_spec(width, length // 4)
    return kernel_call(
        prep_kernel,
        "prep",
        pltpu.PrefetchScalarGridSpec(
            num_scalar_prefetch=1, grid=(4,), in_specs=[row_spec(width, length // 4)] * 2, out_specs=[spec] * 2
        ),
        [jax.ShapeDtypeStruct((width, length), LOW)] * 2,
        0,
        8 * length * width,
        vmem=16,
    )(where, x, cot)


def branch_grad_kernel(g_ref, w_ref, *refs):
    out_ref = refs[-1]
    out_ref[0] = dot(w_ref[...], g_ref[...]).astype(LOW)


def branch_grad(g, down_weight, after=()):
    width, length = g.shape
    blocks = down_weight.shape[0] // width
    return kernel_call(
        branch_grad_kernel,
        "branch_grad",
        pltpu.PrefetchScalarGridSpec(
            num_scalar_prefetch=0,
            grid=(blocks,),
            in_specs=[
                pl.BlockSpec((width, length), lambda b: (0, 0)),
                pl.BlockSpec((width, width), lambda b: (b, 0)),
            ]
            + [pl.BlockSpec(memory_space=pl.ANY)] * len(after),
            out_specs=pl.BlockSpec((1, width, length), lambda b: (b, 0, 0)),
        ),
        jax.ShapeDtypeStruct((blocks, width, length), LOW),
        2 * length * width * width * blocks,
        2 * length * width * (blocks + 1),
        vmem=20,
    )(g, down_weight, *after)


def own_column_static(group, piece, section):
    if section == 1 or group == GROUPS:
        return 3 * group + piece
    return group + GROUPS * piece


def piece_kernel(where_ref, w_ref, *out_refs):
    part = out_refs[0].shape[1] // 3
    for section in range(2):

        @pl.when(where_ref[0] == section)
        def _(section=section):
            for group in range(4):
                for piece in range(3):
                    column = own_column_static(group, piece, section) * part
                    out_refs[group][:, piece * part : (piece + 1) * part] = w_ref[0, :, column : column + part]


def weight_piece(where, weights):
    rows, columns = weights.shape[1:]
    shape = (rows // 4, columns // 4)
    return kernel_call(
        piece_kernel,
        "weight_piece",
        pltpu.PrefetchScalarGridSpec(
            num_scalar_prefetch=1,
            grid=(1,),
            in_specs=[pl.BlockSpec((1, rows // 4, columns), lambda i, w: (0, w[1], 0))],
            out_specs=[whole(shape)] * 4,
        ),
        [jax.ShapeDtypeStruct(shape, LOW)] * 4,
        0,
        rows * columns,
        vmem=58,
    )(where, weights)


def weight_copies(group, wanted, where_ref, own_ref, quarters, target, sem, act):
    quarter = target.shape[0] // 4
    part = target.shape[1] // 3

    @pl.when(where_ref[0] == wanted)
    def _():
        for piece in range(3):
            column = own_column_static(group, piece, wanted) * part
            act(pltpu.make_async_copy(own_ref.at[0, :, pl.ds(column, part)], target.at[:, pl.ds(piece * part, part)], sem.at[piece]))

    @pl.when(where_ref[0] != wanted)
    def _():
        for place, source in enumerate(quarters):
            index = where_ref[1] ^ (0, 2, 1, 3)[place]
            act(pltpu.make_async_copy(source, target.at[pl.ds(index * quarter, quarter), :], sem.at[place]))


def segment_rows(segment):
    tokens = segment.shape[1]
    ids = lax.broadcasted_iota(jnp.int32, (16, tokens), 0)
    same = segment == ids
    real = ids < 5
    queries = jnp.where(real & jnp.logical_not(same), MASKED, 0.0).astype(LOW)
    keys = jnp.where(real & same, 1.0, 0.0).astype(LOW)
    return queries, keys


def two_parts(values):
    high = values.astype(LOW)
    return high, (values - high.astype(FULL)).astype(LOW)


def minus_rows(values):
    high = values.astype(LOW)
    rest = values - high.astype(FULL)
    middle = rest.astype(LOW)
    low = rest - middle.astype(FULL)
    row = lax.broadcasted_iota(jnp.int32, (16, values.shape[1]), 0)
    parts = jnp.where(
        row == 0, high.astype(FULL), jnp.where(row == 1, middle.astype(FULL), jnp.where(row == 2, low, 0.0))
    )
    return (-parts).astype(LOW)


def three_ones(tokens):
    return jnp.where(lax.broadcasted_iota(jnp.int32, (16, tokens), 0) < 3, 1.0, 0.0).astype(LOW)


def head_tasks(heads, blocks, block):
    return [
        (head, slice(i * block, (i + 1) * block), slice(0, (i + 1) * block), i * block)
        for head in range(heads)
        for i in range(blocks)
    ]


def in_stages(tasks, stages):
    for step in range(len(tasks) + len(stages) - 1):
        for late, stage in enumerate(stages):
            if 0 <= step - late < len(tasks):
                stage(tasks[step - late])


def attend_kernel(group, where_ref, own_ref, near_ref, beside_ref, core_ref, across_ref, nt_ref, seg_ref, qkv_ref, mixed_ref, total_ref, w_ref, sem):
    copies = functools.partial(
        weight_copies, group, 0, where_ref, own_ref, (near_ref, beside_ref, core_ref, across_ref), w_ref, sem
    )
    copies(lambda c: c.start())
    copies(lambda c: c.wait())
    length = nt_ref.shape[1]
    width = qkv_ref.shape[0] // 3
    heads, blocks = width // HEAD_DIM, 4
    block = length // blocks
    for part in range(3):
        qkv_ref[part * width : (part + 1) * width, :] = dot(
            w_ref[:, part * width : (part + 1) * width], nt_ref[...], 0, 0
        ).astype(LOW)
    seg_queries, seg_keys = segment_rows(seg_ref[0])
    causal = lax.broadcasted_iota(jnp.int32, (block, block), 0) <= lax.broadcasted_iota(jnp.int32, (block, block), 1)
    ones = three_ones(length)
    scored, weighed = {}, {}

    def score(task):
        head, queries, keys, _ = task
        high, low = two_parts(qkv_ref[head * HEAD_DIM : (head + 1) * HEAD_DIM, queries].astype(FULL) * (SCALE * LOG2E))
        key_rows = qkv_ref[width + head * HEAD_DIM : width + (head + 1) * HEAD_DIM, keys]
        scored[task] = dot(
            jnp.concatenate([key_rows, key_rows, seg_keys[:, keys]], axis=0),
            jnp.concatenate([high, low, seg_queries[:, queries]], axis=0),
            0,
            0,
        )

    def weigh(task):
        before = task[3]
        scores = scored.pop(task)
        last = jnp.where(causal, scores[before:], MASKED)
        highest = jnp.max(last, axis=0, keepdims=True)
        if before:
            highest = jnp.maximum(highest, jnp.max(scores[:before], axis=0, keepdims=True))
        exponents = jnp.exp2(last - highest).astype(LOW)
        if before:
            exponents = jnp.concatenate([jnp.exp2(scores[:before] - highest).astype(LOW), exponents], axis=0)
        weighed[task] = (exponents, highest)

    def mix(task):
        head, queries, keys, _ = task
        exponents, highest = weighed.pop(task)
        values = qkv_ref[2 * width + head * HEAD_DIM : 2 * width + (head + 1) * HEAD_DIM, keys]
        mixed = dot(jnp.concatenate([values, ones[:, keys]], axis=0), exponents)
        total = mixed[HEAD_DIM : HEAD_DIM + 1]
        mixed_ref[head * HEAD_DIM : (head + 1) * HEAD_DIM, queries] = (mixed[:HEAD_DIM] / total).astype(LOW)
        total_ref[head : head + 1, queries] = highest + jnp.log2(total)

    in_stages(head_tasks(heads, blocks, block), (score, weigh, mix))


def attend(group, where, own, received, nt, segments):
    width, length = nt.shape
    part = width // GROUPS
    anywhere = pl.BlockSpec(memory_space=pl.ANY)
    return kernel_call(
        functools.partial(attend_kernel, group),
        "attend",
        pltpu.PrefetchScalarGridSpec(
            num_scalar_prefetch=1,
            grid=(1,),
            in_specs=[anywhere] * 5
            + [
                pl.BlockSpec((width, length), lambda i, w: (0, 0)),
                pl.BlockSpec((1, 1, length), lambda i, w: (w[0], 0, 0)),
            ],
            out_specs=[
                pl.BlockSpec((3 * part, length), lambda i, w: (0, 0)),
                pl.BlockSpec((part, length), lambda i, w: (0, 0)),
                pl.BlockSpec((part // HEAD_DIM, length), lambda i, w: (0, 0)),
                pl.BlockSpec((width, 3 * part), lambda i, w: (0, 0)),
            ],
            scratch_shapes=[pltpu.SemaphoreType.DMA((4,))],
        ),
        [
            jax.ShapeDtypeStruct((3 * part, length), LOW),
            jax.ShapeDtypeStruct((part, length), LOW),
            jax.ShapeDtypeStruct((part // HEAD_DIM, length), FULL),
            jax.ShapeDtypeStruct((width, 3 * part), LOW),
        ],
        4.5e9,
        8 * width * length,
        vmem=24,
    )(where, own, *received, nt, segments)


def attend_back_kernel(where_ref, qkv_ref, gm_ref, total_ref, delta_ref, seg_ref, nt_ref, *rest):
    keep_ref, send_ref, grads_ref, acc = rest[-4:]
    length = nt_ref.shape[1]
    width = gm_ref.shape[0]
    heads, blocks = width // HEAD_DIM, 4
    block = length // blocks
    seg_queries, seg_keys = segment_rows(seg_ref[0])
    ones = three_ones(length)
    causal = lax.broadcasted_iota(jnp.int32, (block, block), 1) <= lax.broadcasted_iota(jnp.int32, (block, block), 0)
    acc[...] = jnp.zeros_like(acc)
    scored, weighed = {}, {}

    def rows(part, head):
        return slice(part * width + head * HEAD_DIM, part * width + (head + 1) * HEAD_DIM)

    def score(task):
        head, queries, keys, _ = task
        high, low = two_parts(qkv_ref[rows(0, head), queries].astype(FULL) * (SCALE * LOG2E))
        key_rows = qkv_ref[rows(1, head), keys]
        scores = dot(
            jnp.concatenate([high, low, seg_queries[:, queries], minus_rows(total_ref[head : head + 1, queries])], axis=0),
            jnp.concatenate([key_rows, key_rows, seg_keys[:, keys], ones[:, keys]], axis=0),
            0,
            0,
        )
        grads = dot(
            jnp.concatenate([gm_ref[rows(0, head), queries], minus_rows(delta_ref[head : head + 1, queries])], axis=0),
            jnp.concatenate([qkv_ref[rows(2, head), keys], ones[:, keys]], axis=0),
            0,
            0,
        )
        scored[task] = (scores, grads)

    def weigh(task):
        before = task[3]
        scores, grads = scored.pop(task)
        last = jnp.where(causal, scores[:, before:], MASKED)
        if before:
            last = jnp.concatenate([scores[:, :before], last], axis=1)
        probs = jnp.exp2(last)
        weighed[task] = (probs.astype(LOW), (probs * grads).astype(LOW))

    def collect(task):
        head, queries, keys, _ = task
        probs, grads = weighed.pop(task)
        acc[rows(2, head), keys] += dot(gm_ref[rows(0, head), queries], probs)
        acc[rows(1, head), keys] += dot(qkv_ref[rows(0, head), queries] * LOW(SCALE), grads)
        acc[rows(0, head), queries] = dot(qkv_ref[rows(1, head), keys], grads, 1, 1) * SCALE

    in_stages(head_tasks(heads, blocks, block), (score, weigh, collect))
    grads_ref[...] = acc[...].astype(LOW)
    for place, rows_ in halves(where_ref, nt_ref.shape[0]):
        (keep_ref, send_ref)[place][...] = dot(nt_ref[rows_, :], grads_ref[...], 1, 1).astype(LOW)


def halves(where_ref, count):
    half = count // 2
    return [
        (0, pl.ds(pl.multiple_of(where_ref[2] * half, half), half)),
        (1, pl.ds(pl.multiple_of((1 - where_ref[2]) * half, half), half)),
    ]


def whole(shape):
    return pl.BlockSpec(shape, lambda *_: (0,) * len(shape))


def attend_back(where, qkv, gm, total, delta, segments, nt, after=()):
    width, length = nt.shape
    part = gm.shape[0]
    arrays = [qkv, gm, total, delta]
    return kernel_call(
        attend_back_kernel,
        "attend_back",
        pltpu.PrefetchScalarGridSpec(
            num_scalar_prefetch=1,
            grid=(1,),
            in_specs=[whole(a.shape) for a in arrays]
            + [pl.BlockSpec((1, 1, length), lambda i, w: (w[0], 0, 0)), whole(nt.shape)]
            + [pl.BlockSpec(memory_space=pl.ANY)] * len(after),
            out_specs=[whole((width // 2, 3 * part))] * 2 + [whole((3 * part, length))],
            scratch_shapes=[pltpu.VMEM((3 * part, length), FULL)],
        ),
        [jax.ShapeDtypeStruct((width // 2, 3 * part), LOW)] * 2 + [jax.ShapeDtypeStruct((3 * part, length), LOW)],
        9e9,
        8 * width * length,
        vmem=28,
    )(where, *arrays, segments, nt, *after)


def middle_kernel(where_ref, own_ref, near_ref, beside_ref, core_ref, across_ref, *refs):
    mixed_refs, (x_ref, seg_ref, mid_ref, nm_ref, sums_ref, w_ref, sem) = refs[:GROUPS], refs[GROUPS:]
    step = pl.program_id(0)

    @pl.when(step == 0)
    def _():
        copies = functools.partial(
            weight_copies, GROUPS, 0, where_ref, own_ref, (near_ref, beside_ref, core_ref, across_ref), w_ref, sem
        )
        copies(lambda c: c.start())
        copies(lambda c: c.wait())
        sums_ref[...] = jnp.zeros_like(sums_ref)

    mixed = jnp.concatenate([ref[...] for ref in mixed_refs], axis=0)
    branch = dot(w_ref[...], mixed, 0, 0)
    middle = (x_ref[0].astype(FULL) + compressed(branch)).astype(LOW)
    mid_ref[...] = middle
    normed, _ = crms(widened(middle))
    nm_ref[...] = normed.astype(LOW)
    valid = seg_ref[0] > 0
    lane = lax.broadcasted_iota(jnp.int32, sums_ref.shape, 1)
    count = jnp.sum(valid.astype(FULL), axis=1, keepdims=True)
    sums_ref[...] += jnp.where(lane == 0, square_sum(middle, valid), 0.0) + jnp.where(lane == 2, count, 0.0)


def middle_of(where, own, received, mixed, x, segments):
    width, length = x.shape[1] + 1, x.shape[2]
    block = length // 4
    anywhere = pl.BlockSpec(memory_space=pl.ANY)
    spec = tokens_spec(width, block)
    return kernel_call(
        middle_kernel,
        "middle",
        pltpu.PrefetchScalarGridSpec(
            num_scalar_prefetch=1,
            grid=(4,),
            in_specs=[anywhere] * 5
            + [tokens_spec(width // GROUPS, block)] * GROUPS
            + [row_spec(width, block), pl.BlockSpec((1, 1, block), lambda t, w: (w[0], 0, t))],
            out_specs=[spec, spec, whole((8, 128)), whole((width, width))],
            scratch_shapes=[pltpu.SemaphoreType.DMA((4,))],
        ),
        [jax.ShapeDtypeStruct((width, length), LOW)] * 2
        + [jax.ShapeDtypeStruct((8, 128), FULL), jax.ShapeDtypeStruct((width, width), LOW)],
        2 * length * width * width,
        12 * length * width,
        vmem=20,
    )(where, own, *received, *mixed, x, segments)


def gelu_both(hidden):
    rate = 0.7978845608028654
    square = hidden * hidden
    half = 0.5 + 0.5 * jnp.tanh(hidden * (rate + (rate * 0.044715) * square))
    slope = half + hidden * (2.0 * rate + (6.0 * rate * 0.044715) * square) * (half - half * half)
    return hidden * half, slope


def chunks(length, count):
    return [slice(i * (length // count), (i + 1) * (length // count)) for i in range(count)]


def hidden_kernel(first, where_ref, own_ref, *refs):
    received, refs = refs[:8], refs[8:]
    (nm_ref, ga_ref, g_ref) = refs[:3]
    (act_ref, grad_ref, keep_ref, send_ref, weights, sem) = refs[-6:]
    step = pl.program_id(0)
    length = nm_ref.shape[1]

    def copies(place, do):
        weight_copies(
            first + 2 * place, 1, where_ref, own_ref, received[4 * place : 4 * place + 4], weights.at[place], sem.at[place], do
        )

    @pl.when(step == 0)
    def _():
        for place in range(2):
            copies(place, lambda c: c.start())

    for place in range(2):

        @pl.when(step == place)
        def _(place=place):
            copies(place, lambda c: c.wait())

    hidden = {}

    def enter(tokens):
        hidden[tokens] = dot(weights[step], nm_ref[:, tokens], 0, 0)

    def bend(tokens):
        value, slope = gelu_both(hidden.pop(tokens))
        act_ref[0, :, tokens] = value.astype(LOW)
        grad_ref[0, :, tokens] = (ga_ref[0, :, tokens].astype(FULL) * slope).astype(LOW)

    in_stages(chunks(length, 4), (enter, bend))
    for place, rows in halves(where_ref, nm_ref.shape[0]):
        (keep_ref, send_ref)[place][0] = dot(act_ref[0, rows, :], g_ref[...], 1, 1).astype(LOW)
    for place, rows in halves(where_ref, nm_ref.shape[0]):
        (keep_ref, send_ref)[place][1] = dot(nm_ref[rows, :], grad_ref[0], 1, 1).astype(LOW)


def hidden_of(first, where, own, received, nm, ga, g, after=()):
    width, length = nm.shape
    anywhere = pl.BlockSpec(memory_space=pl.ANY)
    fixed = whole((width, length))
    place = pl.BlockSpec((1, width, length), lambda b, w: (b, 0, 0))
    return kernel_call(
        functools.partial(hidden_kernel, first),
        "hidden",
        pltpu.PrefetchScalarGridSpec(
            num_scalar_prefetch=1,
            grid=(2,),
            in_specs=[anywhere] * 9
            + [fixed, pl.BlockSpec((1, width, length), lambda b, w: (first + 2 * b, 0, 0)), fixed]
            + [anywhere] * len(after),
            out_specs=[place] * 2 + [pl.BlockSpec((2, width // 2, width), lambda b, w: (b, 0, 0))] * 2,
            scratch_shapes=[pltpu.VMEM((2, width, width), LOW), pltpu.SemaphoreType.DMA((2, 4))],
        ),
        [jax.ShapeDtypeStruct((2, width, length), LOW)] * 2
        + [jax.ShapeDtypeStruct((4, width // 2, width), LOW)] * 2,
        14e9,
        14 * length * width,
        vmem=58,
    )(where, own, *[a for r in received for a in r], nm, ga, g, *after)


def output_kernel(where_ref, own_ref, *refs):
    received, refs = refs[:16], refs[16:]
    (act_a, act_b, grad_a, grad_b, down_ref, mid_ref, cot_ref, seg_ref) = refs[:8]
    (keep_out, send_out, gmid_ref, gab_ref, sums_ref, weights, sem) = refs[-7:]
    step = pl.program_id(0)
    width, length = mid_ref.shape

    def copies(do):
        for group in range(4):
            weight_copies(
                group, 1, where_ref, own_ref, received[4 * group : 4 * group + 4], weights.at[group], sem.at[group], do
            )

    @pl.when(step == 0)
    def _():
        copies(lambda c: c.start())
        copies(lambda c: c.wait())
        sums_ref[...] = jnp.zeros_like(sums_ref)

    on_attention = where_ref[0] == 0
    products = {}

    def multiply(tokens):
        out = grad = 0.0
        for group in range(4):
            act = (act_a, act_b)[group % 2][group // 2, :, tokens]
            slope_grad = (grad_a, grad_b)[group % 2][group // 2, :, tokens]
            out = out + dot(down_ref[group * width : (group + 1) * width, :], act, 0, 0)
            grad = grad + dot(weights[group], slope_grad)
        products[tokens] = out, grad

    def finish(tokens):
        out, grad = products.pop(tokens)
        middle = mid_ref[:, tokens]
        wide = widened(middle)
        output = (wide + compressed(out)).astype(LOW)
        lane = lax.broadcasted_iota(jnp.int32, sums_ref.shape, 1)
        sums_ref[...] += jnp.where(lane == 1, square_sum(output, seg_ref[0][:, tokens] > 0), 0.0)
        keep_out[:, tokens] = jnp.where(on_attention, middle, output)
        send_out[:, tokens] = jnp.where(on_attention, output, middle)
        normed, inverse = crms(wide)
        grad = (cot_ref[0, :, tokens].astype(FULL) + widened_back(crms_back(normed, inverse, grad))).astype(LOW)
        gmid_ref[:, tokens] = grad
        gab_ref[:, tokens] = compressed_back(grad).astype(LOW)

    in_stages(chunks(length, 2), (multiply, finish))


def output_of(where, own, received, acts, grads, down_weight, middle, cot, segments, after=()):
    width, length = middle.shape
    steps = 2
    block = length // steps
    anywhere = pl.BlockSpec(memory_space=pl.ANY)
    spec = tokens_spec(width, block)
    pair = pl.BlockSpec((2, width, block), lambda t, w: (0, 0, t))
    row = jax.ShapeDtypeStruct((width, length), LOW)
    return kernel_call(
        output_kernel,
        "output",
        pltpu.PrefetchScalarGridSpec(
            num_scalar_prefetch=1,
            grid=(steps,),
            in_specs=[anywhere] * 17
            + [pair] * 4
            + [whole(down_weight.shape), spec, row_spec(width, block)]
            + [pl.BlockSpec((1, 1, block), lambda t, w: (w[0], 0, t))]
            + [anywhere] * len(after),
            out_specs=[spec] * 4 + [whole((8, 128))],
            scratch_shapes=[pltpu.VMEM((4, width, width), LOW), pltpu.SemaphoreType.DMA((4, 4))],
        ),
        [row] * 4 + [jax.ShapeDtypeStruct((8, 128), FULL)],
        20e9,
        24 * length * width,
        vmem=58,
    )(where, own, *[a for r in received for a in r], *acts, *grads, down_weight, middle, cot, segments, *after)


def mixed_grad_kernel(where_ref, gab_ref, w_ref, *refs):
    mixed_refs, gm_refs, (delta_ref, keep_ref, send_ref, mixed_all) = refs[:GROUPS], refs[-GROUPS - 4 : -4], refs[-4:]
    gab = gab_ref[...]
    part = gm_refs[0].shape[0]
    heads = part // HEAD_DIM
    for group in range(GROUPS):
        rows = slice(group * part, (group + 1) * part)
        grads = dot(w_ref[rows, :], gab).astype(LOW)
        gm_refs[group][...] = grads
        mixed = mixed_refs[group][...]
        mixed_all[rows, :] = mixed
        product = grads.astype(FULL) * mixed.astype(FULL)
        for head in range(heads):
            delta_ref[group, head : head + 1, :] = jnp.sum(
                product[head * HEAD_DIM : (head + 1) * HEAD_DIM], axis=0, keepdims=True
            )
    for place, rows in halves(where_ref, mixed_all.shape[0]):
        (keep_ref, send_ref)[place][...] = dot(mixed_all[rows, :], gab, 1, 1).astype(LOW)


def mixed_grad(where, gab, w, mixed, after=()):
    width, length = gab.shape
    part = width // GROUPS
    heads = part // HEAD_DIM
    outs = kernel_call(
        mixed_grad_kernel,
        "mixed_grad",
        pltpu.PrefetchScalarGridSpec(
            num_scalar_prefetch=1,
            grid=(1,),
            in_specs=[whole((width, length)), whole((width, width))]
            + [whole((part, length))] * GROUPS
            + [pl.BlockSpec(memory_space=pl.ANY)] * len(after),
            out_specs=[whole((part, length))] * GROUPS
            + [whole((GROUPS, heads, length))]
            + [whole((width // 2, width))] * 2,
            scratch_shapes=[pltpu.VMEM((width, length), LOW)],
        ),
        [jax.ShapeDtypeStruct((part, length), LOW)] * GROUPS
        + [jax.ShapeDtypeStruct((GROUPS, heads, length), FULL)]
        + [jax.ShapeDtypeStruct((width // 2, width), LOW)] * 2,
        4 * length * width * width,
        8 * length * width,
        vmem=28,
    )(where, gab, w, *mixed, *after)
    return outs[:GROUPS], outs[GROUPS], outs[GROUPS + 1], outs[GROUPS + 2]


def input_grad_kernel(where_ref, x_ref, gmid_ref, *refs):
    grad_refs, w_refs, (keep_ref, send_ref) = refs[:GROUPS], refs[GROUPS : 2 * GROUPS], refs[-2:]
    on_attention = where_ref[0] == 0
    grad_normed = dot(w_refs[0][...], grad_refs[0][...])
    for group in range(1, GROUPS):
        grad_normed = grad_normed + dot(w_refs[group][...], grad_refs[group][...])
    normed, inverse = crms(widened(x_ref[0]))
    middle = gmid_ref[...]
    grad = (middle.astype(FULL) + widened_back(crms_back(normed, inverse, grad_normed))).astype(LOW)
    keep_ref[...] = jnp.where(on_attention, grad, middle)
    send_ref[...] = jnp.where(on_attention, middle, grad)


def input_grad(where, x, grad_middle, grads, weights, after=()):
    width, length = grad_middle.shape
    spec = tokens_spec(width, length // 4)
    return kernel_call(
        input_grad_kernel,
        "input_grad",
        pltpu.PrefetchScalarGridSpec(
            num_scalar_prefetch=1,
            grid=(4,),
            in_specs=[row_spec(width, length // 4), spec]
            + [spec] * GROUPS
            + [whole((width, width))] * GROUPS
            + [pl.BlockSpec(memory_space=pl.ANY)] * len(after),
            out_specs=[spec, spec],
        ),
        [jax.ShapeDtypeStruct((width, length), LOW)] * 2,
        6 * length * width * width,
        12 * length * width,
        vmem=58,
    )(where, x, grad_middle, *grads, *weights, *after)


def partner(block, distance):
    size = lax.axis_size("dp")
    return lax.ppermute(block, "dp", [(i, i ^ distance) for i in range(size)])


def across(block):
    return lax.ppermute(block, "section", [(0, 1), (1, 0)])


def split(left, right, distance):
    bit = (lax.axis_index("dp") & distance) // distance
    half = left.shape[1] // 2
    part = lambda a, at: lax.dynamic_slice_in_dim(a, at * half, half, 1)
    return add_low(part(left, bit), part(right, bit)), add_low(part(left, 1 - bit), part(right, 1 - bit))


def add_low(left, right):
    return (left.astype(FULL) + right.astype(FULL)).astype(LOW)


class Scatter:
    def __init__(self, keep, send, order):
        self.order = order
        self.keep, self.got = keep, partner(send, order[0])
        self.sent = send
        self.at = 0

    def step(self, *others):
        self.at += 1
        self.got = later(self.got, *others)
        self.keep, self.sent = split(self.keep, self.got, self.order[self.at])
        self.got = partner(self.sent, self.order[self.at])

    def total(self, *others):
        while self.at < len(self.order) - 1:
            self.step(*others)
        return add_low(self.keep, later(self.got, *others))


class Gather:
    def __init__(self, shard, order, *others):
        self.left = list(reversed(order))
        self.held = later(shard, *others)[None] if others else shard[None]
        self.got = partner(self.held, self.left.pop(0))

    def step(self, *others):
        self.held = jnp.concatenate([self.held, later(self.got, *others)], axis=0)
        self.got = partner(self.held, self.left.pop(0))

    def all(self, *others):
        while self.left:
            self.step(*others)
        return self.held, self.got


def number_of(order):
    me = lax.axis_index("dp").astype(jnp.int32)
    number = jnp.int32(0)
    for distance in order:
        number = number * 2 + (me // distance) % 2
    return number


def later(value, *others):
    return lax.optimization_barrier((value, *others))[0]


def gathered_specs(array, per_step):
    half_steps = array.shape[0] // per_step
    block = (per_step, *array.shape[1:])
    return [
        pl.BlockSpec(block, lambda e, w: (jnp.minimum(e, half_steps - 1), 0, 0)),
        pl.BlockSpec(block, lambda e, w: (jnp.maximum(e - half_steps, 0), 0, 0)),
    ]


def each_entry(number_ref, halves_refs, do):
    steps = pl.num_programs(0)
    per_step = halves_refs[0].shape[0]
    for place, ref in enumerate(halves_refs):

        @pl.when((pl.program_id(0) * 2 >= steps) == (place == 1))
        def _(ref=ref):
            for entry in range(per_step):
                do((number_ref[1] % per_step) ^ entry, ref, entry)


def down_sum_kernel(skip, number_ref, near_ref, far_ref, out_ref):
    rows = out_ref.shape[2]

    def write(place, ref, entry):
        for block in range(2):
            out_ref[block, place] = ref[entry, skip + block * rows : skip + (block + 1) * rows, :].astype(FULL)

    each_entry(number_ref, (near_ref, far_ref), write)


def down_sum(number, skip, near, far, width):
    entries = 2 * near.shape[0]
    rows = width // entries
    per_step = entries // 4
    out = kernel_call(
        functools.partial(down_sum_kernel, skip),
        "down_sum",
        pltpu.PrefetchScalarGridSpec(
            num_scalar_prefetch=1,
            grid=(4,),
            in_specs=gathered_specs(near, per_step),
            out_specs=pl.BlockSpec((2, per_step, rows, width), lambda e, w: (0, (w[1] // per_step) ^ e, 0, 0)),
        ),
        jax.ShapeDtypeStruct((2, entries, rows, width), FULL),
        0,
        12 * width * width,
        vmem=58,
    )(number, near, far)
    return out.reshape(2 * width, width)


def first_sum_kernel(number_ref, near_a, far_a, near_b, far_b, out_ref):
    rows, columns = out_ref.shape[1:]
    width = columns // 4
    part = width // 3

    def write(section, numbers):
        def put(place, ref, entry):
            for at, number in enumerate(numbers):
                values = ref[entry, at * rows : (at + 1) * rows, :].astype(FULL)
                if section == 1:
                    out_ref[place, :, number * width : (number + 1) * width] = values
                elif number == 0:
                    out_ref[place, :, 3 * width :] = values
                else:
                    for piece in range(3):
                        column = own_column_static(number - 1, piece, 0) * part
                        out_ref[place, :, column : column + part] = values[:, piece * part : (piece + 1) * part]

        return put

    for section in range(2):

        @pl.when(number_ref[0] == section)
        def _(section=section):
            each_entry(number_ref, (near_a, far_a), write(section, (0, 1)))
            each_entry(number_ref, (near_b, far_b), write(section, (2, 3)))


def first_sum(number, a, b, width):
    entries = 2 * a[0].shape[0]
    rows = width // entries
    per_step = entries // 4
    out = kernel_call(
        first_sum_kernel,
        "first_sum",
        pltpu.PrefetchScalarGridSpec(
            num_scalar_prefetch=1,
            grid=(4,),
            in_specs=gathered_specs(a[0], per_step) + gathered_specs(b[0], per_step),
            out_specs=pl.BlockSpec((per_step, rows, 4 * width), lambda e, w: ((w[1] // per_step) ^ e, 0, 0)),
        ),
        jax.ShapeDtypeStruct((entries, rows, 4 * width), FULL),
        0,
        24 * width * width,
        vmem=58,
    )(number, *a, *b)
    return out.reshape(width, 4 * width)


def on_device(stream_in, cotangent, weights_first, down_weight, segments):
    rows_dev, length, compact_width = stream_in.shape
    width = compact_width + 1
    section = lax.axis_index("section").astype(jnp.int32)
    index = lax.axis_index("dp").astype(jnp.int32)
    size = lax.axis_size("dp")
    on_attention = section == 0
    where = jnp.stack([section, index & 3, index & 1])
    segments3 = segments.reshape(rows_dev, 1, length)
    order = [1 << i for i in range(size.bit_length() - 1)]

    near = [across(piece) for piece in weight_piece(where, weights_first)]
    x, cot = jnp.transpose(stream_in, (0, 2, 1)), jnp.transpose(cotangent, (0, 2, 1))
    nt, g = prep(where, x, cot)
    ga = branch_grad(g, down_weight, after=(near[0],))
    attended, received = [], []
    for group in range(4):
        ahead = (nt, ga, *[a[1] for a in attended])[group]
        quarter = later(near[group], ahead)
        beside = partner(quarter, 2)
        received.append((quarter, beside, partner(quarter, 1), partner(beside, 1)))
        if group < GROUPS:
            attended.append(attend(group, where, weights_first, received[group], nt, segments3))
    mixed = [a[1] for a in attended]
    middle, nm, sums_mid, out_weights = middle_of(where, weights_first, received[GROUPS], mixed, x, segments3)

    act_a, grad_a, *sums = hidden_of(0, where, weights_first, received[0::2], nm, ga, g)
    early = Scatter(*sums, order)
    early.step()
    act_b, grad_b, *sums = hidden_of(1, where, weights_first, received[1::2], nm, ga, g, after=(early.sent,))
    late = Scatter(*sums, order)
    keep_out, send_out, grad_mid, gab, sums_out = output_of(
        where, weights_first, received, (act_a, act_b), (grad_a, grad_b), down_weight, middle, cot, segments3, after=(late.sent,)
    )
    early.step(gab)
    late.step(gab)
    received_out = across(send_out)
    gm, delta, keep_w, send_w = mixed_grad(where, gab, out_weights, mixed, after=(early.sent, late.sent))
    keeps, sends, grads = [keep_w], [send_w], []

    def backward(group, *after):
        qkv, _, total, _ = attended[group]
        keep_w, send_w, grad = attend_back(where, qkv, gm[group], total, delta[group], segments3, nt, after=after)
        keeps.append(keep_w)
        sends.append(send_w)
        grads.append(grad)

    backward(0)
    early.step(grads[0])
    attn_a = Scatter(jnp.stack(keeps), jnp.stack(sends), order)
    backward(1, early.sent, attn_a.sent)
    late.step(grads[1])
    attn_a.step(grads[1])
    backward(2, late.sent, attn_a.sent)
    late.step(grads[2])
    attn_a.step(grads[2])
    attn_b = Scatter(jnp.stack(keeps[2:]), later(jnp.stack(sends[2:]), late.sent, attn_a.sent), order)
    attn_b.step()
    keep_grad, send_grad = input_grad(
        where, x, grad_mid, grads, [a[3] for a in attended], after=(attn_b.sent,)
    )
    attn_a.step(keep_grad)
    attn_b.step(keep_grad, attn_a.sent)
    early, late = early.total(attn_b.sent), late.total(attn_b.sent)
    rows = early.shape[1]
    attn_a = attn_a.total(early, late)

    flat = lambda a: a.reshape(-1, width)
    scalars = (sums_mid + sums_out)[0, :3]

    def scalar_rows(values):
        high = values.astype(LOW)
        rest = values - high.astype(FULL)
        middle_part = rest.astype(LOW)
        low = (rest - middle_part.astype(FULL)).astype(LOW)
        packed = jnp.concatenate([high, middle_part, low])
        return jnp.zeros((16, width), LOW).at[0, :9].set(packed)

    def scalars_of(block):
        parts = block[..., 0, :9].astype(FULL)
        return parts[..., :3] + parts[..., 3:6] + parts[..., 6:9]

    up = jnp.stack([early[1], late[1], early[3], late[3]])
    lower, upper = jnp.stack([early[0], late[0]]), jnp.stack([early[2], late[2]])
    mine_dn, theirs_dn = jnp.where(on_attention, lower, upper), jnp.where(on_attention, upper, lower)
    mine_a, theirs_a = jnp.where(on_attention, attn_a, up[:2]), jnp.where(on_attention, up[:2], attn_a)
    sent_a = jnp.concatenate([scalar_rows(scalars), flat(theirs_dn), flat(theirs_a)])
    swapped = across(sent_a)
    attn_b.step(sent_a)
    swapped = later(swapped, attn_b.sent)
    pair = scalars + scalars_of(swapped[:16])
    shard_a = add_low(flat(mine_a), swapped[16 + 2 * rows :])
    shard_dn = add_low(flat(mine_dn), swapped[16 : 16 + 2 * rows])
    sum_a = Gather(shard_a, order)
    sum_dn = Gather(jnp.concatenate([scalar_rows(pair), shard_dn]), order, sum_a.held)
    attn_b = attn_b.total(sum_dn.held)
    mine_b, theirs_b = jnp.where(on_attention, attn_b, up[2:]), jnp.where(on_attention, up[2:], attn_b)
    swapped_b = across(flat(theirs_b))
    sum_a.step(theirs_b)
    sum_dn.step(sum_a.held)
    sum_b = Gather(add_low(flat(mine_b), later(swapped_b, sum_dn.held)), order)
    received_grad = across(later(send_grad, sum_b.held))
    sum_a.step(sum_b.held)
    sum_dn.step(sum_a.held)
    sum_b.step(sum_dn.held)
    sum_a.step(sum_b.held)
    sum_b.step(sum_a.held)
    sum_dn.step(sum_b.held)
    sum_a, sum_dn, sum_b = sum_a.all(), sum_dn.all(), sum_b.all()
    number = jnp.stack([section, number_of(order)])
    grad_down = down_sum(number, 16, *sum_dn, width)
    grad_first = first_sum(number, sum_a, sum_b, width)
    totals = sum(jnp.sum(scalars_of(m[:, :16]), axis=0) for m in sum_dn)
    square = jnp.where(on_attention, totals[0], totals[1])
    residual_rms = jnp.sqrt(square / (totals[2] * width)).reshape(1)
    slots = jnp.float32(rows_dev * length * size)
    token_count = jnp.where(on_attention, totals[2], slots - totals[2]).astype(jnp.int32).reshape(1)

    def stacked(kept, other):
        kept, other = kept[:-1], other[:-1]
        both = jnp.where(on_attention, jnp.stack([kept, other]), jnp.stack([other, kept]))
        return jnp.transpose(both, (0, 2, 1))[None]

    return (
        stacked(keep_out, received_out),
        stacked(keep_grad, received_grad),
        grad_first[None],
        grad_down,
        residual_rms,
        token_count,
    )


def solution(mesh):
    placed = (
        P("dp", None, None),
        P("dp", None, None),
        P("section", None, None),
        P(),
        P("dp", None),
    )
    return jax.shard_map(
        on_device,
        mesh=mesh,
        in_specs=placed,
        out_specs=(
            P("section", "dp", None, None),
            P("section", "dp", None, None),
            P("section", None, None),
            P("section", None),
            P("section"),
            P("section"),
        ),
        check_vma=False,
    )
```

```python
import functools

import jax
import jax.numpy as jnp
from jax import lax
from jax.experimental import pallas as pl
from jax.experimental.pallas import tpu as pltpu
from jax.sharding import PartitionSpec as P

HEADS = 12
HEAD_DIM = 64
GROUPS = 3
EPSILON = 1e-06
MASKED = -1e30
SCALE = HEAD_DIM ** (-0.5)
LOG2E = 1.4426950408889634
LOW = jnp.bfloat16
FULL = jnp.float32


def dot(left, right, left_dim=1, right_dim=0):
    return lax.dot_general(
        left, right, (((left_dim,), (right_dim,)), ((), ())), preferred_element_type=FULL
    )


def kernel_call(body, name, grid_spec, out_shape, flops, moved, vmem=32):
    return pl.pallas_call(
        body,
        grid_spec=grid_spec,
        out_shape=out_shape,
        compiler_params=pltpu.CompilerParams(vmem_limit_bytes=vmem * 2**20),
        cost_estimate=pl.CostEstimate(flops=int(flops * 3), bytes_accessed=int(moved * 3), transcendentals=0),
        name=name,
    )


def last_row(block):
    return lax.broadcasted_iota(jnp.int32, block.shape, 0) == block.shape[0] - 1


def widened(block):
    values = jnp.where(last_row(block), 0.0, block.astype(FULL))
    return jnp.where(last_row(block), -jnp.sum(values, axis=0, keepdims=True), values)


def crms(values):
    inverse = lax.rsqrt(jnp.mean(values * values, axis=0, keepdims=True) + EPSILON)
    return values * inverse, inverse


def crms_back(normed, inverse, grad):
    return inverse * (grad - normed * jnp.mean(grad * normed, axis=0, keepdims=True))


def compressed(branch):
    return branch - jnp.mean(branch, axis=0, keepdims=True)


def widened_back(grad):
    return grad - grad[grad.shape[0] - 1 :]


def compressed_back(block):
    values = jnp.where(last_row(block), 0.0, block.astype(FULL))
    return values - jnp.mean(values, axis=0, keepdims=True)


def square_sum(rounded, valid):
    wide = widened(rounded)
    per_token = jnp.sum(wide * wide, axis=0, keepdims=True)
    return jnp.sum(jnp.where(valid, per_token, 0.0), axis=1, keepdims=True)


def prep_kernel(where_ref, x_ref, cot_ref, nt_ref, g_ref):
    normed, _ = crms(widened(x_ref[0]))
    nt_ref[...] = normed.astype(LOW)
    g_ref[...] = compressed_back(cot_ref[0]).astype(LOW)


def tokens_spec(width, block):
    return pl.BlockSpec((width, block), lambda t, *_: (0, t))


def row_spec(width, block):
    return pl.BlockSpec((1, width, block), lambda t, w: (w[0], 0, t))


def prep(where, x, cot):
    width, length = x.shape[1] + 1, x.shape[2]
    spec = tokens_spec(width, length // 4)
    return kernel_call(
        prep_kernel,
        "prep",
        pltpu.PrefetchScalarGridSpec(
            num_scalar_prefetch=1, grid=(4,), in_specs=[row_spec(width, length // 4)] * 2, out_specs=[spec] * 2
        ),
        [jax.ShapeDtypeStruct((width, length), LOW)] * 2,
        0,
        8 * length * width,
        vmem=16,
    )(where, x, cot)


def branch_grad_kernel(g_ref, w_ref, *refs):
    out_ref = refs[-1]
    out_ref[0] = dot(w_ref[...], g_ref[...]).astype(LOW)


def branch_grad(g, down_weight, after=()):
    width, length = g.shape
    blocks = down_weight.shape[0] // width
    return kernel_call(
        branch_grad_kernel,
        "branch_grad",
        pltpu.PrefetchScalarGridSpec(
            num_scalar_prefetch=0,
            grid=(blocks,),
            in_specs=[
                pl.BlockSpec((width, length), lambda b: (0, 0)),
                pl.BlockSpec((width, width), lambda b: (b, 0)),
            ]
            + [pl.BlockSpec(memory_space=pltpu.HBM)] * len(after),
            out_specs=pl.BlockSpec((1, width, length), lambda b: (b, 0, 0)),
        ),
        pltpu.HBM((blocks, width, length), LOW),
        2 * length * width * width * blocks,
        2 * length * width * (blocks + 1),
        vmem=20,
    )(g, down_weight, *after)


def own_column_static(group, piece, section):
    if section == 1 or group == GROUPS:
        return 3 * group + piece
    return group + GROUPS * piece


def piece_kernel(where_ref, w_ref, *out_refs):
    part = out_refs[0].shape[1] // 3
    for section in range(2):

        @pl.when(where_ref[0] == section)
        def _(section=section):
            for group in range(4):
                for piece in range(3):
                    column = own_column_static(group, piece, section) * part
                    out_refs[group][:, piece * part : (piece + 1) * part] = w_ref[0, :, column : column + part]


def weight_piece(where, weights):
    rows, columns = weights.shape[1:]
    shape = (rows // 4, columns // 4)
    return kernel_call(
        piece_kernel,
        "weight_piece",
        pltpu.PrefetchScalarGridSpec(
            num_scalar_prefetch=1,
            grid=(1,),
            in_specs=[pl.BlockSpec((1, rows // 4, columns), lambda i, w: (0, w[1], 0))],
            out_specs=[whole(shape)] * 4,
        ),
        [jax.ShapeDtypeStruct(shape, LOW)] * 4,
        0,
        rows * columns,
        vmem=58,
    )(where, weights)


def weight_copies(group, wanted, where_ref, own_ref, quarters, target, sem, act):
    quarter = target.shape[0] // 4
    part = target.shape[1] // 3

    @pl.when(where_ref[0] == wanted)
    def _():
        for piece in range(3):
            column = own_column_static(group, piece, wanted) * part
            act(pltpu.make_async_copy(own_ref.at[0, :, pl.ds(column, part)], target.at[:, pl.ds(piece * part, part)], sem.at[piece]))

    @pl.when(where_ref[0] != wanted)
    def _():
        for place, source in enumerate(quarters):
            index = where_ref[1] ^ (0, 2, 1, 3)[place]
            act(pltpu.make_async_copy(source, target.at[pl.ds(index * quarter, quarter), :], sem.at[place]))


def segment_rows(segment):
    tokens = segment.shape[1]
    ids = lax.broadcasted_iota(jnp.int32, (16, tokens), 0)
    same = segment == ids
    real = ids < 5
    queries = jnp.where(real & jnp.logical_not(same), MASKED, 0.0).astype(LOW)
    keys = jnp.where(real & same, 1.0, 0.0).astype(LOW)
    return queries, keys


def two_parts(values):
    high = values.astype(LOW)
    return high, (values - high.astype(FULL)).astype(LOW)


def minus_rows(values):
    high = values.astype(LOW)
    rest = values - high.astype(FULL)
    middle = rest.astype(LOW)
    low = rest - middle.astype(FULL)
    row = lax.broadcasted_iota(jnp.int32, (16, values.shape[1]), 0)
    parts = jnp.where(
        row == 0, high.astype(FULL), jnp.where(row == 1, middle.astype(FULL), jnp.where(row == 2, low, 0.0))
    )
    return (-parts).astype(LOW)


def three_ones(tokens):
    return jnp.where(lax.broadcasted_iota(jnp.int32, (16, tokens), 0) < 3, 1.0, 0.0).astype(LOW)


def head_tasks(heads, blocks, block):
    return [
        (head, slice(i * block, (i + 1) * block), slice(0, (i + 1) * block), i * block)
        for head in range(heads)
        for i in range(blocks)
    ]


def in_stages(tasks, stages):
    for step in range(len(tasks) + len(stages) - 1):
        for late, stage in enumerate(stages):
            if 0 <= step - late < len(tasks):
                stage(tasks[step - late])


def attend_kernel(group, where_ref, own_ref, near_ref, beside_ref, core_ref, across_ref, nt_ref, seg_ref, qkv_ref, mixed_ref, total_ref, w_ref, sem):
    copies = functools.partial(
        weight_copies, group, 0, where_ref, own_ref, (near_ref, beside_ref, core_ref, across_ref), w_ref, sem
    )
    copies(lambda c: c.start())
    copies(lambda c: c.wait())
    length = nt_ref.shape[1]
    width = qkv_ref.shape[0] // 3
    heads, blocks = width // HEAD_DIM, 4
    block = length // blocks
    for part in range(3):
        qkv_ref[part * width : (part + 1) * width, :] = dot(
            w_ref[:, part * width : (part + 1) * width], nt_ref[...], 0, 0
        ).astype(LOW)
    seg_queries, seg_keys = segment_rows(seg_ref[0])
    causal = lax.broadcasted_iota(jnp.int32, (block, block), 0) <= lax.broadcasted_iota(jnp.int32, (block, block), 1)
    ones = three_ones(length)
    scored, weighed = {}, {}

    def score(task):
        head, queries, keys, _ = task
        high, low = two_parts(qkv_ref[head * HEAD_DIM : (head + 1) * HEAD_DIM, queries].astype(FULL) * (SCALE * LOG2E))
        key_rows = qkv_ref[width + head * HEAD_DIM : width + (head + 1) * HEAD_DIM, keys]
        scored[task] = dot(
            jnp.concatenate([key_rows, key_rows, seg_keys[:, keys]], axis=0),
            jnp.concatenate([high, low, seg_queries[:, queries]], axis=0),
            0,
            0,
        )

    def weigh(task):
        before = task[3]
        scores = scored.pop(task)
        last = jnp.where(causal, scores[before:], MASKED)
        highest = jnp.max(last, axis=0, keepdims=True)
        if before:
            highest = jnp.maximum(highest, jnp.max(scores[:before], axis=0, keepdims=True))
        exponents = jnp.exp2(last - highest).astype(LOW)
        if before:
            exponents = jnp.concatenate([jnp.exp2(scores[:before] - highest).astype(LOW), exponents], axis=0)
        weighed[task] = (exponents, highest)

    def mix(task):
        head, queries, keys, _ = task
        exponents, highest = weighed.pop(task)
        values = qkv_ref[2 * width + head * HEAD_DIM : 2 * width + (head + 1) * HEAD_DIM, keys]
        mixed = dot(jnp.concatenate([values, ones[:, keys]], axis=0), exponents)
        total = mixed[HEAD_DIM : HEAD_DIM + 1]
        mixed_ref[head * HEAD_DIM : (head + 1) * HEAD_DIM, queries] = (mixed[:HEAD_DIM] / total).astype(LOW)
        total_ref[head : head + 1, queries] = highest + jnp.log2(total)

    in_stages(head_tasks(heads, blocks, block), (score, weigh, mix))


def attend(group, where, own, received, nt, segments):
    width, length = nt.shape
    part = width // GROUPS
    anywhere = pl.BlockSpec(memory_space=pltpu.HBM)
    return kernel_call(
        functools.partial(attend_kernel, group),
        "attend",
        pltpu.PrefetchScalarGridSpec(
            num_scalar_prefetch=1,
            grid=(1,),
            in_specs=[anywhere] * 5
            + [
                pl.BlockSpec((width, length), lambda i, w: (0, 0)),
                pl.BlockSpec((1, 1, length), lambda i, w: (w[0], 0, 0)),
            ],
            out_specs=[
                pl.BlockSpec((3 * part, length), lambda i, w: (0, 0)),
                pl.BlockSpec((part, length), lambda i, w: (0, 0)),
                pl.BlockSpec((part // HEAD_DIM, length), lambda i, w: (0, 0)),
                pl.BlockSpec((width, 3 * part), lambda i, w: (0, 0)),
            ],
            scratch_shapes=[pltpu.SemaphoreType.DMA((4,))],
        ),
        [
            pltpu.HBM((3 * part, length), LOW),
            jax.ShapeDtypeStruct((part, length), LOW),
            pltpu.HBM((part // HEAD_DIM, length), FULL),
            pltpu.HBM((width, 3 * part), LOW),
        ],
        4.5e9,
        8 * width * length,
        vmem=24,
    )(where, own, *received, nt, segments)


def attend_back_kernel(where_ref, qkv_ref, gm_ref, total_ref, delta_ref, seg_ref, nt_ref, *rest):
    keep_ref, send_ref, grads_ref, acc = rest[-4:]
    length = nt_ref.shape[1]
    width = gm_ref.shape[0]
    heads, blocks = width // HEAD_DIM, 4
    block = length // blocks
    seg_queries, seg_keys = segment_rows(seg_ref[0])
    ones = three_ones(length)
    causal = lax.broadcasted_iota(jnp.int32, (block, block), 1) <= lax.broadcasted_iota(jnp.int32, (block, block), 0)
    acc[...] = jnp.zeros_like(acc)
    scored, weighed = {}, {}

    def rows(part, head):
        return slice(part * width + head * HEAD_DIM, part * width + (head + 1) * HEAD_DIM)

    def score(task):
        head, queries, keys, _ = task
        high, low = two_parts(qkv_ref[rows(0, head), queries].astype(FULL) * (SCALE * LOG2E))
        key_rows = qkv_ref[rows(1, head), keys]
        scores = dot(
            jnp.concatenate([high, low, seg_queries[:, queries], minus_rows(total_ref[head : head + 1, queries])], axis=0),
            jnp.concatenate([key_rows, key_rows, seg_keys[:, keys], ones[:, keys]], axis=0),
            0,
            0,
        )
        grads = dot(
            jnp.concatenate([gm_ref[rows(0, head), queries], minus_rows(delta_ref[head : head + 1, queries])], axis=0),
            jnp.concatenate([qkv_ref[rows(2, head), keys], ones[:, keys]], axis=0),
            0,
            0,
        )
        scored[task] = (scores, grads)

    def weigh(task):
        before = task[3]
        scores, grads = scored.pop(task)
        last = jnp.where(causal, scores[:, before:], MASKED)
        if before:
            last = jnp.concatenate([scores[:, :before], last], axis=1)
        probs = jnp.exp2(last)
        weighed[task] = (probs.astype(LOW), (probs * grads).astype(LOW))

    def collect(task):
        head, queries, keys, _ = task
        probs, grads = weighed.pop(task)
        acc[rows(2, head), keys] += dot(gm_ref[rows(0, head), queries], probs)
        acc[rows(1, head), keys] += dot(qkv_ref[rows(0, head), queries] * LOW(SCALE), grads)
        acc[rows(0, head), queries] = dot(qkv_ref[rows(1, head), keys], grads, 1, 1) * SCALE

    in_stages(head_tasks(heads, blocks, block), (score, weigh, collect))
    grads_ref[...] = acc[...].astype(LOW)
    for place, rows_ in halves(where_ref, nt_ref.shape[0]):
        (keep_ref, send_ref)[place][...] = dot(nt_ref[rows_, :], grads_ref[...], 1, 1).astype(LOW)


def halves(where_ref, count):
    half = count // 2
    return [
        (0, pl.ds(pl.multiple_of(where_ref[2] * half, half), half)),
        (1, pl.ds(pl.multiple_of((1 - where_ref[2]) * half, half), half)),
    ]


def whole(shape):
    return pl.BlockSpec(shape, lambda *_: (0,) * len(shape))


def attend_back(where, qkv, gm, total, delta, segments, nt, after=()):
    width, length = nt.shape
    part = gm.shape[0]
    arrays = [qkv, gm, total, delta]
    return kernel_call(
        attend_back_kernel,
        "attend_back",
        pltpu.PrefetchScalarGridSpec(
            num_scalar_prefetch=1,
            grid=(1,),
            in_specs=[whole(a.shape) for a in arrays]
            + [pl.BlockSpec((1, 1, length), lambda i, w: (w[0], 0, 0)), whole(nt.shape)]
            + [pl.BlockSpec(memory_space=pltpu.HBM)] * len(after),
            out_specs=[whole((width // 2, 3 * part))] * 2 + [whole((3 * part, length))],
            scratch_shapes=[pltpu.VMEM((3 * part, length), FULL)],
        ),
        [jax.ShapeDtypeStruct((width // 2, 3 * part), LOW)] * 2 + [jax.ShapeDtypeStruct((3 * part, length), LOW)],
        9e9,
        8 * width * length,
        vmem=28,
    )(where, *arrays, segments, nt, *after)


def middle_kernel(where_ref, own_ref, near_ref, beside_ref, core_ref, across_ref, *refs):
    mixed_refs, (x_ref, seg_ref, mid_ref, nm_ref, sums_ref, w_ref, sem) = refs[:GROUPS], refs[GROUPS:]
    step = pl.program_id(0)

    @pl.when(step == 0)
    def _():
        copies = functools.partial(
            weight_copies, GROUPS, 0, where_ref, own_ref, (near_ref, beside_ref, core_ref, across_ref), w_ref, sem
        )
        copies(lambda c: c.start())
        copies(lambda c: c.wait())
        sums_ref[...] = jnp.zeros_like(sums_ref)

    mixed = jnp.concatenate([ref[...] for ref in mixed_refs], axis=0)
    branch = dot(w_ref[...], mixed, 0, 0)
    middle = (x_ref[0].astype(FULL) + compressed(branch)).astype(LOW)
    mid_ref[...] = middle
    normed, _ = crms(widened(middle))
    nm_ref[...] = normed.astype(LOW)
    valid = seg_ref[0] > 0
    lane = lax.broadcasted_iota(jnp.int32, sums_ref.shape, 1)
    count = jnp.sum(valid.astype(FULL), axis=1, keepdims=True)
    sums_ref[...] += jnp.where(lane == 0, square_sum(middle, valid), 0.0) + jnp.where(lane == 2, count, 0.0)


def middle_of(where, own, received, mixed, x, segments):
    width, length = x.shape[1] + 1, x.shape[2]
    block = length // 4
    anywhere = pl.BlockSpec(memory_space=pltpu.HBM)
    spec = tokens_spec(width, block)
    return kernel_call(
        middle_kernel,
        "middle",
        pltpu.PrefetchScalarGridSpec(
            num_scalar_prefetch=1,
            grid=(4,),
            in_specs=[anywhere] * 5
            + [tokens_spec(width // GROUPS, block)] * GROUPS
            + [row_spec(width, block), pl.BlockSpec((1, 1, block), lambda t, w: (w[0], 0, t))],
            out_specs=[spec, spec, whole((8, 128)), whole((width, width))],
            scratch_shapes=[pltpu.SemaphoreType.DMA((4,))],
        ),
        [jax.ShapeDtypeStruct((width, length), LOW)] * 2
        + [jax.ShapeDtypeStruct((8, 128), FULL), jax.ShapeDtypeStruct((width, width), LOW)],
        2 * length * width * width,
        12 * length * width,
        vmem=20,
    )(where, own, *received, *mixed, x, segments)


def gelu_both(hidden):
    rate = 0.7978845608028654
    square = hidden * hidden
    half = 0.5 + 0.5 * jnp.tanh(hidden * (rate + (rate * 0.044715) * square))
    slope = half + hidden * (2.0 * rate + (6.0 * rate * 0.044715) * square) * (half - half * half)
    return hidden * half, slope


def chunks(length, count):
    return [slice(i * (length // count), (i + 1) * (length // count)) for i in range(count)]


def hidden_kernel(first, where_ref, own_ref, *refs):
    received, refs = refs[:8], refs[8:]
    (nm_ref, ga_ref, g_ref) = refs[:3]
    (act_ref, grad_ref, keep_ref, send_ref, weights, sem) = refs[-6:]
    step = pl.program_id(0)
    length = nm_ref.shape[1]

    def copies(place, do):
        weight_copies(
            first + 2 * place, 1, where_ref, own_ref, received[4 * place : 4 * place + 4], weights.at[place], sem.at[place], do
        )

    @pl.when(step == 0)
    def _():
        for place in range(2):
            copies(place, lambda c: c.start())

    for place in range(2):

        @pl.when(step == place)
        def _(place=place):
            copies(place, lambda c: c.wait())

    hidden = {}

    def enter(tokens):
        hidden[tokens] = dot(weights[step], nm_ref[:, tokens], 0, 0)

    def bend(tokens):
        value, slope = gelu_both(hidden.pop(tokens))
        act_ref[0, :, tokens] = value.astype(LOW)
        grad_ref[0, :, tokens] = (ga_ref[0, :, tokens].astype(FULL) * slope).astype(LOW)

    in_stages(chunks(length, 4), (enter, bend))
    for place, rows in halves(where_ref, nm_ref.shape[0]):
        (keep_ref, send_ref)[place][1, 0] = dot(act_ref[0, rows, :], g_ref[...], 1, 1).astype(LOW)
    for place, rows in halves(where_ref, nm_ref.shape[0]):
        (keep_ref, send_ref)[place][0, 0] = dot(nm_ref[rows, :], grad_ref[0], 1, 1).astype(LOW)


def hidden_of(first, where, own, received, nm, ga, g, after=()):
    width, length = nm.shape
    anywhere = pl.BlockSpec(memory_space=pltpu.HBM)
    fixed = whole((width, length))
    place = pl.BlockSpec((1, width, length), lambda b, w: (b, 0, 0))
    return kernel_call(
        functools.partial(hidden_kernel, first),
        "hidden",
        pltpu.PrefetchScalarGridSpec(
            num_scalar_prefetch=1,
            grid=(2,),
            in_specs=[anywhere] * 9
            + [fixed, pl.BlockSpec((1, width, length), lambda b, w: (first + 2 * b, 0, 0)), fixed]
            + [anywhere] * len(after),
            out_specs=[place] * 2 + [pl.BlockSpec((2, 1, width // 2, width), lambda b, w: (0, b, 0, 0))] * 2,
            scratch_shapes=[pltpu.VMEM((2, width, width), LOW), pltpu.SemaphoreType.DMA((2, 4))],
        ),
        [pltpu.HBM((2, width, length), LOW)] * 2
        + [jax.ShapeDtypeStruct((2, 2, width // 2, width), LOW)] * 2,
        14e9,
        14 * length * width,
        vmem=58 if first else 34,
    )(where, own, *[a for r in received for a in r], nm, ga, g, *after)


def output_kernel(where_ref, own_ref, *refs):
    received, refs = refs[:16], refs[16:]
    (act_a, act_b, grad_a, grad_b, down_ref, mid_ref, cot_ref, seg_ref) = refs[:8]
    (keep_out, send_out, gmid_ref, gab_ref, sums_ref, weights, sem) = refs[-7:]
    step = pl.program_id(0)
    width, length = mid_ref.shape

    def copies(do):
        for group in range(4):
            weight_copies(
                group, 1, where_ref, own_ref, received[4 * group : 4 * group + 4], weights.at[group], sem.at[group], do
            )

    @pl.when(step == 0)
    def _():
        copies(lambda c: c.start())
        copies(lambda c: c.wait())
        sums_ref[...] = jnp.zeros_like(sums_ref)

    on_attention = where_ref[0] == 0
    products = {}

    def multiply(tokens):
        out = grad = 0.0
        for group in range(4):
            act = (act_a, act_b)[group % 2][group // 2, :, tokens]
            slope_grad = (grad_a, grad_b)[group % 2][group // 2, :, tokens]
            out = out + dot(down_ref[group * width : (group + 1) * width, :], act, 0, 0)
            grad = grad + dot(weights[group], slope_grad)
        products[tokens] = out, grad

    def finish(tokens):
        out, grad = products.pop(tokens)
        middle = mid_ref[:, tokens]
        wide = widened(middle)
        output = (wide + compressed(out)).astype(LOW)
        lane = lax.broadcasted_iota(jnp.int32, sums_ref.shape, 1)
        sums_ref[...] += jnp.where(lane == 1, square_sum(output, seg_ref[0][:, tokens] > 0), 0.0)
        keep_out[:, tokens] = jnp.where(on_attention, middle, output)
        send_out[:, tokens] = jnp.where(on_attention, output, middle)
        normed, inverse = crms(wide)
        grad = (cot_ref[0, :, tokens].astype(FULL) + widened_back(crms_back(normed, inverse, grad))).astype(LOW)
        gmid_ref[:, tokens] = grad
        gab_ref[:, tokens] = compressed_back(grad).astype(LOW)

    in_stages(chunks(length, 2), (multiply, finish))


def output_of(where, own, received, acts, grads, down_weight, middle, cot, segments, after=()):
    width, length = middle.shape
    steps = 2
    block = length // steps
    anywhere = pl.BlockSpec(memory_space=pltpu.HBM)
    spec = tokens_spec(width, block)
    pair = pl.BlockSpec((2, width, block), lambda t, w: (0, 0, t))
    row = jax.ShapeDtypeStruct((width, length), LOW)
    return kernel_call(
        output_kernel,
        "output",
        pltpu.PrefetchScalarGridSpec(
            num_scalar_prefetch=1,
            grid=(steps,),
            in_specs=[anywhere] * 17
            + [pair] * 4
            + [whole(down_weight.shape), spec, row_spec(width, block)]
            + [pl.BlockSpec((1, 1, block), lambda t, w: (w[0], 0, t))]
            + [anywhere] * len(after),
            out_specs=[spec] * 4 + [whole((8, 128))],
            scratch_shapes=[pltpu.VMEM((4, width, width), LOW), pltpu.SemaphoreType.DMA((4, 4))],
        ),
        [row] * 4 + [jax.ShapeDtypeStruct((8, 128), FULL)],
        20e9,
        24 * length * width,
        vmem=40,
    )(where, own, *[a for r in received for a in r], *acts, *grads, down_weight, middle, cot, segments, *after)


def mixed_grad_kernel(where_ref, gab_ref, w_ref, *refs):
    mixed_refs, gm_refs, (delta_ref, keep_ref, send_ref, mixed_all) = refs[:GROUPS], refs[-GROUPS - 4 : -4], refs[-4:]
    gab = gab_ref[...]
    part = gm_refs[0].shape[0]
    heads = part // HEAD_DIM
    for group in range(GROUPS):
        rows = slice(group * part, (group + 1) * part)
        grads = dot(w_ref[rows, :], gab).astype(LOW)
        gm_refs[group][...] = grads
        mixed = mixed_refs[group][...]
        mixed_all[rows, :] = mixed
        product = grads.astype(FULL) * mixed.astype(FULL)
        for head in range(heads):
            delta_ref[group, head : head + 1, :] = jnp.sum(
                product[head * HEAD_DIM : (head + 1) * HEAD_DIM], axis=0, keepdims=True
            )
    for place, rows in halves(where_ref, mixed_all.shape[0]):
        (keep_ref, send_ref)[place][...] = dot(mixed_all[rows, :], gab, 1, 1).astype(LOW)


def mixed_grad(where, gab, w, mixed, after=()):
    width, length = gab.shape
    part = width // GROUPS
    heads = part // HEAD_DIM
    outs = kernel_call(
        mixed_grad_kernel,
        "mixed_grad",
        pltpu.PrefetchScalarGridSpec(
            num_scalar_prefetch=1,
            grid=(1,),
            in_specs=[whole((width, length)), whole((width, width))]
            + [whole((part, length))] * GROUPS
            + [pl.BlockSpec(memory_space=pltpu.HBM)] * len(after),
            out_specs=[whole((part, length))] * GROUPS
            + [whole((GROUPS, heads, length))]
            + [whole((width // 2, width))] * 2,
            scratch_shapes=[pltpu.VMEM((width, length), LOW)],
        ),
        [jax.ShapeDtypeStruct((part, length), LOW)] * GROUPS
        + [jax.ShapeDtypeStruct((GROUPS, heads, length), FULL)]
        + [jax.ShapeDtypeStruct((width // 2, width), LOW)] * 2,
        4 * length * width * width,
        8 * length * width,
        vmem=28,
    )(where, gab, w, *mixed, *after)
    return outs[:GROUPS], outs[GROUPS], outs[GROUPS + 1], outs[GROUPS + 2]


def input_grad_kernel(where_ref, x_ref, gmid_ref, *refs):
    grad_refs, w_refs, (keep_ref, send_ref) = refs[:GROUPS], refs[GROUPS : 2 * GROUPS], refs[-2:]
    on_attention = where_ref[0] == 0
    grad_normed = dot(w_refs[0][...], grad_refs[0][...])
    for group in range(1, GROUPS):
        grad_normed = grad_normed + dot(w_refs[group][...], grad_refs[group][...])
    normed, inverse = crms(widened(x_ref[0]))
    middle = gmid_ref[...]
    grad = (middle.astype(FULL) + widened_back(crms_back(normed, inverse, grad_normed))).astype(LOW)
    keep_ref[...] = jnp.where(on_attention, grad, middle)
    send_ref[...] = jnp.where(on_attention, middle, grad)


def input_grad(where, x, grad_middle, grads, weights, after=()):
    width, length = grad_middle.shape
    spec = tokens_spec(width, length // 4)
    return kernel_call(
        input_grad_kernel,
        "input_grad",
        pltpu.PrefetchScalarGridSpec(
            num_scalar_prefetch=1,
            grid=(4,),
            in_specs=[row_spec(width, length // 4), spec]
            + [spec] * GROUPS
            + [whole((width, width))] * GROUPS
            + [pl.BlockSpec(memory_space=pltpu.HBM)] * len(after),
            out_specs=[spec, spec],
        ),
        [jax.ShapeDtypeStruct((width, length), LOW)] * 2,
        6 * length * width * width,
        12 * length * width,
        vmem=24,
    )(where, x, grad_middle, *grads, *weights, *after)


def partner(block, distance):
    size = lax.axis_size("dp")
    return lax.ppermute(block, "dp", [(i, i ^ distance) for i in range(size)])


def across(block):
    return lax.ppermute(block, "section", [(0, 1), (1, 0)])


def split(left, right, distance):
    bit = (lax.axis_index("dp") & distance) // distance
    half = left.shape[1] // 2
    part = lambda a, at: lax.dynamic_slice_in_dim(a, at * half, half, 1)
    return add_low(part(left, bit), part(right, bit)), add_low(part(left, 1 - bit), part(right, 1 - bit))


def add_low(left, right):
    return (left.astype(FULL) + right.astype(FULL)).astype(LOW)


class Scatter:
    def __init__(self, keep, got, order):
        self.order = order
        self.keep, self.got = keep, got
        self.at = 0

    def step(self, *others):
        self.at += 1
        self.got = later(self.got, *others)
        self.keep, self.sent = split(self.keep, self.got, self.order[self.at])
        self.got = partner(self.sent, self.order[self.at])

    def total(self, *others):
        while self.at < len(self.order) - 1:
            self.step(*others)
        return add_low(self.keep, later(self.got, *others))


class Gather:
    def __init__(self, shard, order, *others):
        self.left = list(reversed(order))
        self.held = later(shard, *others)[None] if others else shard[None]
        self.got = partner(self.held, self.left.pop(0))

    def step(self, *others):
        self.held = jnp.concatenate([self.held, later(self.got, *others)], axis=0)
        self.got = partner(self.held, self.left.pop(0))

    def all(self, *others):
        while self.left:
            self.step(*others)
        return self.held, self.got


def number_of(order):
    me = lax.axis_index("dp").astype(jnp.int32)
    number = jnp.int32(0)
    for distance in order:
        number = number * 2 + (me // distance) % 2
    return number


def later(value, *others):
    return lax.optimization_barrier((value, *others))[0]


def gathered_specs(array, per_step):
    half_steps = array.shape[0] // per_step
    block = (per_step, *array.shape[1:])
    return [
        pl.BlockSpec(block, lambda e, w: (jnp.minimum(e, half_steps - 1), 0, 0)),
        pl.BlockSpec(block, lambda e, w: (jnp.maximum(e - half_steps, 0), 0, 0)),
    ]


def each_entry(number_ref, halves_refs, do):
    steps = pl.num_programs(0)
    per_step = halves_refs[0].shape[0]
    for place, ref in enumerate(halves_refs):

        @pl.when((pl.program_id(0) * 2 >= steps) == (place == 1))
        def _(ref=ref):
            for entry in range(per_step):
                do((number_ref[1] % per_step) ^ entry, ref, entry)


def down_sum_kernel(number_ref, near_ref, far_ref, out_ref):
    rows = out_ref.shape[2]

    def write(place, ref, entry):
        for block in range(2):
            out_ref[block, place] = ref[entry, block * rows : (block + 1) * rows, :].astype(FULL)

    each_entry(number_ref, (near_ref, far_ref), write)


def down_sum(number, near, far, width):
    entries = 2 * near.shape[0]
    rows = width // entries
    per_step = entries // 4
    out = kernel_call(
        down_sum_kernel,
        "down_sum",
        pltpu.PrefetchScalarGridSpec(
            num_scalar_prefetch=1,
            grid=(4,),
            in_specs=gathered_specs(near, per_step),
            out_specs=pl.BlockSpec((2, per_step, rows, width), lambda e, w: (0, (w[1] // per_step) ^ e, 0, 0)),
        ),
        jax.ShapeDtypeStruct((2, entries, rows, width), FULL),
        0,
        12 * width * width,
        vmem=58,
    )(number, near, far)
    return out.reshape(2 * width, width)


def first_sum_kernel(number_ref, near_a, far_a, near_b, far_b, out_ref):
    rows, columns = out_ref.shape[1:]
    width = columns // 4
    part = width // 3

    def write(section, numbers, start):
        def put(place, ref, entry):
            for at, number in enumerate(numbers):
                values = ref[entry, start + at * rows : start + (at + 1) * rows, :].astype(FULL)
                if section == 1:
                    out_ref[place, :, number * width : (number + 1) * width] = values
                elif number == 0:
                    out_ref[place, :, 3 * width :] = values
                else:
                    for piece in range(3):
                        column = own_column_static(number - 1, piece, 0) * part
                        out_ref[place, :, column : column + part] = values[:, piece * part : (piece + 1) * part]

        return put

    for section in range(2):

        numbers, others = ((0, 1), (2, 3)) if section == 0 else ((0, 2), (1, 3))

        @pl.when(number_ref[0] == section)
        def _(section=section, numbers=numbers, others=others):
            each_entry(number_ref, (near_a, far_a), write(section, numbers, 16))
            each_entry(number_ref, (near_b, far_b), write(section, others, 0))


def first_sum(number, a, b, width):
    entries = 2 * a[0].shape[0]
    rows = width // entries
    per_step = entries // 4
    out = kernel_call(
        first_sum_kernel,
        "first_sum",
        pltpu.PrefetchScalarGridSpec(
            num_scalar_prefetch=1,
            grid=(4,),
            in_specs=gathered_specs(a[0], per_step) + gathered_specs(b[0], per_step),
            out_specs=pl.BlockSpec((per_step, rows, 4 * width), lambda e, w: ((w[1] // per_step) ^ e, 0, 0)),
        ),
        jax.ShapeDtypeStruct((entries, rows, 4 * width), FULL),
        0,
        24 * width * width,
        vmem=58,
    )(number, *a, *b)
    return out.reshape(width, 4 * width)


def on_device(stream_in, cotangent, weights_first, down_weight, segments):
    rows_dev, length, compact_width = stream_in.shape
    width = compact_width + 1
    section = lax.axis_index("section").astype(jnp.int32)
    index = lax.axis_index("dp").astype(jnp.int32)
    size = lax.axis_size("dp")
    on_attention = section == 0
    where = jnp.stack([section, index & 3, index & 1])
    segments3 = segments.reshape(rows_dev, 1, length)
    order = [1 << i for i in range(size.bit_length() - 1)]
    flat = lambda a: a.reshape(-1, width)

    near = [across(piece) for piece in weight_piece(where, weights_first)]
    x, cot = jnp.transpose(stream_in, (0, 2, 1)), jnp.transpose(cotangent, (0, 2, 1))
    nt, g = prep(where, x, cot)
    ga = branch_grad(g, down_weight, after=(near[0],))
    attended, received, besides = [], [], [partner(later(near[0], nt), 2), partner(later(near[1], ga), 2)]
    for group in range(4):
        quarter, beside = near[group], besides[group]
        done = [attended[group - 1][1] if group else ga]
        received.append((quarter, beside, partner(quarter, 1), partner(later(beside, *done), 1)))
        if group < 2:
            besides.append(partner(later(near[group + 2], *done), 2))
        if group < GROUPS:
            attended.append(attend(group, where, weights_first, received[group], nt, segments3))
    mixed = [a[1] for a in attended]
    middle, nm, sums_mid, out_weights = middle_of(where, weights_first, received[GROUPS], mixed, x, segments3)

    act_a, grad_a, kept_a, sent_a = hidden_of(0, where, weights_first, received[0::2], nm, ga, g)
    got_a = partner(sent_a, 1)
    up_a = Scatter(kept_a[0], got_a[0], order)
    up_a.step()
    act_b, grad_b, kept_b, sent_b = hidden_of(1, where, weights_first, received[1::2], nm, ga, g, after=(up_a.sent,))
    up_a.step(act_b)
    got_b = partner(later(sent_b, up_a.sent), 1)
    up_b = Scatter(kept_b[0], got_b[0], order)
    up_b.step()
    kept, sent = [], []
    for keep, got in ((kept_a[1], got_a[1]), (kept_b[1], got_b[1])):
        lower, upper = add_low(keep[0], got[0]), add_low(keep[1], got[1])
        kept.append(jnp.where(on_attention, lower, upper))
        sent.append(jnp.where(on_attention, upper, lower))
    kept, sent = jnp.stack(kept), later(jnp.stack(sent), up_b.sent)
    down = Scatter(kept, across(sent), order)
    keep_out, send_out, grad_mid, gab, sums_out = output_of(
        where, weights_first, received, (act_a, act_b), (grad_a, grad_b), down_weight, middle, cot, segments3, after=(sent,)
    )
    up_a.step(gab)
    up_b.step(up_a.sent)
    down.step(up_b.sent)
    gm, delta, keep_w, send_w = mixed_grad(where, gab, out_weights, mixed, after=(down.sent,))
    keeps, sends, grads = [keep_w], [send_w], []

    def backward(group, *after):
        qkv, _, total, _ = attended[group]
        keep_w, send_w, grad = attend_back(where, qkv, gm[group], total, delta[group], segments3, nt, after=after)
        keeps.append(keep_w)
        sends.append(send_w)
        grads.append(grad)

    up_a = up_a.total(delta)
    backward(0, up_a)
    up_b.step(grads[0])
    down.step(up_b.sent)
    sent_a = later(jnp.stack(sends), down.sent)
    attn_a = Scatter(jnp.stack(keeps), partner(sent_a, 1), order)
    backward(1, sent_a)
    attn_a.step(grads[1])
    down.step(attn_a.sent)
    up_b = up_b.total(grads[1])
    rows = up_a.shape[1]
    received_out = across(send_out)
    backward(2, down.sent, up_b)
    down = down.total(grads[2])
    sum_dn = Gather(flat(down), order)
    attn_a.step(sum_dn.held)
    attn_b = Scatter(jnp.stack(keeps[2:]), partner(later(jnp.stack(sends[2:]), attn_a.sent), 1), order)
    attn_b.step()
    sum_dn.step(attn_b.sent)
    attn_a.step(sum_dn.held)
    keep_grad, send_grad = input_grad(
        where, x, grad_mid, grads, [a[3] for a in attended], after=(attn_a.sent, received_out)
    )
    sum_dn.step(keep_grad)
    attn_b.step(sum_dn.held)
    attn_a = attn_a.total(attn_b.sent)

    scalars = (sums_mid + sums_out)[0, :3]

    def scalar_rows(values):
        high = values.astype(LOW)
        rest = values - high.astype(FULL)
        middle_part = rest.astype(LOW)
        low = (rest - middle_part.astype(FULL)).astype(LOW)
        packed = jnp.concatenate([high, middle_part, low])
        return jnp.zeros((16, width), LOW).at[0, :9].set(packed)

    def scalars_of(block):
        parts = block[..., 0, :9].astype(FULL)
        return parts[..., :3] + parts[..., 3:6] + parts[..., 6:9]

    mine_a, theirs_a = jnp.where(on_attention, attn_a, up_a), jnp.where(on_attention, up_a, attn_a)
    sent_a = jnp.concatenate([scalar_rows(scalars), flat(theirs_a)])
    swapped = across(sent_a)
    attn_b.step(sent_a)
    swapped = later(swapped, attn_b.sent)
    pair = scalars + scalars_of(swapped[:16])
    shard_a = add_low(flat(mine_a), swapped[16:])
    sum_a = Gather(jnp.concatenate([scalar_rows(pair), shard_a]), order)
    attn_b = attn_b.total(sum_a.held)
    mine_b, theirs_b = jnp.where(on_attention, attn_b, up_b), jnp.where(on_attention, up_b, attn_b)
    swapped_b = across(flat(theirs_b))
    sum_a.step(theirs_b)
    sum_b = Gather(add_low(flat(mine_b), later(swapped_b, sum_a.held)), order)
    received_grad = across(later(send_grad, sum_b.held))
    sum_a.step(sum_b.held)
    sum_b.step(sum_a.held)
    sum_dn.step(sum_b.held)
    number = jnp.stack([section, number_of(order)])
    grad_down = down_sum(number, *sum_dn.all(), width)

    def stacked(kept, other):
        kept, other = kept[:-1], other[:-1]
        both = jnp.where(on_attention, jnp.stack([kept, other]), jnp.stack([other, kept]))
        return jnp.transpose(both, (0, 2, 1))[None]

    stream_out = stacked(keep_out, received_out)
    sum_b.step(sum_dn.held)
    sum_a.step(sum_b.held)
    sum_a, sum_b = sum_a.all(), sum_b.all(grad_down, stream_out)
    grad_first = first_sum(number, sum_a, sum_b, width)
    totals = sum(jnp.sum(scalars_of(m[:, :16]), axis=0) for m in sum_a)
    square = jnp.where(on_attention, totals[0], totals[1])
    residual_rms = jnp.sqrt(square / (totals[2] * width)).reshape(1)
    slots = jnp.float32(rows_dev * length * size)
    token_count = jnp.where(on_attention, totals[2], slots - totals[2]).astype(jnp.int32).reshape(1)

    return (
        stream_out,
        stacked(keep_grad, received_grad),
        grad_first[None],
        grad_down,
        residual_rms,
        token_count,
    )


def solution(mesh):
    placed = (
        P("dp", None, None),
        P("dp", None, None),
        P("section", None, None),
        P(),
        P("dp", None),
    )
    return jax.shard_map(
        on_device,
        mesh=mesh,
        in_specs=placed,
        out_specs=(
            P("section", "dp", None, None),
            P("section", "dp", None, None),
            P("section", None, None),
            P("section", None),
            P("section"),
            P("section"),
        ),
        check_vma=False,
    )
```

```python
import functools

import jax
import jax.numpy as jnp
from jax import lax
from jax.experimental import pallas as pl
from jax.experimental.pallas import tpu as pltpu
from jax.sharding import PartitionSpec as P

HEADS = 12
HEAD_DIM = 64
GROUPS = 3
EPSILON = 1e-06
MASKED = -1e30
SCALE = HEAD_DIM ** (-0.5)
LOG2E = 1.4426950408889634
LOW = jnp.bfloat16
FULL = jnp.float32


def dot(left, right, left_dim=1, right_dim=0):
    return lax.dot_general(
        left, right, (((left_dim,), (right_dim,)), ((), ())), preferred_element_type=FULL
    )


def kernel_call(body, name, grid_spec, out_shape, flops, moved, vmem=32):
    return pl.pallas_call(
        body,
        grid_spec=grid_spec,
        out_shape=out_shape,
        compiler_params=pltpu.CompilerParams(vmem_limit_bytes=vmem * 2**20),
        cost_estimate=pl.CostEstimate(flops=int(flops * 3), bytes_accessed=int(moved * 3), transcendentals=0),
        name=name,
    )


def last_row(block):
    return lax.broadcasted_iota(jnp.int32, block.shape, 0) == block.shape[0] - 1


def widened(block):
    values = jnp.where(last_row(block), 0.0, block.astype(FULL))
    return jnp.where(last_row(block), -jnp.sum(values, axis=0, keepdims=True), values)


def crms(values):
    inverse = lax.rsqrt(jnp.mean(values * values, axis=0, keepdims=True) + EPSILON)
    return values * inverse, inverse


def crms_back(normed, inverse, grad):
    return inverse * (grad - normed * jnp.mean(grad * normed, axis=0, keepdims=True))


def compressed(branch):
    return branch - jnp.mean(branch, axis=0, keepdims=True)


def widened_back(grad):
    return grad - grad[grad.shape[0] - 1 :]


def compressed_back(block):
    values = jnp.where(last_row(block), 0.0, block.astype(FULL))
    return values - jnp.mean(values, axis=0, keepdims=True)


def square_sum(rounded, valid):
    wide = widened(rounded)
    per_token = jnp.sum(wide * wide, axis=0, keepdims=True)
    return jnp.sum(jnp.where(valid, per_token, 0.0), axis=1, keepdims=True)


def prep_kernel(where_ref, x_ref, cot_ref, nt_ref, g_ref):
    normed, _ = crms(widened(x_ref[0]))
    nt_ref[...] = normed.astype(LOW)
    g_ref[...] = compressed_back(cot_ref[0]).astype(LOW)


def tokens_spec(width, block):
    return pl.BlockSpec((width, block), lambda t, *_: (0, t))


def row_spec(width, block):
    return pl.BlockSpec((1, width, block), lambda t, w: (w[0], 0, t))


def prep(where, x, cot):
    width, length = x.shape[1] + 1, x.shape[2]
    spec = tokens_spec(width, length // 4)
    return kernel_call(
        prep_kernel,
        "prep",
        pltpu.PrefetchScalarGridSpec(
            num_scalar_prefetch=1, grid=(4,), in_specs=[row_spec(width, length // 4)] * 2, out_specs=[spec] * 2
        ),
        [jax.ShapeDtypeStruct((width, length), LOW)] * 2,
        0,
        8 * length * width,
        vmem=16,
    )(where, x, cot)


def branch_grad_kernel(g_ref, w_ref, *refs):
    out_ref = refs[-1]
    out_ref[0] = dot(w_ref[...], g_ref[...]).astype(LOW)


def branch_grad(g, down_weight, after=()):
    width, length = g.shape
    blocks = down_weight.shape[0] // width
    return kernel_call(
        branch_grad_kernel,
        "branch_grad",
        pltpu.PrefetchScalarGridSpec(
            num_scalar_prefetch=0,
            grid=(blocks,),
            in_specs=[
                pl.BlockSpec((width, length), lambda b: (0, 0)),
                pl.BlockSpec((width, width), lambda b: (b, 0)),
            ]
            + [pl.BlockSpec(memory_space=pltpu.HBM)] * len(after),
            out_specs=pl.BlockSpec((1, width, length), lambda b: (b, 0, 0)),
        ),
        pltpu.HBM((blocks, width, length), LOW),
        2 * length * width * width * blocks,
        2 * length * width * (blocks + 1),
        vmem=20,
    )(g, down_weight, *after)


def own_column_static(group, piece, section):
    if section == 1 or group == GROUPS:
        return 3 * group + piece
    return group + GROUPS * piece


def piece_kernel(where_ref, w_ref, *out_refs):
    part = out_refs[0].shape[1] // 3
    for section in range(2):

        @pl.when(where_ref[0] == section)
        def _(section=section):
            for group in range(4):
                for piece in range(3):
                    column = own_column_static(group, piece, section) * part
                    out_refs[group][:, piece * part : (piece + 1) * part] = w_ref[0, :, column : column + part]


def weight_piece(where, weights):
    rows, columns = weights.shape[1:]
    shape = (rows // 4, columns // 4)
    return kernel_call(
        piece_kernel,
        "weight_piece",
        pltpu.PrefetchScalarGridSpec(
            num_scalar_prefetch=1,
            grid=(1,),
            in_specs=[pl.BlockSpec((1, rows // 4, columns), lambda i, w: (0, w[1], 0))],
            out_specs=[whole(shape)] * 4,
        ),
        [jax.ShapeDtypeStruct(shape, LOW)] * 4,
        0,
        rows * columns,
        vmem=58,
    )(where, weights)


def weight_copies(group, wanted, where_ref, own_ref, quarters, target, sem, act):
    quarter = target.shape[0] // 4
    part = target.shape[1] // 3

    @pl.when(where_ref[0] == wanted)
    def _():
        for piece in range(3):
            column = own_column_static(group, piece, wanted) * part
            act(pltpu.make_async_copy(own_ref.at[0, :, pl.ds(column, part)], target.at[:, pl.ds(piece * part, part)], sem.at[piece]))

    @pl.when(where_ref[0] != wanted)
    def _():
        for place, source in enumerate(quarters):
            index = where_ref[1] ^ (0, 2, 1, 3)[place]
            act(pltpu.make_async_copy(source, target.at[pl.ds(index * quarter, quarter), :], sem.at[place]))


def segment_rows(segment):
    tokens = segment.shape[1]
    ids = lax.broadcasted_iota(jnp.int32, (16, tokens), 0)
    same = segment == ids
    real = ids < 5
    queries = jnp.where(real & jnp.logical_not(same), MASKED, 0.0).astype(LOW)
    keys = jnp.where(real & same, 1.0, 0.0).astype(LOW)
    return queries, keys


def two_parts(values):
    high = values.astype(LOW)
    return high, (values - high.astype(FULL)).astype(LOW)


def minus_rows(values):
    high = values.astype(LOW)
    rest = values - high.astype(FULL)
    middle = rest.astype(LOW)
    low = rest - middle.astype(FULL)
    row = lax.broadcasted_iota(jnp.int32, (16, values.shape[1]), 0)
    parts = jnp.where(
        row == 0, high.astype(FULL), jnp.where(row == 1, middle.astype(FULL), jnp.where(row == 2, low, 0.0))
    )
    return (-parts).astype(LOW)


def three_ones(tokens):
    return jnp.where(lax.broadcasted_iota(jnp.int32, (16, tokens), 0) < 3, 1.0, 0.0).astype(LOW)


def head_tasks(heads, blocks, block):
    return [
        (head, slice(i * block, (i + 1) * block), slice(0, (i + 1) * block), i * block)
        for head in range(heads)
        for i in range(blocks)
    ]


def in_stages(tasks, stages):
    for step in range(len(tasks) + len(stages) - 1):
        for late, stage in enumerate(stages):
            if 0 <= step - late < len(tasks):
                stage(tasks[step - late])


def attend_kernel(group, where_ref, own_ref, near_ref, beside_ref, core_ref, across_ref, nt_ref, seg_ref, qkv_ref, mixed_ref, total_ref, w_ref, sem):
    copies = functools.partial(
        weight_copies, group, 0, where_ref, own_ref, (near_ref, beside_ref, core_ref, across_ref), w_ref, sem
    )
    copies(lambda c: c.start())
    copies(lambda c: c.wait())
    length = nt_ref.shape[1]
    width = qkv_ref.shape[0] // 3
    heads, blocks = width // HEAD_DIM, 4
    block = length // blocks
    for part in range(3):
        qkv_ref[part * width : (part + 1) * width, :] = dot(
            w_ref[:, part * width : (part + 1) * width], nt_ref[...], 0, 0
        ).astype(LOW)
    seg_queries, seg_keys = segment_rows(seg_ref[0])
    causal = lax.broadcasted_iota(jnp.int32, (block, block), 0) <= lax.broadcasted_iota(jnp.int32, (block, block), 1)
    ones = three_ones(length)
    scored, weighed = {}, {}

    def score(task):
        head, queries, keys, _ = task
        high, low = two_parts(qkv_ref[head * HEAD_DIM : (head + 1) * HEAD_DIM, queries].astype(FULL) * (SCALE * LOG2E))
        key_rows = qkv_ref[width + head * HEAD_DIM : width + (head + 1) * HEAD_DIM, keys]
        scored[task] = dot(
            jnp.concatenate([key_rows, key_rows, seg_keys[:, keys]], axis=0),
            jnp.concatenate([high, low, seg_queries[:, queries]], axis=0),
            0,
            0,
        )

    def weigh(task):
        before = task[3]
        scores = scored.pop(task)
        last = jnp.where(causal, scores[before:], MASKED)
        highest = jnp.max(last, axis=0, keepdims=True)
        if before:
            highest = jnp.maximum(highest, jnp.max(scores[:before], axis=0, keepdims=True))
        exponents = jnp.exp2(last - highest).astype(LOW)
        if before:
            exponents = jnp.concatenate([jnp.exp2(scores[:before] - highest).astype(LOW), exponents], axis=0)
        weighed[task] = (exponents, highest)

    def mix(task):
        head, queries, keys, _ = task
        exponents, highest = weighed.pop(task)
        values = qkv_ref[2 * width + head * HEAD_DIM : 2 * width + (head + 1) * HEAD_DIM, keys]
        mixed = dot(jnp.concatenate([values, ones[:, keys]], axis=0), exponents)
        total = mixed[HEAD_DIM : HEAD_DIM + 1]
        mixed_ref[head * HEAD_DIM : (head + 1) * HEAD_DIM, queries] = (mixed[:HEAD_DIM] / total).astype(LOW)
        total_ref[head : head + 1, queries] = highest + jnp.log2(total)

    in_stages(head_tasks(heads, blocks, block), (score, weigh, mix))


def attend(group, where, own, received, nt, segments):
    width, length = nt.shape
    part = width // GROUPS
    anywhere = pl.BlockSpec(memory_space=pltpu.HBM)
    return kernel_call(
        functools.partial(attend_kernel, group),
        "attend",
        pltpu.PrefetchScalarGridSpec(
            num_scalar_prefetch=1,
            grid=(1,),
            in_specs=[anywhere] * 5
            + [
                pl.BlockSpec((width, length), lambda i, w: (0, 0)),
                pl.BlockSpec((1, 1, length), lambda i, w: (w[0], 0, 0)),
            ],
            out_specs=[
                pl.BlockSpec((3 * part, length), lambda i, w: (0, 0)),
                pl.BlockSpec((part, length), lambda i, w: (0, 0)),
                pl.BlockSpec((part // HEAD_DIM, length), lambda i, w: (0, 0)),
                pl.BlockSpec((width, 3 * part), lambda i, w: (0, 0)),
            ],
            scratch_shapes=[pltpu.SemaphoreType.DMA((4,))],
        ),
        [
            pltpu.HBM((3 * part, length), LOW),
            jax.ShapeDtypeStruct((part, length), LOW),
            pltpu.HBM((part // HEAD_DIM, length), FULL),
            pltpu.HBM((width, 3 * part), LOW),
        ],
        4.5e9,
        8 * width * length,
        vmem=24,
    )(where, own, *received, nt, segments)


def attend_back_kernel(where_ref, qkv_ref, gm_ref, total_ref, delta_ref, seg_ref, nt_ref, *rest):
    keep_ref, send_ref, grads_ref, acc = rest[-4:]
    length = nt_ref.shape[1]
    width = gm_ref.shape[0]
    heads, blocks = width // HEAD_DIM, 4
    block = length // blocks
    seg_queries, seg_keys = segment_rows(seg_ref[0])
    ones = three_ones(length)
    causal = lax.broadcasted_iota(jnp.int32, (block, block), 1) <= lax.broadcasted_iota(jnp.int32, (block, block), 0)
    acc[...] = jnp.zeros_like(acc)
    scored, weighed = {}, {}

    def rows(part, head):
        return slice(part * width + head * HEAD_DIM, part * width + (head + 1) * HEAD_DIM)

    def score(task):
        head, queries, keys, _ = task
        high, low = two_parts(qkv_ref[rows(0, head), queries].astype(FULL) * (SCALE * LOG2E))
        key_rows = qkv_ref[rows(1, head), keys]
        scores = dot(
            jnp.concatenate([high, low, seg_queries[:, queries], minus_rows(total_ref[head : head + 1, queries])], axis=0),
            jnp.concatenate([key_rows, key_rows, seg_keys[:, keys], ones[:, keys]], axis=0),
            0,
            0,
        )
        grads = dot(
            jnp.concatenate([gm_ref[rows(0, head), queries], minus_rows(delta_ref[head : head + 1, queries])], axis=0),
            jnp.concatenate([qkv_ref[rows(2, head), keys], ones[:, keys]], axis=0),
            0,
            0,
        )
        scored[task] = (scores, grads)

    def weigh(task):
        before = task[3]
        scores, grads = scored.pop(task)
        last = jnp.where(causal, scores[:, before:], MASKED)
        if before:
            last = jnp.concatenate([scores[:, :before], last], axis=1)
        probs = jnp.exp2(last)
        weighed[task] = (probs.astype(LOW), (probs * grads).astype(LOW))

    def collect(task):
        head, queries, keys, _ = task
        probs, grads = weighed.pop(task)
        acc[rows(2, head), keys] += dot(gm_ref[rows(0, head), queries], probs)
        acc[rows(1, head), keys] += dot(qkv_ref[rows(0, head), queries] * LOW(SCALE), grads)
        acc[rows(0, head), queries] = dot(qkv_ref[rows(1, head), keys], grads, 1, 1) * SCALE

    in_stages(head_tasks(heads, blocks, block), (score, weigh, collect))
    grads_ref[...] = acc[...].astype(LOW)
    for place, rows_ in halves(where_ref, nt_ref.shape[0]):
        (keep_ref, send_ref)[place][...] = dot(nt_ref[rows_, :], grads_ref[...], 1, 1).astype(LOW)


def halves(where_ref, count):
    half = count // 2
    return [
        (0, pl.ds(pl.multiple_of(where_ref[2] * half, half), half)),
        (1, pl.ds(pl.multiple_of((1 - where_ref[2]) * half, half), half)),
    ]


def whole(shape):
    return pl.BlockSpec(shape, lambda *_: (0,) * len(shape))


def attend_back(where, qkv, gm, total, delta, segments, nt, after=()):
    width, length = nt.shape
    part = gm.shape[0]
    arrays = [qkv, gm, total, delta]
    return kernel_call(
        attend_back_kernel,
        "attend_back",
        pltpu.PrefetchScalarGridSpec(
            num_scalar_prefetch=1,
            grid=(1,),
            in_specs=[whole(a.shape) for a in arrays]
            + [pl.BlockSpec((1, 1, length), lambda i, w: (w[0], 0, 0)), whole(nt.shape)]
            + [pl.BlockSpec(memory_space=pltpu.HBM)] * len(after),
            out_specs=[whole((width // 2, 3 * part))] * 2 + [whole((3 * part, length))],
            scratch_shapes=[pltpu.VMEM((3 * part, length), FULL)],
        ),
        [jax.ShapeDtypeStruct((width // 2, 3 * part), LOW)] * 2 + [pltpu.HBM((3 * part, length), LOW)],
        9e9,
        8 * width * length,
        vmem=28,
    )(where, *arrays, segments, nt, *after)


def middle_kernel(where_ref, own_ref, near_ref, beside_ref, core_ref, across_ref, *refs):
    mixed_refs, (x_ref, seg_ref, mid_ref, nm_ref, sums_ref, w_ref, sem) = refs[:GROUPS], refs[GROUPS:]
    step = pl.program_id(0)

    @pl.when(step == 0)
    def _():
        copies = functools.partial(
            weight_copies, GROUPS, 0, where_ref, own_ref, (near_ref, beside_ref, core_ref, across_ref), w_ref, sem
        )
        copies(lambda c: c.start())
        copies(lambda c: c.wait())
        sums_ref[...] = jnp.zeros_like(sums_ref)

    mixed = jnp.concatenate([ref[...] for ref in mixed_refs], axis=0)
    branch = dot(w_ref[...], mixed, 0, 0)
    middle = (x_ref[0].astype(FULL) + compressed(branch)).astype(LOW)
    mid_ref[...] = middle
    normed, _ = crms(widened(middle))
    nm_ref[...] = normed.astype(LOW)
    valid = seg_ref[0] > 0
    lane = lax.broadcasted_iota(jnp.int32, sums_ref.shape, 1)
    count = jnp.sum(valid.astype(FULL), axis=1, keepdims=True)
    sums_ref[...] += jnp.where(lane == 0, square_sum(middle, valid), 0.0) + jnp.where(lane == 2, count, 0.0)


def middle_of(where, own, received, mixed, x, segments):
    width, length = x.shape[1] + 1, x.shape[2]
    block = length // 4
    anywhere = pl.BlockSpec(memory_space=pltpu.HBM)
    spec = tokens_spec(width, block)
    return kernel_call(
        middle_kernel,
        "middle",
        pltpu.PrefetchScalarGridSpec(
            num_scalar_prefetch=1,
            grid=(4,),
            in_specs=[anywhere] * 5
            + [tokens_spec(width // GROUPS, block)] * GROUPS
            + [row_spec(width, block), pl.BlockSpec((1, 1, block), lambda t, w: (w[0], 0, t))],
            out_specs=[spec, spec, whole((8, 128)), whole((width, width))],
            scratch_shapes=[pltpu.SemaphoreType.DMA((4,))],
        ),
        [pltpu.HBM((width, length), LOW)] * 2
        + [jax.ShapeDtypeStruct((8, 128), FULL), pltpu.HBM((width, width), LOW)],
        2 * length * width * width,
        12 * length * width,
        vmem=20,
    )(where, own, *received, *mixed, x, segments)


def gelu_both(hidden):
    rate = 0.7978845608028654
    square = hidden * hidden
    half = 0.5 + 0.5 * jnp.tanh(hidden * (rate + (rate * 0.044715) * square))
    slope = half + hidden * (2.0 * rate + (6.0 * rate * 0.044715) * square) * (half - half * half)
    return hidden * half, slope


def chunks(length, count):
    return [slice(i * (length // count), (i + 1) * (length // count)) for i in range(count)]


def hidden_kernel(first, where_ref, own_ref, *refs):
    received, refs = refs[:8], refs[8:]
    (nm_hbm, ga_hbm, g_hbm) = refs[:3]
    (act_hbm, grad_hbm, keep_hbm, send_hbm) = refs[-15:-11]
    (weights, nm_ref, g_ref, ga_ref, act_ref, grad_ref, keep_ref, send_ref, w_sem, in_sem, out_sem) = refs[-11:]
    length = nm_ref.shape[1]

    def copies(place, do):
        weight_copies(
            first + 2 * place, 1, where_ref, own_ref, received[4 * place : 4 * place + 4], weights.at[place], w_sem.at[place], do
        )

    nm_copy = pltpu.make_async_copy(nm_hbm, nm_ref, in_sem.at[0])
    g_copy = pltpu.make_async_copy(g_hbm, g_ref, in_sem.at[1])
    ga_copies = [pltpu.make_async_copy(ga_hbm.at[first + 2 * i], ga_ref.at[i], in_sem.at[2 + i]) for i in range(2)]
    nm_copy.start()
    copies(0, lambda c: c.start())
    ga_copies[0].start()
    g_copy.start()
    copies(1, lambda c: c.start())
    ga_copies[1].start()
    hidden, sent = {}, []

    def send(source, target):
        copy = pltpu.make_async_copy(source, target, out_sem.at[len(sent)])
        copy.start()
        sent.append(copy)

    def enter(task):
        place, tokens = task
        hidden[task] = dot(weights[place], nm_ref[:, tokens], 0, 0)

    def bend(task):
        place, tokens = task
        value, slope = gelu_both(hidden.pop(task))
        act_ref[place, :, tokens] = value.astype(LOW)
        grad_ref[place, :, tokens] = (ga_ref[place, :, tokens].astype(FULL) * slope).astype(LOW)

    def down(place, which):
        rows = halves(where_ref, nm_ref.shape[0])[which][1]
        target, out = ((keep_ref, keep_hbm), (send_ref, send_hbm))[which]
        target[1, place] = dot(act_ref[place, rows, :], g_ref[...], 1, 1).astype(LOW)
        send(target.at[1, place], out.at[1, place])

    def up(place, which):
        rows = halves(where_ref, nm_ref.shape[0])[which][1]
        target, out = ((keep_ref, keep_hbm), (send_ref, send_hbm))[which]
        target[0, place] = dot(nm_ref[rows, :], grad_ref[place], 1, 1).astype(LOW)
        send(target.at[0, place], out.at[0, place])

    def finished(place):
        send(act_ref.at[place], act_hbm.at[place])
        send(grad_ref.at[place], grad_hbm.at[place])

    def tasks(place):
        return [(place, tokens) for tokens in chunks(length, 4)]

    nm_copy.wait()
    copies(0, lambda c: c.wait())
    ga_copies[0].wait()
    in_stages(tasks(0), (enter, bend))
    g_copy.wait()
    copies(1, lambda c: c.wait())
    ga_copies[1].wait()
    finished(0)
    between = [(down, 1), (down, 0), (up, 1), (up, 0)]
    last = None
    for task, (product, which) in zip(tasks(1), between, strict=True):
        enter(task)
        if last is not None:
            bend(last)
        product(0, which)
        last = task
    bend(last)
    finished(1)
    for product, which in between:
        product(1, which)
    for copy in sent:
        copy.wait()


def hidden_of(first, where, own, received, nm, ga, g, after=()):
    width, length = nm.shape
    anywhere = pl.BlockSpec(memory_space=pltpu.HBM)
    out_shape = [pltpu.HBM((2, width, length), LOW)] * 2 + [pltpu.HBM((2, 2, width // 2, width), LOW)] * 2
    return kernel_call(
        functools.partial(hidden_kernel, first),
        "hidden",
        pltpu.PrefetchScalarGridSpec(
            num_scalar_prefetch=1,
            grid=(1,),
            in_specs=[anywhere] * (12 + len(after)),
            out_specs=[anywhere] * 4,
            scratch_shapes=[
                pltpu.VMEM((2, width, width), LOW),
                pltpu.VMEM((width, length), LOW),
                pltpu.VMEM((width, length), LOW),
                pltpu.VMEM((2, width, length), LOW),
                pltpu.VMEM((2, width, length), LOW),
                pltpu.VMEM((2, width, length), LOW),
                pltpu.VMEM((2, 2, width // 2, width), LOW),
                pltpu.VMEM((2, 2, width // 2, width), LOW),
                pltpu.SemaphoreType.DMA((2, 4)),
                pltpu.SemaphoreType.DMA((4,)),
                pltpu.SemaphoreType.DMA((12,)),
            ],
        ),
        out_shape,
        14e9,
        14 * length * width,
        vmem=58,
    )(where, own, *[a for r in received for a in r], nm, ga, g, *after)


def output_kernel(where_ref, own_ref, *refs):
    received, refs = refs[:16], refs[16:]
    (act_a, act_b, grad_a, grad_b, down_ref, mid_ref, cot_ref, seg_ref) = refs[:8]
    (keep_out, send_out, gmid_ref, gab_ref, sums_ref, weights, sem) = refs[-7:]
    step = pl.program_id(0)
    width, length = mid_ref.shape

    def copies(do):
        for group in range(4):
            weight_copies(
                group, 1, where_ref, own_ref, received[4 * group : 4 * group + 4], weights.at[group], sem.at[group], do
            )

    @pl.when(step == 0)
    def _():
        copies(lambda c: c.start())
        copies(lambda c: c.wait())
        sums_ref[...] = jnp.zeros_like(sums_ref)

    on_attention = where_ref[0] == 0
    products = {}

    def multiply(tokens):
        out = grad = 0.0
        for group in range(4):
            act = (act_a, act_b)[group % 2][group // 2, :, tokens]
            slope_grad = (grad_a, grad_b)[group % 2][group // 2, :, tokens]
            out = out + dot(down_ref[group * width : (group + 1) * width, :], act, 0, 0)
            grad = grad + dot(weights[group], slope_grad)
        products[tokens] = out, grad

    def finish(tokens):
        out, grad = products.pop(tokens)
        middle = mid_ref[:, tokens]
        wide = widened(middle)
        output = (wide + compressed(out)).astype(LOW)
        lane = lax.broadcasted_iota(jnp.int32, sums_ref.shape, 1)
        sums_ref[...] += jnp.where(lane == 1, square_sum(output, seg_ref[0][:, tokens] > 0), 0.0)
        keep_out[:, tokens] = jnp.where(on_attention, middle, output)
        send_out[:, tokens] = jnp.where(on_attention, output, middle)
        normed, inverse = crms(wide)
        grad = (cot_ref[0, :, tokens].astype(FULL) + widened_back(crms_back(normed, inverse, grad))).astype(LOW)
        gmid_ref[:, tokens] = grad
        gab_ref[:, tokens] = compressed_back(grad).astype(LOW)

    in_stages(chunks(length, 2), (multiply, finish))


def output_of(where, own, received, acts, grads, down_weight, middle, cot, segments, after=()):
    width, length = middle.shape
    steps = 2
    block = length // steps
    anywhere = pl.BlockSpec(memory_space=pltpu.HBM)
    spec = tokens_spec(width, block)
    pair = pl.BlockSpec((2, width, block), lambda t, w: (0, 0, t))
    row = jax.ShapeDtypeStruct((width, length), LOW)
    return kernel_call(
        output_kernel,
        "output",
        pltpu.PrefetchScalarGridSpec(
            num_scalar_prefetch=1,
            grid=(steps,),
            in_specs=[anywhere] * 17
            + [pair] * 4
            + [whole(down_weight.shape), spec, row_spec(width, block)]
            + [pl.BlockSpec((1, 1, block), lambda t, w: (w[0], 0, t))]
            + [anywhere] * len(after),
            out_specs=[spec] * 4 + [whole((8, 128))],
            scratch_shapes=[pltpu.VMEM((4, width, width), LOW), pltpu.SemaphoreType.DMA((4, 4))],
        ),
        [row] * 4 + [jax.ShapeDtypeStruct((8, 128), FULL)],
        20e9,
        24 * length * width,
        vmem=40,
    )(where, own, *[a for r in received for a in r], *acts, *grads, down_weight, middle, cot, segments, *after)


def mixed_grad_kernel(where_ref, gab_ref, w_ref, *refs):
    mixed_refs, gm_refs, (delta_ref, keep_ref, send_ref, mixed_all) = refs[:GROUPS], refs[-GROUPS - 4 : -4], refs[-4:]
    gab = gab_ref[...]
    part = gm_refs[0].shape[0]
    heads = part // HEAD_DIM
    for group in range(GROUPS):
        rows = slice(group * part, (group + 1) * part)
        grads = dot(w_ref[rows, :], gab).astype(LOW)
        gm_refs[group][...] = grads
        mixed = mixed_refs[group][...]
        mixed_all[rows, :] = mixed
        product = grads.astype(FULL) * mixed.astype(FULL)
        for head in range(heads):
            delta_ref[group, head : head + 1, :] = jnp.sum(
                product[head * HEAD_DIM : (head + 1) * HEAD_DIM], axis=0, keepdims=True
            )
    for place, rows in halves(where_ref, mixed_all.shape[0]):
        (keep_ref, send_ref)[place][...] = dot(mixed_all[rows, :], gab, 1, 1).astype(LOW)


def mixed_grad(where, gab, w, mixed, after=()):
    width, length = gab.shape
    part = width // GROUPS
    heads = part // HEAD_DIM
    outs = kernel_call(
        mixed_grad_kernel,
        "mixed_grad",
        pltpu.PrefetchScalarGridSpec(
            num_scalar_prefetch=1,
            grid=(1,),
            in_specs=[whole((width, length)), whole((width, width))]
            + [whole((part, length))] * GROUPS
            + [pl.BlockSpec(memory_space=pltpu.HBM)] * len(after),
            out_specs=[whole((part, length))] * GROUPS
            + [whole((GROUPS, heads, length))]
            + [whole((width // 2, width))] * 2,
            scratch_shapes=[pltpu.VMEM((width, length), LOW)],
        ),
        [jax.ShapeDtypeStruct((part, length), LOW)] * GROUPS
        + [jax.ShapeDtypeStruct((GROUPS, heads, length), FULL)]
        + [jax.ShapeDtypeStruct((width // 2, width), LOW)] * 2,
        4 * length * width * width,
        8 * length * width,
        vmem=28,
    )(where, gab, w, *mixed, *after)
    return outs[:GROUPS], outs[GROUPS], outs[GROUPS + 1], outs[GROUPS + 2]


def input_grad_kernel(where_ref, x_ref, gmid_ref, *refs):
    grad_refs, w_refs, (keep_ref, *send_refs) = refs[:GROUPS], refs[GROUPS : 2 * GROUPS], refs[-3:]
    on_attention = where_ref[0] == 0
    grad_normed = dot(w_refs[0][...], grad_refs[0][...])
    for group in range(1, GROUPS):
        grad_normed = grad_normed + dot(w_refs[group][...], grad_refs[group][...])
    normed, inverse = crms(widened(x_ref[0]))
    middle = gmid_ref[...]
    grad = (middle.astype(FULL) + widened_back(crms_back(normed, inverse, grad_normed))).astype(LOW)
    keep_ref[...] = jnp.where(on_attention, grad, middle)
    sent = jnp.where(on_attention, middle, grad)
    for half, send_ref in enumerate(send_refs):

        @pl.when(pl.program_id(0) // 2 == half)
        def _(send_ref=send_ref):
            send_ref[...] = sent


def input_grad(where, x, grad_middle, grads, weights, after=()):
    width, length = grad_middle.shape
    spec = tokens_spec(width, length // 4)
    return kernel_call(
        input_grad_kernel,
        "input_grad",
        pltpu.PrefetchScalarGridSpec(
            num_scalar_prefetch=1,
            grid=(4,),
            in_specs=[row_spec(width, length // 4), spec]
            + [spec] * GROUPS
            + [whole((width, width))] * GROUPS
            + [pl.BlockSpec(memory_space=pltpu.HBM)] * len(after),
            out_specs=[
                spec,
                pl.BlockSpec((width, length // 4), lambda t, w: (0, jnp.minimum(t, 1))),
                pl.BlockSpec((width, length // 4), lambda t, w: (0, jnp.maximum(t - 2, 0))),
            ],
        ),
        [jax.ShapeDtypeStruct((width, length), LOW)] + [jax.ShapeDtypeStruct((width, length // 2), LOW)] * 2,
        6 * length * width * width,
        12 * length * width,
        vmem=30,
    )(where, x, grad_middle, *grads, *weights, *after)


def rows_kernel(where_ref, kept_ref, *refs):
    other_refs, out_ref = refs[:-1], refs[-1]
    kept = kept_ref[...].astype(FULL)
    half = pl.program_id(0) * len(other_refs) // pl.num_programs(0)
    other = other_refs[0][...].astype(FULL)
    if len(other_refs) > 1:
        other = jnp.where(half == 0, other, other_refs[1][...].astype(FULL))
    mine = where_ref[0] == 0
    out_ref[...] = jnp.stack([jnp.where(mine, kept, other), jnp.where(mine, other, kept)], axis=1).astype(LOW)


def rows_of(where, kept, others, after=()):
    width, length = kept.shape
    steps = 4
    block = length // steps
    part = steps // len(others)
    place = [
        lambda t, w, first=i * part: (0, jnp.clip(t - first, 0, part - 1)) for i in range(len(others))
    ]

    def body(where_ref, *refs):
        rows_kernel(where_ref, *refs[: 1 + len(others)], refs[-1])

    out = kernel_call(
        body,
        "rows",
        pltpu.PrefetchScalarGridSpec(
            num_scalar_prefetch=1,
            grid=(steps,),
            in_specs=[tokens_spec(width, block)]
            + [pl.BlockSpec((width, block), at) for at in place]
            + [pl.BlockSpec(memory_space=pltpu.HBM)] * len(after),
            out_specs=pl.BlockSpec((width, 2, block), lambda t, w: (0, 0, t)),
        ),
        pltpu.HBM((width - 1, 2, length), LOW),
        length,
        length,
        vmem=40,
    )(where, kept, *others, *after)
    return jnp.transpose(out, (1, 2, 0))[None]


def partner(block, distance):
    size = lax.axis_size("dp")
    return lax.ppermute(block, "dp", [(i, i ^ distance) for i in range(size)])


def across(block):
    return lax.ppermute(block, "section", [(0, 1), (1, 0)])


def split(left, right, distance):
    bit = (lax.axis_index("dp") & distance) // distance
    half = left.shape[1] // 2
    part = lambda a, at: lax.dynamic_slice_in_dim(a, at * half, half, 1)
    return add_low(part(left, bit), part(right, bit)), add_low(part(left, 1 - bit), part(right, 1 - bit))


def add_low(left, right):
    return (left.astype(FULL) + right.astype(FULL)).astype(LOW)


class Scatter:
    def __init__(self, keep, got, order):
        self.order = order
        self.keep, self.got = keep, got
        self.at = 0

    def step(self, *others):
        self.at += 1
        self.got = later(self.got, *others)
        self.keep, self.sent = split(self.keep, self.got, self.order[self.at])
        self.got = partner(self.sent, self.order[self.at])

    def total(self, *others):
        while self.at < len(self.order) - 1:
            self.step(*others)
        return add_low(self.keep, later(self.got, *others))


class Gather:
    def __init__(self, shard, order, *others):
        self.left = list(reversed(order))
        self.held = later(shard, *others)[None] if others else shard[None]
        self.got = partner(self.held, self.left.pop(0))

    def step(self, *others):
        self.held = jnp.concatenate([self.held, later(self.got, *others)], axis=0)
        self.got = partner(self.held, self.left.pop(0))

    def all(self, *others):
        while self.left:
            self.step(*others)
        return self.held, self.got


def number_of(order):
    me = lax.axis_index("dp").astype(jnp.int32)
    number = jnp.int32(0)
    for distance in order:
        number = number * 2 + (me // distance) % 2
    return number


def later(value, *others):
    return lax.optimization_barrier((value, *others))[0]


def gathered_specs(array, per_step):
    half_steps = array.shape[0] // per_step
    block = (per_step, *array.shape[1:])
    return [
        pl.BlockSpec(block, lambda e, w: (jnp.minimum(e, half_steps - 1), 0, 0)),
        pl.BlockSpec(block, lambda e, w: (jnp.maximum(e - half_steps, 0), 0, 0)),
    ]


def each_entry(number_ref, halves_refs, do):
    steps = pl.num_programs(0)
    per_step = halves_refs[0].shape[0]
    for place, ref in enumerate(halves_refs):

        @pl.when((pl.program_id(0) * 2 >= steps) == (place == 1))
        def _(ref=ref):
            for entry in range(per_step):
                do((number_ref[1] % per_step) ^ entry, ref, entry)


def down_sum_kernel(number_ref, near_ref, far_ref, out_ref):
    rows = out_ref.shape[2]

    def write(place, ref, entry):
        for block in range(2):
            out_ref[block, place] = ref[entry, block * rows : (block + 1) * rows, :].astype(FULL)

    each_entry(number_ref, (near_ref, far_ref), write)


def down_sum(number, near, far, width):
    entries = 2 * near.shape[0]
    rows = width // entries
    per_step = entries // 4
    out = kernel_call(
        down_sum_kernel,
        "down_sum",
        pltpu.PrefetchScalarGridSpec(
            num_scalar_prefetch=1,
            grid=(4,),
            in_specs=gathered_specs(near, per_step),
            out_specs=pl.BlockSpec((2, per_step, rows, width), lambda e, w: (0, (w[1] // per_step) ^ e, 0, 0)),
        ),
        jax.ShapeDtypeStruct((2, entries, rows, width), FULL),
        0,
        width,
        vmem=58,
    )(number, near, far)
    return out.reshape(2 * width, width)


def columns_of(numbers):
    if numbers[0] < 0:
        return [[(0, 3 * block, 3)] for block in (-numbers[0] - 1, -numbers[1] - 1)]
    return [
        [(0, 9, 3)] if block == 0 else [(piece, own_column_static(block - 1, piece, 0), 1) for piece in range(3)]
        for block in numbers
    ]


def counts_of(section, slots, width, near_ref, far_ref):
    rows = sum(ref[entry, :16, :128].astype(FULL) for ref in (near_ref, far_ref) for entry in range(ref.shape[0]))
    lane = lax.broadcasted_iota(jnp.int32, (1, 128), 1)
    total = [
        jnp.sum(jnp.where((lane % 3 == which) & (lane < 9), rows[:1], 0.0), axis=1, keepdims=True) for which in range(3)
    ]
    square = jnp.where(section == 0, total[0], total[1])
    count = jnp.where(section == 0, total[2], slots - total[2])
    root = jnp.sqrt(square / (total[2] * width))
    return jnp.broadcast_to(jnp.where(lane == 0, root, jnp.where(lane == 1, count, 0.0)), (8, 128))


def first_sum_kernel(skip, blocks, slots, number_ref, near_ref, far_ref, *refs):
    buffer, sem = refs[-2:]
    out_ref = refs[-4] if slots else refs[-3]
    entries, rows, columns = out_ref.shape
    width = columns // 4
    part = width // 3
    half = entries // 2
    if slots:
        refs[-3][...] = counts_of(number_ref[0], slots, width, near_ref, far_ref)
    for section in range(2):

        @pl.when(number_ref[0] == section)
        def _(section=section):
            pieces = columns_of(blocks[section])

            def copies(place, do):
                first = pl.multiple_of(jnp.where(number_ref[1] < half, place, 1 - place) * half, half)
                for at in range(2):
                    for order, (start, column, size) in enumerate(pieces[at]):
                        do(
                            pltpu.make_async_copy(
                                buffer.at[at, pl.ds(first, half), :, pl.ds(start * part, size * part)],
                                out_ref.at[pl.ds(first, half), :, pl.ds(column * part, size * part)],
                                sem.at[place, at, order],
                            )
                        )

            for place, ref in enumerate((near_ref, far_ref)):
                for entry in range(half):
                    for at in range(2):
                        values = ref[entry, skip + at * rows : skip + (at + 1) * rows, :]
                        buffer[at, number_ref[1] ^ (entry + place * half)] = values.astype(FULL)
                copies(place, lambda c: c.start())
            for place in range(2):
                copies(place, lambda c: c.wait())


def first_sum(number, skip, blocks, gathered, width, before=None, slots=None):
    near, far = gathered
    entries = 2 * near.shape[0]
    rows = width // entries
    held = [] if before is None else [before]
    anywhere = pl.BlockSpec(memory_space=pl.ANY)
    return pl.pallas_call(
        functools.partial(first_sum_kernel, skip, blocks, slots),
        grid_spec=pltpu.PrefetchScalarGridSpec(
            num_scalar_prefetch=1,
            grid=(1,),
            in_specs=[whole(near.shape), whole(far.shape)] + [anywhere] * len(held),
            out_specs=[anywhere] + [whole((8, 128))] * bool(slots),
            scratch_shapes=[pltpu.VMEM((2, entries, rows, width), FULL), pltpu.SemaphoreType.DMA((2, 2, 3))],
        ),
        out_shape=[jax.ShapeDtypeStruct((entries, rows, 4 * width), FULL)]
        + [jax.ShapeDtypeStruct((8, 128), FULL)] * bool(slots),
        input_output_aliases={3: 0} if held else {},
        compiler_params=pltpu.CompilerParams(vmem_limit_bytes=24 * 2**20),
        cost_estimate=pl.CostEstimate(flops=1000, bytes_accessed=1000, transcendentals=0),
        name="first_sum",
    )(number, near, far, *held)


def on_device(stream_in, cotangent, weights_first, down_weight, segments):
    rows_dev, length, compact_width = stream_in.shape
    width = compact_width + 1
    section = lax.axis_index("section").astype(jnp.int32)
    index = lax.axis_index("dp").astype(jnp.int32)
    size = lax.axis_size("dp")
    on_attention = section == 0
    where = jnp.stack([section, index & 3, index & 1])
    segments3 = segments.reshape(rows_dev, 1, length)
    order = [1 << i for i in range(size.bit_length() - 1)]
    flat = lambda a: a.reshape(-1, width)

    near = [across(piece) for piece in weight_piece(where, weights_first)]
    x, cot = jnp.transpose(stream_in, (0, 2, 1)), jnp.transpose(cotangent, (0, 2, 1))
    nt, g = prep(where, x, cot)
    ga = branch_grad(g, down_weight, after=(near[0],))
    attended, received, besides = [], [], [partner(later(near[0], nt), 2), partner(later(near[1], ga), 2)]
    for group in range(4):
        quarter, beside = near[group], besides[group]
        done = [attended[group - 1][1] if group else ga]
        received.append((quarter, beside, partner(quarter, 1), partner(later(beside, *done), 1)))
        if group < 2:
            besides.append(partner(later(near[group + 2], *done), 2))
        if group < GROUPS:
            attended.append(attend(group, where, weights_first, received[group], nt, segments3))
    mixed = [a[1] for a in attended]
    middle, nm, sums_mid, out_weights = middle_of(where, weights_first, received[GROUPS], mixed, x, segments3)

    act_a, grad_a, kept_a, sent_a = hidden_of(0, where, weights_first, received[0::2], nm, ga, g)
    got_a = partner(sent_a, 1)
    up_a = Scatter(kept_a[0], got_a[0], order)
    up_a.step()
    act_b, grad_b, kept_b, sent_b = hidden_of(1, where, weights_first, received[1::2], nm, ga, g, after=(up_a.sent,))
    up_a.step(act_b)
    got_b = partner(later(sent_b, up_a.sent), 1)
    up_b = Scatter(kept_b[0], got_b[0], order)
    up_b.step()
    kept, sent = [], []
    for keep, got in ((kept_a[1], got_a[1]), (kept_b[1], got_b[1])):
        lower, upper = add_low(keep[0], got[0]), add_low(keep[1], got[1])
        kept.append(jnp.where(on_attention, lower, upper))
        sent.append(jnp.where(on_attention, upper, lower))
    kept, sent = jnp.stack(kept), later(jnp.stack(sent), up_b.sent)
    down = Scatter(kept, across(sent), order)
    keep_out, send_out, grad_mid, gab, sums_out = output_of(
        where, weights_first, received, (act_a, act_b), (grad_a, grad_b), down_weight, middle, cot, segments3, after=(sent,)
    )
    up_a.step(gab)
    up_b.step(up_a.sent)
    down.step(up_b.sent)
    gm, delta, keep_w, send_w = mixed_grad(where, gab, out_weights, mixed, after=(down.sent,))
    keeps, sends, grads = [keep_w], [send_w], []

    def backward(group, *after):
        qkv, _, total, _ = attended[group]
        keep_w, send_w, grad = attend_back(where, qkv, gm[group], total, delta[group], segments3, nt, after=after)
        keeps.append(keep_w)
        sends.append(send_w)
        grads.append(grad)

    up_a = up_a.total(delta)
    backward(0, up_a)
    up_b.step(grads[0])
    down.step(up_b.sent)
    sent_a = later(jnp.stack(sends), down.sent)
    attn_a = Scatter(jnp.stack(keeps), partner(sent_a, 1), order)
    backward(1, sent_a)
    attn_a.step(grads[1])
    down.step(attn_a.sent)
    up_b = up_b.total(grads[1])
    rows = up_a.shape[1]
    received_out = across(send_out)
    backward(2, down.sent, up_b)
    down = down.total(grads[2])
    sum_dn = Gather(flat(down), order)
    attn_a.step(sum_dn.held)
    attn_b = Scatter(jnp.stack(keeps[2:]), partner(later(jnp.stack(sends[2:]), attn_a.sent), 1), order)
    attn_b.step()
    keep_grad, *send_grad = input_grad(
        where, x, grad_mid, grads, [a[3] for a in attended], after=(attn_b.sent, received_out)
    )
    received_grad = [across(send_grad[0])]
    sum_dn.step(keep_grad)
    attn_a.step(sum_dn.held)
    attn_b.step(attn_a.sent)
    sum_dn.step(attn_b.sent)
    attn_a = attn_a.total(sum_dn.held)

    scalars = (sums_mid + sums_out)[0, :3]

    def scalar_rows(values):
        high = values.astype(LOW)
        rest = values - high.astype(FULL)
        middle_part = rest.astype(LOW)
        low = (rest - middle_part.astype(FULL)).astype(LOW)
        packed = jnp.concatenate([high, middle_part, low])
        return jnp.zeros((16, width), LOW).at[0, :9].set(packed)

    def scalars_of(block):
        parts = block[..., 0, :9].astype(FULL)
        return parts[..., :3] + parts[..., 3:6] + parts[..., 6:9]

    mine_a, theirs_a = jnp.where(on_attention, attn_a, up_a), jnp.where(on_attention, up_a, attn_a)
    sent_a = jnp.concatenate([scalar_rows(scalars), flat(theirs_a)])
    swapped = across(sent_a)
    attn_b.step(sent_a)
    swapped = later(swapped, attn_b.sent, received_grad[0])
    pair = scalars + scalars_of(swapped[:16])
    shard_a = add_low(flat(mine_a), swapped[16:])
    sum_a = Gather(jnp.concatenate([scalar_rows(pair), shard_a]), order)
    attn_b = attn_b.total(sum_a.held)
    mine_b, theirs_b = jnp.where(on_attention, attn_b, up_b), jnp.where(on_attention, up_b, attn_b)
    swapped_b = across(flat(theirs_b))
    sum_dn.step(theirs_b)
    sum_b = Gather(add_low(flat(mine_b), later(swapped_b, sum_dn.held)), order)
    received_grad.append(across(later(send_grad[1], sum_b.held)))
    sum_a.step(sum_b.held)
    number = jnp.stack([section, number_of(order)])
    grad_down = down_sum(later(number, sum_a.held), *sum_dn.all(), width)
    sum_b.step(grad_down)
    sum_a.step(sum_b.held)
    stream_out = rows_of(where, keep_out, [received_out], after=(sum_a.held,))
    sum_b.step(stream_out)
    stream_grad = rows_of(where, keep_grad, received_grad, after=(sum_b.held,))
    sum_a.step(stream_grad)
    sum_b.step(sum_a.held)
    sum_a, sum_b = sum_a.all(), sum_b.all()
    slots = float(rows_dev * length * size)
    grad_first, counts = first_sum(later(number, sum_b[0]), 16, ((0, 1), (-1, -3)), sum_a, width, slots=slots)
    (grad_first,) = first_sum(number, 0, ((2, 3), (-2, -4)), sum_b, width, before=grad_first)
    grad_first = grad_first.reshape(width, 4 * width)
    residual_rms, token_count = counts[0, :1], counts[0, 1:2].astype(jnp.int32)
    return (
        stream_out,
        stream_grad,
        grad_first[None],
        grad_down,
        residual_rms,
        token_count,
    )


def solution(mesh):
    placed = (
        P("dp", None, None),
        P("dp", None, None),
        P("section", None, None),
        P(),
        P("dp", None),
    )
    return jax.shard_map(
        on_device,
        mesh=mesh,
        in_specs=placed,
        out_specs=(
            P("section", "dp", None, None),
            P("section", "dp", None, None),
            P("section", None, None),
            P("section", None),
            P("section"),
            P("section"),
        ),
        check_vma=False,
    )
```

```python
import functools

import jax
import jax.numpy as jnp
from jax import lax
from jax.experimental import pallas as pl
from jax.experimental.pallas import tpu as pltpu
from jax.sharding import PartitionSpec as P

HEADS = 12
HEAD_DIM = 64
GROUPS = 3
EPSILON = 1e-06
MASKED = -1e30
SCALE = HEAD_DIM ** (-0.5)
LOG2E = 1.4426950408889634
LOW = jnp.bfloat16
FULL = jnp.float32


def dot(left, right, left_dim=1, right_dim=0):
    return lax.dot_general(
        left, right, (((left_dim,), (right_dim,)), ((), ())), preferred_element_type=FULL
    )


def kernel_call(body, name, grid_spec, out_shape, flops, moved, vmem=32):
    return pl.pallas_call(
        body,
        grid_spec=grid_spec,
        out_shape=out_shape,
        compiler_params=pltpu.CompilerParams(vmem_limit_bytes=vmem * 2**20),
        cost_estimate=pl.CostEstimate(flops=int(flops * 3), bytes_accessed=int(moved * 3), transcendentals=0),
        name=name,
    )


def last_row(block):
    return lax.broadcasted_iota(jnp.int32, block.shape, 0) == block.shape[0] - 1


def widened(block):
    values = jnp.where(last_row(block), 0.0, block.astype(FULL))
    return jnp.where(last_row(block), -jnp.sum(values, axis=0, keepdims=True), values)


def crms(values):
    inverse = lax.rsqrt(jnp.mean(values * values, axis=0, keepdims=True) + EPSILON)
    return values * inverse, inverse


def crms_back(normed, inverse, grad):
    return inverse * (grad - normed * jnp.mean(grad * normed, axis=0, keepdims=True))


def compressed(branch):
    return branch - jnp.mean(branch, axis=0, keepdims=True)


def widened_back(grad):
    return grad - grad[grad.shape[0] - 1 :]


def compressed_back(block):
    values = jnp.where(last_row(block), 0.0, block.astype(FULL))
    return values - jnp.mean(values, axis=0, keepdims=True)


def square_sum(rounded, valid):
    wide = widened(rounded)
    per_token = jnp.sum(wide * wide, axis=0, keepdims=True)
    return jnp.sum(jnp.where(valid, per_token, 0.0), axis=1, keepdims=True)


def prep_kernel(where_ref, x_ref, cot_ref, nt_ref, g_ref):
    normed, _ = crms(widened(x_ref[0]))
    nt_ref[...] = normed.astype(LOW)
    g_ref[...] = compressed_back(cot_ref[0]).astype(LOW)


def tokens_spec(width, block):
    return pl.BlockSpec((width, block), lambda t, *_: (0, t))


def row_spec(width, block):
    return pl.BlockSpec((1, width, block), lambda t, w: (w[0], 0, t))


def prep(where, x, cot):
    width, length = x.shape[1] + 1, x.shape[2]
    spec = tokens_spec(width, length // 4)
    return kernel_call(
        prep_kernel,
        "prep",
        pltpu.PrefetchScalarGridSpec(
            num_scalar_prefetch=1, grid=(4,), in_specs=[row_spec(width, length // 4)] * 2, out_specs=[spec] * 2
        ),
        [jax.ShapeDtypeStruct((width, length), LOW)] * 2,
        0,
        8 * length * width,
        vmem=16,
    )(where, x, cot)


def branch_grad_kernel(g_ref, w_ref, *refs):
    out_ref = refs[-1]
    out_ref[0] = dot(w_ref[...], g_ref[...]).astype(LOW)


def branch_grad(g, down_weight, after=()):
    width, length = g.shape
    blocks = down_weight.shape[0] // width
    return kernel_call(
        branch_grad_kernel,
        "branch_grad",
        pltpu.PrefetchScalarGridSpec(
            num_scalar_prefetch=0,
            grid=(blocks,),
            in_specs=[
                pl.BlockSpec((width, length), lambda b: (0, 0)),
                pl.BlockSpec((width, width), lambda b: (b, 0)),
            ]
            + [pl.BlockSpec(memory_space=pltpu.HBM)] * len(after),
            out_specs=pl.BlockSpec((1, width, length), lambda b: (b, 0, 0)),
        ),
        pltpu.HBM((blocks, width, length), LOW),
        2 * length * width * width * blocks,
        2 * length * width * (blocks + 1),
        vmem=20,
    )(g, down_weight, *after)


def own_column_static(group, piece, section):
    if section == 1 or group == GROUPS:
        return 3 * group + piece
    return group + GROUPS * piece


def piece_kernel(where_ref, w_ref, *out_refs):
    part = out_refs[0].shape[1] // 3
    for section in range(2):

        @pl.when(where_ref[0] == section)
        def _(section=section):
            for group in range(4):
                for piece in range(3):
                    column = own_column_static(group, piece, section) * part
                    out_refs[group][:, piece * part : (piece + 1) * part] = w_ref[0, :, column : column + part]


def weight_piece(where, weights):
    rows, columns = weights.shape[1:]
    shape = (rows // 4, columns // 4)
    return kernel_call(
        piece_kernel,
        "weight_piece",
        pltpu.PrefetchScalarGridSpec(
            num_scalar_prefetch=1,
            grid=(1,),
            in_specs=[pl.BlockSpec((1, rows // 4, columns), lambda i, w: (0, w[1], 0))],
            out_specs=[whole(shape)] * 4,
        ),
        [jax.ShapeDtypeStruct(shape, LOW)] * 4,
        0,
        rows * columns,
        vmem=58,
    )(where, weights)


def weight_copies(group, wanted, where_ref, own_ref, quarters, target, sem, act):
    quarter = target.shape[0] // 4
    part = target.shape[1] // 3

    @pl.when(where_ref[0] == wanted)
    def _():
        for piece in range(3):
            column = own_column_static(group, piece, wanted) * part
            act(pltpu.make_async_copy(own_ref.at[0, :, pl.ds(column, part)], target.at[:, pl.ds(piece * part, part)], sem.at[piece]))

    @pl.when(where_ref[0] != wanted)
    def _():
        for place, source in enumerate(quarters):
            index = where_ref[1] ^ (0, 2, 1, 3)[place]
            act(pltpu.make_async_copy(source, target.at[pl.ds(index * quarter, quarter), :], sem.at[place]))


def segment_rows(segment):
    tokens = segment.shape[1]
    ids = lax.broadcasted_iota(jnp.int32, (16, tokens), 0)
    same = segment == ids
    real = ids < 5
    queries = jnp.where(real & jnp.logical_not(same), MASKED, 0.0).astype(LOW)
    keys = jnp.where(real & same, 1.0, 0.0).astype(LOW)
    return queries, keys


def two_parts(values):
    high = values.astype(LOW)
    return high, (values - high.astype(FULL)).astype(LOW)


def minus_rows(values):
    high = values.astype(LOW)
    rest = values - high.astype(FULL)
    middle = rest.astype(LOW)
    low = rest - middle.astype(FULL)
    row = lax.broadcasted_iota(jnp.int32, (16, values.shape[1]), 0)
    parts = jnp.where(
        row == 0, high.astype(FULL), jnp.where(row == 1, middle.astype(FULL), jnp.where(row == 2, low, 0.0))
    )
    return (-parts).astype(LOW)


def three_ones(tokens):
    return jnp.where(lax.broadcasted_iota(jnp.int32, (16, tokens), 0) < 3, 1.0, 0.0).astype(LOW)


def head_tasks(heads, blocks, block):
    return [
        (head, slice(i * block, (i + 1) * block), slice(0, (i + 1) * block), i * block)
        for head in range(heads)
        for i in range(blocks)
    ]


def in_stages(tasks, stages):
    for step in range(len(tasks) + len(stages) - 1):
        for late, stage in enumerate(stages):
            if 0 <= step - late < len(tasks):
                stage(tasks[step - late])


def attend_kernel(group, where_ref, own_ref, near_ref, beside_ref, core_ref, across_ref, nt_ref, seg_ref, qkv_ref, mixed_ref, total_ref, w_ref, sem):
    copies = functools.partial(
        weight_copies, group, 0, where_ref, own_ref, (near_ref, beside_ref, core_ref, across_ref), w_ref, sem
    )
    copies(lambda c: c.start())
    copies(lambda c: c.wait())
    length = nt_ref.shape[1]
    width = qkv_ref.shape[0] // 3
    heads, blocks = width // HEAD_DIM, 4
    block = length // blocks
    for part in range(3):
        qkv_ref[part * width : (part + 1) * width, :] = dot(
            w_ref[:, part * width : (part + 1) * width], nt_ref[...], 0, 0
        ).astype(LOW)
    seg_queries, seg_keys = segment_rows(seg_ref[0])
    causal = lax.broadcasted_iota(jnp.int32, (block, block), 0) <= lax.broadcasted_iota(jnp.int32, (block, block), 1)
    ones = three_ones(length)
    scored, weighed = {}, {}

    def score(task):
        head, queries, keys, _ = task
        high, low = two_parts(qkv_ref[head * HEAD_DIM : (head + 1) * HEAD_DIM, queries].astype(FULL) * (SCALE * LOG2E))
        key_rows = qkv_ref[width + head * HEAD_DIM : width + (head + 1) * HEAD_DIM, keys]
        scored[task] = dot(
            jnp.concatenate([key_rows, key_rows, seg_keys[:, keys]], axis=0),
            jnp.concatenate([high, low, seg_queries[:, queries]], axis=0),
            0,
            0,
        )

    def weigh(task):
        before = task[3]
        scores = scored.pop(task)
        last = jnp.where(causal, scores[before:], MASKED)
        highest = jnp.max(last, axis=0, keepdims=True)
        if before:
            highest = jnp.maximum(highest, jnp.max(scores[:before], axis=0, keepdims=True))
        exponents = jnp.exp2(last - highest).astype(LOW)
        if before:
            exponents = jnp.concatenate([jnp.exp2(scores[:before] - highest).astype(LOW), exponents], axis=0)
        weighed[task] = (exponents, highest)

    def mix(task):
        head, queries, keys, _ = task
        exponents, highest = weighed.pop(task)
        values = qkv_ref[2 * width + head * HEAD_DIM : 2 * width + (head + 1) * HEAD_DIM, keys]
        mixed = dot(jnp.concatenate([values, ones[:, keys]], axis=0), exponents)
        total = mixed[HEAD_DIM : HEAD_DIM + 1]
        mixed_ref[head * HEAD_DIM : (head + 1) * HEAD_DIM, queries] = (mixed[:HEAD_DIM] / total).astype(LOW)
        total_ref[head : head + 1, queries] = highest + jnp.log2(total)

    in_stages(head_tasks(heads, blocks, block), (score, weigh, mix))


def attend(group, where, own, received, nt, segments):
    width, length = nt.shape
    part = width // GROUPS
    anywhere = pl.BlockSpec(memory_space=pltpu.HBM)
    return kernel_call(
        functools.partial(attend_kernel, group),
        "attend",
        pltpu.PrefetchScalarGridSpec(
            num_scalar_prefetch=1,
            grid=(1,),
            in_specs=[anywhere] * 5
            + [
                pl.BlockSpec((width, length), lambda i, w: (0, 0)),
                pl.BlockSpec((1, 1, length), lambda i, w: (w[0], 0, 0)),
            ],
            out_specs=[
                pl.BlockSpec((3 * part, length), lambda i, w: (0, 0)),
                pl.BlockSpec((part, length), lambda i, w: (0, 0)),
                pl.BlockSpec((part // HEAD_DIM, length), lambda i, w: (0, 0)),
                pl.BlockSpec((width, 3 * part), lambda i, w: (0, 0)),
            ],
            scratch_shapes=[pltpu.SemaphoreType.DMA((4,))],
        ),
        [
            pltpu.HBM((3 * part, length), LOW),
            jax.ShapeDtypeStruct((part, length), LOW),
            pltpu.HBM((part // HEAD_DIM, length), FULL),
            pltpu.HBM((width, 3 * part), LOW),
        ],
        4.5e9,
        8 * width * length,
        vmem=24,
    )(where, own, *received, nt, segments)


def attend_back_kernel(where_ref, qkv_ref, gm_ref, total_ref, delta_ref, seg_ref, nt_ref, *rest):
    keep_ref, send_ref, grads_ref, acc = rest[-4:]
    length = nt_ref.shape[1]
    width = gm_ref.shape[0]
    heads, blocks = width // HEAD_DIM, 4
    block = length // blocks
    seg_queries, seg_keys = segment_rows(seg_ref[0])
    ones = three_ones(length)
    causal = lax.broadcasted_iota(jnp.int32, (block, block), 1) <= lax.broadcasted_iota(jnp.int32, (block, block), 0)
    acc[...] = jnp.zeros_like(acc)
    scored, weighed = {}, {}

    def rows(part, head):
        return slice(part * width + head * HEAD_DIM, part * width + (head + 1) * HEAD_DIM)

    def score(task):
        head, queries, keys, _ = task
        high, low = two_parts(qkv_ref[rows(0, head), queries].astype(FULL) * (SCALE * LOG2E))
        key_rows = qkv_ref[rows(1, head), keys]
        scores = dot(
            jnp.concatenate([high, low, seg_queries[:, queries], minus_rows(total_ref[head : head + 1, queries])], axis=0),
            jnp.concatenate([key_rows, key_rows, seg_keys[:, keys], ones[:, keys]], axis=0),
            0,
            0,
        )
        grads = dot(
            jnp.concatenate([gm_ref[rows(0, head), queries], minus_rows(delta_ref[head : head + 1, queries])], axis=0),
            jnp.concatenate([qkv_ref[rows(2, head), keys], ones[:, keys]], axis=0),
            0,
            0,
        )
        scored[task] = (scores, grads)

    def weigh(task):
        before = task[3]
        scores, grads = scored.pop(task)
        last = jnp.where(causal, scores[:, before:], MASKED)
        if before:
            last = jnp.concatenate([scores[:, :before], last], axis=1)
        probs = jnp.exp2(last)
        weighed[task] = (probs.astype(LOW), (probs * grads).astype(LOW))

    def collect(task):
        head, queries, keys, _ = task
        probs, grads = weighed.pop(task)
        acc[rows(2, head), keys] += dot(gm_ref[rows(0, head), queries], probs)
        acc[rows(1, head), keys] += dot(qkv_ref[rows(0, head), queries] * LOW(SCALE), grads)
        acc[rows(0, head), queries] = dot(qkv_ref[rows(1, head), keys], grads, 1, 1) * SCALE

    in_stages(head_tasks(heads, blocks, block), (score, weigh, collect))
    grads_ref[...] = acc[...].astype(LOW)
    for place, rows_ in halves(where_ref, nt_ref.shape[0]):
        (keep_ref, send_ref)[place][...] = dot(nt_ref[rows_, :], grads_ref[...], 1, 1).astype(LOW)


def halves(where_ref, count):
    half = count // 2
    return [
        (0, pl.ds(pl.multiple_of(where_ref[2] * half, half), half)),
        (1, pl.ds(pl.multiple_of((1 - where_ref[2]) * half, half), half)),
    ]


def whole(shape):
    return pl.BlockSpec(shape, lambda *_: (0,) * len(shape))


def attend_back(where, qkv, gm, total, delta, segments, nt, after=()):
    width, length = nt.shape
    part = gm.shape[0]
    arrays = [qkv, gm, total, delta]
    return kernel_call(
        attend_back_kernel,
        "attend_back",
        pltpu.PrefetchScalarGridSpec(
            num_scalar_prefetch=1,
            grid=(1,),
            in_specs=[whole(a.shape) for a in arrays]
            + [pl.BlockSpec((1, 1, length), lambda i, w: (w[0], 0, 0)), whole(nt.shape)]
            + [pl.BlockSpec(memory_space=pltpu.HBM)] * len(after),
            out_specs=[whole((width // 2, 3 * part))] * 2 + [whole((3 * part, length))],
            scratch_shapes=[pltpu.VMEM((3 * part, length), FULL)],
        ),
        [jax.ShapeDtypeStruct((width // 2, 3 * part), LOW)] * 2 + [pltpu.HBM((3 * part, length), LOW)],
        9e9,
        8 * width * length,
        vmem=28,
    )(where, *arrays, segments, nt, *after)


def middle_kernel(where_ref, own_ref, near_ref, beside_ref, core_ref, across_ref, *refs):
    mixed_refs, (x_ref, seg_ref, mid_ref, nm_ref, sums_ref, w_ref, sem) = refs[:GROUPS], refs[GROUPS:]
    step = pl.program_id(0)

    @pl.when(step == 0)
    def _():
        copies = functools.partial(
            weight_copies, GROUPS, 0, where_ref, own_ref, (near_ref, beside_ref, core_ref, across_ref), w_ref, sem
        )
        copies(lambda c: c.start())
        copies(lambda c: c.wait())
        sums_ref[...] = jnp.zeros_like(sums_ref)

    mixed = jnp.concatenate([ref[...] for ref in mixed_refs], axis=0)
    branch = dot(w_ref[...], mixed, 0, 0)
    middle = (x_ref[0].astype(FULL) + compressed(branch)).astype(LOW)
    mid_ref[...] = middle
    normed, _ = crms(widened(middle))
    nm_ref[...] = normed.astype(LOW)
    valid = seg_ref[0] > 0
    lane = lax.broadcasted_iota(jnp.int32, sums_ref.shape, 1)
    count = jnp.sum(valid.astype(FULL), axis=1, keepdims=True)
    sums_ref[...] += jnp.where(lane == 0, square_sum(middle, valid), 0.0) + jnp.where(lane == 2, count, 0.0)


def middle_of(where, own, received, mixed, x, segments):
    width, length = x.shape[1] + 1, x.shape[2]
    block = length // 4
    anywhere = pl.BlockSpec(memory_space=pltpu.HBM)
    spec = tokens_spec(width, block)
    return kernel_call(
        middle_kernel,
        "middle",
        pltpu.PrefetchScalarGridSpec(
            num_scalar_prefetch=1,
            grid=(4,),
            in_specs=[anywhere] * 5
            + [tokens_spec(width // GROUPS, block)] * GROUPS
            + [row_spec(width, block), pl.BlockSpec((1, 1, block), lambda t, w: (w[0], 0, t))],
            out_specs=[spec, spec, whole((8, 128)), whole((width, width))],
            scratch_shapes=[pltpu.SemaphoreType.DMA((4,))],
        ),
        [pltpu.HBM((width, length), LOW)] * 2
        + [jax.ShapeDtypeStruct((8, 128), FULL), pltpu.HBM((width, width), LOW)],
        2 * length * width * width,
        12 * length * width,
        vmem=20,
    )(where, own, *received, *mixed, x, segments)


def gelu_both(hidden):
    rate = 0.7978845608028654
    square = hidden * hidden
    half = 0.5 + 0.5 * jnp.tanh(hidden * (rate + (rate * 0.044715) * square))
    slope = half + hidden * (2.0 * rate + (6.0 * rate * 0.044715) * square) * (half - half * half)
    return hidden * half, slope


def chunks(length, count):
    return [slice(i * (length // count), (i + 1) * (length // count)) for i in range(count)]


def hidden_kernel(first, where_ref, own_ref, *refs):
    received, refs = refs[:8], refs[8:]
    (nm_hbm, ga_hbm, g_hbm) = refs[:3]
    (act_hbm, grad_hbm, w_hbm, *sums_hbm) = refs[-17:-10]
    (weights, nm_ref, g_ref, ga_ref, act_ref, grad_ref, sums_ref, w_sem, in_sem, out_sem) = refs[-10:]
    length = nm_ref.shape[1]

    def copies(place, do):
        weight_copies(
            first + 2 * place, 1, where_ref, own_ref, received[4 * place : 4 * place + 4], weights.at[place], w_sem.at[place], do
        )

    nm_copy = pltpu.make_async_copy(nm_hbm, nm_ref, in_sem.at[0])
    g_copy = pltpu.make_async_copy(g_hbm, g_ref, in_sem.at[1])
    ga_copies = [pltpu.make_async_copy(ga_hbm.at[first + 2 * i], ga_ref.at[i], in_sem.at[2 + i]) for i in range(2)]
    nm_copy.start()
    copies(0, lambda c: c.start())
    ga_copies[0].start()
    g_copy.start()
    copies(1, lambda c: c.start())
    ga_copies[1].start()
    hidden, sent = {}, []

    def send(source, target):
        copy = pltpu.make_async_copy(source, target, out_sem.at[len(sent)])
        copy.start()
        sent.append(copy)

    def enter(task):
        place, tokens = task
        hidden[task] = dot(weights[place], nm_ref[:, tokens], 0, 0)

    def bend(task):
        place, tokens = task
        value, slope = gelu_both(hidden.pop(task))
        act_ref[place, :, tokens] = value.astype(LOW)
        grad_ref[place, :, tokens] = (ga_ref[place, :, tokens].astype(FULL) * slope).astype(LOW)

    def down(place, which):
        rows = halves(where_ref, nm_ref.shape[0])[which][1]
        sums_ref[2 + which, place] = dot(act_ref[place, rows, :], g_ref[...], 1, 1).astype(LOW)
        send(sums_ref.at[2 + which, place], sums_hbm[2 + which].at[place])

    def up(place, which):
        rows = halves(where_ref, nm_ref.shape[0])[which][1]
        sums_ref[which, place] = dot(nm_ref[rows, :], grad_ref[place], 1, 1).astype(LOW)
        send(sums_ref.at[which, place], sums_hbm[which].at[place])

    def finished(place):
        send(weights.at[place], w_hbm.at[place])
        send(act_ref.at[place], act_hbm.at[place])
        send(grad_ref.at[place], grad_hbm.at[place])

    def tasks(place):
        return [(place, tokens) for tokens in chunks(length, 4)]

    nm_copy.wait()
    copies(0, lambda c: c.wait())
    ga_copies[0].wait()
    in_stages(tasks(0), (enter, bend))
    g_copy.wait()
    copies(1, lambda c: c.wait())
    ga_copies[1].wait()
    finished(0)
    between = [(down, 1), (down, 0), (up, 1), (up, 0)]
    last = None
    for task, (product, which) in zip(tasks(1), between, strict=True):
        enter(task)
        if last is not None:
            bend(last)
        product(0, which)
        last = task
    bend(last)
    finished(1)
    for product, which in between:
        product(1, which)
    for copy in sent:
        copy.wait()


def hidden_of(first, where, own, received, nm, ga, g, after=()):
    width, length = nm.shape
    anywhere = pl.BlockSpec(memory_space=pltpu.HBM)
    out_shape = (
        [pltpu.HBM((2, width, length), LOW)] * 2
        + [pltpu.HBM((2, width, width), LOW)]
        + [pltpu.HBM((2, width // 2, width), LOW)] * 4
    )
    return kernel_call(
        functools.partial(hidden_kernel, first),
        "hidden",
        pltpu.PrefetchScalarGridSpec(
            num_scalar_prefetch=1,
            grid=(1,),
            in_specs=[anywhere] * (12 + len(after)),
            out_specs=[anywhere] * 7,
            scratch_shapes=[
                pltpu.VMEM((2, width, width), LOW),
                pltpu.VMEM((width, length), LOW),
                pltpu.VMEM((width, length), LOW),
                pltpu.VMEM((2, width, length), LOW),
                pltpu.VMEM((2, width, length), LOW),
                pltpu.VMEM((2, width, length), LOW),
                pltpu.VMEM((4, 2, width // 2, width), LOW),
                pltpu.SemaphoreType.DMA((2, 4)),
                pltpu.SemaphoreType.DMA((4,)),
                pltpu.SemaphoreType.DMA((14,)),
            ],
        ),
        out_shape,
        14e9,
        14 * length * width,
        vmem=58,
    )(where, own, *[a for r in received for a in r], nm, ga, g, *after)


def output_kernel(where_ref, *refs):
    (act_a, act_b, grad_a, grad_b, up_a, up_b, down_ref, mid_ref, cot_ref, seg_ref) = refs[:10]
    (keep_out, send_out, gmid_ref, gab_ref, sums_ref) = refs[-5:]
    step = pl.program_id(0)
    width, length = mid_ref.shape

    @pl.when(step == 0)
    def _():
        sums_ref[...] = jnp.zeros_like(sums_ref)

    on_attention = where_ref[0] == 0
    products = {}

    def multiply(tokens):
        out = grad = 0.0
        for group in range(4):
            act = (act_a, act_b)[group % 2][group // 2, :, tokens]
            slope_grad = (grad_a, grad_b)[group % 2][group // 2, :, tokens]
            out = out + dot(down_ref[group * width : (group + 1) * width, :], act, 0, 0)
            grad = grad + dot((up_a, up_b)[group % 2][group // 2], slope_grad)
        products[tokens] = out, grad

    def finish(tokens):
        out, grad = products.pop(tokens)
        middle = mid_ref[:, tokens]
        wide = widened(middle)
        output = (wide + compressed(out)).astype(LOW)
        lane = lax.broadcasted_iota(jnp.int32, sums_ref.shape, 1)
        sums_ref[...] += jnp.where(lane == 1, square_sum(output, seg_ref[0][:, tokens] > 0), 0.0)
        keep_out[:, tokens] = jnp.where(on_attention, middle, output)
        send_out[:, tokens] = jnp.where(on_attention, output, middle)
        normed, inverse = crms(wide)
        grad = (cot_ref[0, :, tokens].astype(FULL) + widened_back(crms_back(normed, inverse, grad))).astype(LOW)
        gmid_ref[:, tokens] = grad
        gab_ref[:, tokens] = compressed_back(grad).astype(LOW)

    in_stages(chunks(length, 2), (multiply, finish))


def output_of(where, acts, grads, ups, down_weight, middle, cot, segments, after=()):
    width, length = middle.shape
    steps = 2
    block = length // steps
    spec = tokens_spec(width, block)
    pair = pl.BlockSpec((2, width, block), lambda t, w: (0, 0, t))
    row = jax.ShapeDtypeStruct((width, length), LOW)
    return kernel_call(
        output_kernel,
        "output",
        pltpu.PrefetchScalarGridSpec(
            num_scalar_prefetch=1,
            grid=(steps,),
            in_specs=[pair] * 4
            + [pl.BlockSpec((2, width, width), lambda t, w: (0, 0, 0), pipeline_mode=pl.Buffered(1))] * 2
            + [pl.BlockSpec(down_weight.shape, lambda t, w: (0, 0), pipeline_mode=pl.Buffered(1))]
            + [spec, row_spec(width, block)]
            + [pl.BlockSpec((1, 1, block), lambda t, w: (w[0], 0, t))]
            + [pl.BlockSpec(memory_space=pltpu.HBM)] * len(after),
            out_specs=[spec] * 4 + [whole((8, 128))],
        ),
        [row] * 4 + [jax.ShapeDtypeStruct((8, 128), FULL)],
        20e9,
        24 * length * width,
        vmem=40,
    )(where, *acts, *grads, *ups, down_weight, middle, cot, segments, *after)


def mixed_grad_kernel(where_ref, gab_ref, w_ref, *refs):
    mixed_refs, gm_refs, (delta_ref, keep_ref, send_ref, mixed_all) = refs[:GROUPS], refs[-GROUPS - 4 : -4], refs[-4:]
    gab = gab_ref[...]
    part = gm_refs[0].shape[0]
    heads = part // HEAD_DIM
    for group in range(GROUPS):
        rows = slice(group * part, (group + 1) * part)
        grads = dot(w_ref[rows, :], gab).astype(LOW)
        gm_refs[group][...] = grads
        mixed = mixed_refs[group][...]
        mixed_all[rows, :] = mixed
        product = grads.astype(FULL) * mixed.astype(FULL)
        for head in range(heads):
            delta_ref[group, head : head + 1, :] = jnp.sum(
                product[head * HEAD_DIM : (head + 1) * HEAD_DIM], axis=0, keepdims=True
            )
    for place, rows in halves(where_ref, mixed_all.shape[0]):
        (keep_ref, send_ref)[place][...] = dot(mixed_all[rows, :], gab, 1, 1).astype(LOW)


def mixed_grad(where, gab, w, mixed, after=()):
    width, length = gab.shape
    part = width // GROUPS
    heads = part // HEAD_DIM
    outs = kernel_call(
        mixed_grad_kernel,
        "mixed_grad",
        pltpu.PrefetchScalarGridSpec(
            num_scalar_prefetch=1,
            grid=(1,),
            in_specs=[whole((width, length)), whole((width, width))]
            + [whole((part, length))] * GROUPS
            + [pl.BlockSpec(memory_space=pltpu.HBM)] * len(after),
            out_specs=[whole((part, length))] * GROUPS
            + [whole((GROUPS, heads, length))]
            + [whole((width // 2, width))] * 2,
            scratch_shapes=[pltpu.VMEM((width, length), LOW)],
        ),
        [jax.ShapeDtypeStruct((part, length), LOW)] * GROUPS
        + [jax.ShapeDtypeStruct((GROUPS, heads, length), FULL)]
        + [jax.ShapeDtypeStruct((width // 2, width), LOW)] * 2,
        4 * length * width * width,
        8 * length * width,
        vmem=28,
    )(where, gab, w, *mixed, *after)
    return outs[:GROUPS], outs[GROUPS], outs[GROUPS + 1], outs[GROUPS + 2]


def input_grad_kernel(where_ref, x_ref, gmid_ref, *refs):
    grad_refs, w_refs, (keep_ref, *send_refs) = refs[:GROUPS], refs[GROUPS : 2 * GROUPS], refs[-3:]
    on_attention = where_ref[0] == 0
    grad_normed = dot(w_refs[0][...], grad_refs[0][...])
    for group in range(1, GROUPS):
        grad_normed = grad_normed + dot(w_refs[group][...], grad_refs[group][...])
    normed, inverse = crms(widened(x_ref[0]))
    middle = gmid_ref[...]
    grad = (middle.astype(FULL) + widened_back(crms_back(normed, inverse, grad_normed))).astype(LOW)
    keep_ref[...] = jnp.where(on_attention, grad, middle)
    sent = jnp.where(on_attention, middle, grad)
    for part, send_ref in enumerate(send_refs):

        @pl.when((pl.program_id(0) > 0) == (part == 1))
        def _(send_ref=send_ref):
            send_ref[...] = sent


def input_grad(where, x, grad_middle, grads, weights, after=()):
    width, length = grad_middle.shape
    spec = tokens_spec(width, length // 4)
    return kernel_call(
        input_grad_kernel,
        "input_grad",
        pltpu.PrefetchScalarGridSpec(
            num_scalar_prefetch=1,
            grid=(4,),
            in_specs=[row_spec(width, length // 4), spec]
            + [spec] * GROUPS
            + [whole((width, width))] * GROUPS
            + [pl.BlockSpec(memory_space=pltpu.HBM)] * len(after),
            out_specs=[
                spec,
                pl.BlockSpec((width, length // 4), lambda t, w: (0, 0)),
                pl.BlockSpec((width, length // 4), lambda t, w: (0, jnp.maximum(t - 1, 0))),
            ],
        ),
        [jax.ShapeDtypeStruct((width, tokens), LOW) for tokens in (length, length // 4, length - length // 4)],
        6 * length * width * width,
        12 * length * width,
        vmem=30,
    )(where, x, grad_middle, *grads, *weights, *after)


def rows_kernel(where_ref, kept_ref, *refs):
    other_refs, out_ref = refs[:-1], refs[-1]
    kept = kept_ref[...].astype(FULL)
    other = other_refs[0][...].astype(FULL)
    if len(other_refs) > 1:
        other = jnp.where(pl.program_id(0) == 0, other, other_refs[1][...].astype(FULL))
    mine = where_ref[0] == 0
    out_ref[...] = jnp.stack([jnp.where(mine, kept, other), jnp.where(mine, other, kept)], axis=1).astype(LOW)


def rows_of(where, kept, others, after=()):
    width, length = kept.shape
    block = length // 4
    places = [lambda t, w: (0, t)] if len(others) == 1 else [lambda t, w: (0, 0), lambda t, w: (0, jnp.maximum(t - 1, 0))]

    def body(where_ref, *refs):
        rows_kernel(where_ref, *refs[: 1 + len(others)], refs[-1])

    out = kernel_call(
        body,
        "rows",
        pltpu.PrefetchScalarGridSpec(
            num_scalar_prefetch=1,
            grid=(4,),
            in_specs=[tokens_spec(width, block)]
            + [pl.BlockSpec((width, block), place) for place in places]
            + [pl.BlockSpec(memory_space=pltpu.HBM)] * len(after),
            out_specs=pl.BlockSpec((width, 2, block), lambda t, w: (0, 0, t)),
        ),
        pltpu.HBM((width - 1, 2, length), LOW),
        2e10,
        length,
        vmem=40,
    )(where, kept, *others, *after)
    return jnp.transpose(out, (1, 2, 0))[None]


def partner(block, distance):
    size = lax.axis_size("dp")
    return lax.ppermute(block, "dp", [(i, i ^ distance) for i in range(size)])


def across(block):
    return lax.ppermute(block, "section", [(0, 1), (1, 0)])


def split(left, right, distance):
    bit = (lax.axis_index("dp") & distance) // distance
    half = left.shape[1] // 2
    part = lambda a, at: lax.dynamic_slice_in_dim(a, at * half, half, 1)
    return add_low(part(left, bit), part(right, bit)), add_low(part(left, 1 - bit), part(right, 1 - bit))


def add_low(left, right):
    return (left.astype(FULL) + right.astype(FULL)).astype(LOW)


class Scatter:
    def __init__(self, keep, got, order):
        self.order = order
        self.keep, self.got = keep, got
        self.at = 0

    def step(self, *others):
        self.at += 1
        self.got = later(self.got, *others)
        self.keep, self.sent = split(self.keep, self.got, self.order[self.at])
        self.got = partner(self.sent, self.order[self.at])

    def total(self, *others):
        while self.at < len(self.order) - 1:
            self.step(*others)
        return add_low(self.keep, later(self.got, *others))


class Gather:
    def __init__(self, shard, order, *others):
        self.left = list(reversed(order))
        self.held = later(shard, *others)[None] if others else shard[None]
        self.got = partner(self.held, self.left.pop(0))

    def step(self, *others):
        self.held = jnp.concatenate([self.held, later(self.got, *others)], axis=0)
        self.got = partner(self.held, self.left.pop(0))

    def all(self, *others):
        while self.left:
            self.step(*others)
        return self.held, self.got


def number_of(order):
    me = lax.axis_index("dp").astype(jnp.int32)
    number = jnp.int32(0)
    for distance in order:
        number = number * 2 + (me // distance) % 2
    return number


def later(value, *others):
    return lax.optimization_barrier((value, *others))[0]


def gathered_specs(array, per_step):
    half_steps = array.shape[0] // per_step
    block = (per_step, *array.shape[1:])
    return [
        pl.BlockSpec(block, lambda e, w: (jnp.minimum(e, half_steps - 1), 0, 0)),
        pl.BlockSpec(block, lambda e, w: (jnp.maximum(e - half_steps, 0), 0, 0)),
    ]


def each_entry(number_ref, halves_refs, do):
    steps = pl.num_programs(0)
    per_step = halves_refs[0].shape[0]
    for place, ref in enumerate(halves_refs):

        @pl.when((pl.program_id(0) * 2 >= steps) == (place == 1))
        def _(ref=ref):
            for entry in range(per_step):
                do((number_ref[1] % per_step) ^ entry, ref, entry)


def down_sum_kernel(number_ref, near_ref, far_ref, out_ref):
    rows = out_ref.shape[2]

    def write(place, ref, entry):
        for block in range(2):
            out_ref[block, place] = ref[entry, block * rows : (block + 1) * rows, :].astype(FULL)

    each_entry(number_ref, (near_ref, far_ref), write)


def down_sum(number, near, far, width):
    entries = 2 * near.shape[0]
    rows = width // entries
    per_step = entries // 4
    out = kernel_call(
        down_sum_kernel,
        "down_sum",
        pltpu.PrefetchScalarGridSpec(
            num_scalar_prefetch=1,
            grid=(4,),
            in_specs=gathered_specs(near, per_step),
            out_specs=pl.BlockSpec((2, per_step, rows, width), lambda e, w: (0, (w[1] // per_step) ^ e, 0, 0)),
        ),
        jax.ShapeDtypeStruct((2, entries, rows, width), FULL),
        2e10,
        width,
        vmem=58,
    )(number, near, far)
    return out.reshape(2 * width, width)


def columns_of(numbers):
    if numbers[0] < 0:
        return [[(0, 3 * block, 3)] for block in (-numbers[0] - 1, -numbers[1] - 1)]
    return [
        [(0, 9, 3)] if block == 0 else [(piece, own_column_static(block - 1, piece, 0), 1) for piece in range(3)]
        for block in numbers
    ]


def counts_of(section, slots, width, near_ref, far_ref):
    rows = sum(ref[entry, :16, :128].astype(FULL) for ref in (near_ref, far_ref) for entry in range(ref.shape[0]))
    lane = lax.broadcasted_iota(jnp.int32, (1, 128), 1)
    total = [
        jnp.sum(jnp.where((lane % 3 == which) & (lane < 9), rows[:1], 0.0), axis=1, keepdims=True) for which in range(3)
    ]
    square = jnp.where(section == 0, total[0], total[1])
    count = jnp.where(section == 0, total[2], slots - total[2])
    root = jnp.sqrt(square / (total[2] * width))
    return jnp.broadcast_to(jnp.where(lane == 0, root, jnp.where(lane == 1, count, 0.0)), (8, 128))


def first_sum_kernel(skip, blocks, slots, number_ref, near_ref, far_ref, *refs):
    buffer, sem = refs[-2:]
    out_ref = refs[-4] if slots else refs[-3]
    entries, rows, columns = out_ref.shape
    width = columns // 4
    part = width // 3
    half = entries // 2
    if slots:
        refs[-3][...] = counts_of(number_ref[0], slots, width, near_ref, far_ref)
    for section in range(2):

        @pl.when(number_ref[0] == section)
        def _(section=section):
            pieces = columns_of(blocks[section])

            def copies(place, do):
                first = pl.multiple_of(jnp.where(number_ref[1] < half, place, 1 - place) * half, half)
                for at in range(2):
                    for order, (start, column, size) in enumerate(pieces[at]):
                        do(
                            pltpu.make_async_copy(
                                buffer.at[at, pl.ds(first, half), :, pl.ds(start * part, size * part)],
                                out_ref.at[pl.ds(first, half), :, pl.ds(column * part, size * part)],
                                sem.at[place, at, order],
                            )
                        )

            for place, ref in enumerate((near_ref, far_ref)):
                for entry in range(half):
                    for at in range(2):
                        values = ref[entry, skip + at * rows : skip + (at + 1) * rows, :]
                        buffer[at, number_ref[1] ^ (entry + place * half)] = values.astype(FULL)
                copies(place, lambda c: c.start())
            for place in range(2):
                copies(place, lambda c: c.wait())


def first_sum(number, skip, blocks, gathered, width, before=None, slots=None):
    near, far = gathered
    entries = 2 * near.shape[0]
    rows = width // entries
    held = [] if before is None else [before]
    anywhere = pl.BlockSpec(memory_space=pl.ANY)
    return pl.pallas_call(
        functools.partial(first_sum_kernel, skip, blocks, slots),
        grid_spec=pltpu.PrefetchScalarGridSpec(
            num_scalar_prefetch=1,
            grid=(1,),
            in_specs=[whole(near.shape), whole(far.shape)] + [anywhere] * len(held),
            out_specs=[anywhere] + [whole((8, 128))] * bool(slots),
            scratch_shapes=[pltpu.VMEM((2, entries, rows, width), FULL), pltpu.SemaphoreType.DMA((2, 2, 3))],
        ),
        out_shape=[jax.ShapeDtypeStruct((entries, rows, 4 * width), FULL)]
        + [jax.ShapeDtypeStruct((8, 128), FULL)] * bool(slots),
        input_output_aliases={3: 0} if held else {},
        compiler_params=pltpu.CompilerParams(vmem_limit_bytes=24 * 2**20),
        cost_estimate=pl.CostEstimate(flops=1000, bytes_accessed=1000, transcendentals=0),
        name="first_sum",
    )(number, near, far, *held)


def on_device(stream_in, cotangent, weights_first, down_weight, segments):
    rows_dev, length, compact_width = stream_in.shape
    width = compact_width + 1
    section = lax.axis_index("section").astype(jnp.int32)
    index = lax.axis_index("dp").astype(jnp.int32)
    size = lax.axis_size("dp")
    on_attention = section == 0
    where = jnp.stack([section, index & 3, index & 1])
    segments3 = segments.reshape(rows_dev, 1, length)
    order = [1 << i for i in range(size.bit_length() - 1)]
    flat = lambda a: a.reshape(-1, width)

    near = [across(piece) for piece in weight_piece(where, weights_first)]
    x, cot = jnp.transpose(stream_in, (0, 2, 1)), jnp.transpose(cotangent, (0, 2, 1))
    nt, g = prep(where, x, cot)
    ga = branch_grad(g, down_weight, after=(near[0],))
    attended, received, besides = [], [], [partner(later(near[0], nt), 2), partner(later(near[1], ga), 2)]
    for group in range(4):
        quarter, beside = near[group], besides[group]
        done = [attended[group - 1][1] if group else ga]
        received.append((quarter, beside, partner(quarter, 1), partner(later(beside, *done), 1)))
        if group < 2:
            besides.append(partner(later(near[group + 2], *done), 2))
        if group < GROUPS:
            attended.append(attend(group, where, weights_first, received[group], nt, segments3))
    mixed = [a[1] for a in attended]
    middle, nm, sums_mid, out_weights = middle_of(where, weights_first, received[GROUPS], mixed, x, segments3)

    act_a, grad_a, weights_a, keep_up, send_up, *down_a = hidden_of(0, where, weights_first, received[0::2], nm, ga, g)
    up_a = Scatter(keep_up, partner(send_up, 1), order)
    got_a = partner(down_a[1], 1)
    up_a.step()
    act_b, grad_b, weights_b, keep_up, send_up, *down_b = hidden_of(
        1, where, weights_first, received[1::2], nm, ga, g, after=(up_a.sent,)
    )
    up_a.step(act_b)
    up_b = Scatter(keep_up, partner(later(send_up, up_a.sent), 1), order)
    got_b = partner(later(down_b[1], up_a.sent), 1)
    up_b.step()
    kept, sent = [], []
    for keep, got in ((down_a[0], got_a), (down_b[0], got_b)):
        lower, upper = add_low(keep[0], got[0]), add_low(keep[1], got[1])
        kept.append(jnp.where(on_attention, lower, upper))
        sent.append(jnp.where(on_attention, upper, lower))
    kept, sent = jnp.stack(kept), later(jnp.stack(sent), up_b.sent)
    down = Scatter(kept, across(sent), order)
    keep_out, send_out, grad_mid, gab, sums_out = output_of(
        where, (act_a, act_b), (grad_a, grad_b), (weights_a, weights_b), down_weight, middle, cot, segments3, after=(sent,)
    )
    up_a.step(gab)
    up_b.step(up_a.sent)
    down.step(up_b.sent)
    gm, delta, keep_w, send_w = mixed_grad(where, gab, out_weights, mixed, after=(down.sent,))
    keeps, sends, grads = [keep_w], [send_w], []

    def backward(group, *after):
        qkv, _, total, _ = attended[group]
        keep_w, send_w, grad = attend_back(where, qkv, gm[group], total, delta[group], segments3, nt, after=after)
        keeps.append(keep_w)
        sends.append(send_w)
        grads.append(grad)

    up_a = up_a.total(delta)
    backward(0, up_a)
    up_b.step(grads[0])
    down.step(up_b.sent)
    sent_a = later(jnp.stack(sends), down.sent)
    attn_a = Scatter(jnp.stack(keeps), partner(sent_a, 1), order)
    backward(1, sent_a)
    attn_a.step(grads[1])
    down.step(attn_a.sent)
    up_b = up_b.total(grads[1])
    rows = up_a.shape[1]
    received_out = across(send_out)
    backward(2, down.sent, up_b)
    down = down.total(grads[2])
    sum_dn = Gather(flat(down), order)
    attn_a.step(sum_dn.held)
    attn_b = Scatter(jnp.stack(keeps[2:]), partner(later(jnp.stack(sends[2:]), attn_a.sent), 1), order)
    attn_b.step()
    keep_grad, *send_grad = input_grad(
        where, x, grad_mid, grads, [a[3] for a in attended], after=(attn_b.sent, received_out)
    )
    attn_a.step(keep_grad)
    attn_b.step(attn_a.sent)
    sum_dn.step(attn_b.sent)
    attn_a = attn_a.total(sum_dn.held)

    scalars = (sums_mid + sums_out)[0, :3]

    def scalar_rows(values):
        high = values.astype(LOW)
        rest = values - high.astype(FULL)
        middle_part = rest.astype(LOW)
        low = (rest - middle_part.astype(FULL)).astype(LOW)
        packed = jnp.concatenate([high, middle_part, low])
        return jnp.zeros((16, width), LOW).at[0, :9].set(packed)

    def scalars_of(block):
        parts = block[..., 0, :9].astype(FULL)
        return parts[..., :3] + parts[..., 3:6] + parts[..., 6:9]

    mine_a, theirs_a = jnp.where(on_attention, attn_a, up_a), jnp.where(on_attention, up_a, attn_a)
    sent_a = jnp.concatenate([scalar_rows(scalars), flat(theirs_a)])
    swapped = across(sent_a)
    attn_b.step(sent_a)
    swapped = later(swapped, attn_b.sent)
    pair = scalars + scalars_of(swapped[:16])
    shard_a = add_low(flat(mine_a), swapped[16:])
    sum_a = Gather(jnp.concatenate([scalar_rows(pair), shard_a]), order)
    received_grad = [across(later(send_grad[0], sum_a.held))]
    sum_dn.step(sum_a.held)
    received_grad[0] = later(received_grad[0], sum_dn.held)
    attn_b = attn_b.total(received_grad[0])
    mine_b, theirs_b = jnp.where(on_attention, attn_b, up_b), jnp.where(on_attention, up_b, attn_b)
    swapped_b = across(flat(theirs_b))
    received_grad.append(across(later(send_grad[1], theirs_b)))
    sum_a.step(theirs_b)
    stream_out = rows_of(where, keep_out, [received_out], after=(sum_a.held,))
    sum_b = Gather(add_low(flat(mine_b), later(swapped_b, stream_out)), order)
    sum_a.step(sum_b.held)
    sum_dn.step(sum_a.held)
    number = jnp.stack([section, number_of(order)])
    grad_down = down_sum(later(number, sum_dn.held), *sum_dn.all(), width)
    sum_b.step(grad_down)
    sum_b.step(sum_a.got)
    stream_grad = rows_of(where, keep_grad, received_grad, after=(sum_b.held,))
    sum_a.step(stream_grad)
    sum_b.step(sum_a.held)
    sum_a, sum_b = sum_a.all(), sum_b.all()
    slots = float(rows_dev * length * size)
    grad_first, counts = first_sum(later(number, sum_b[0]), 16, ((0, 1), (-1, -3)), sum_a, width, slots=slots)
    (grad_first,) = first_sum(number, 0, ((2, 3), (-2, -4)), sum_b, width, before=grad_first)
    grad_first = grad_first.reshape(width, 4 * width)
    residual_rms, token_count = counts[0, :1], counts[0, 1:2].astype(jnp.int32)
    return (
        stream_out,
        stream_grad,
        grad_first[None],
        grad_down,
        residual_rms,
        token_count,
    )


def solution(mesh):
    placed = (
        P("dp", None, None),
        P("dp", None, None),
        P("section", None, None),
        P(),
        P("dp", None),
    )
    return jax.shard_map(
        on_device,
        mesh=mesh,
        in_specs=placed,
        out_specs=(
            P("section", "dp", None, None),
            P("section", "dp", None, None),
            P("section", None, None),
            P("section", None),
            P("section"),
            P("section"),
        ),
        check_vma=False,
    )
```

```python
import functools

import jax
import jax.numpy as jnp
from jax import lax
from jax.experimental import pallas as pl
from jax.experimental.pallas import tpu as pltpu
from jax.sharding import PartitionSpec as P

HEADS = 12
HEAD_DIM = 64
GROUPS = 3
EPSILON = 1e-06
MASKED = -1e30
SCALE = HEAD_DIM ** (-0.5)
LOG2E = 1.4426950408889634
LOW = jnp.bfloat16
FULL = jnp.float32


def dot(left, right, left_dim=1, right_dim=0):
    return lax.dot_general(
        left, right, (((left_dim,), (right_dim,)), ((), ())), preferred_element_type=FULL
    )


def kernel_call(body, name, grid_spec, out_shape, flops, moved, vmem=32):
    return pl.pallas_call(
        body,
        grid_spec=grid_spec,
        out_shape=out_shape,
        compiler_params=pltpu.CompilerParams(vmem_limit_bytes=vmem * 2**20),
        cost_estimate=pl.CostEstimate(flops=int(flops * 3), bytes_accessed=int(moved * 3), transcendentals=0),
        name=name,
    )


def last_row(block):
    return lax.broadcasted_iota(jnp.int32, block.shape, 0) == block.shape[0] - 1


def widened(block):
    values = jnp.where(last_row(block), 0.0, block.astype(FULL))
    return jnp.where(last_row(block), -jnp.sum(values, axis=0, keepdims=True), values)


def crms(values):
    inverse = lax.rsqrt(jnp.mean(values * values, axis=0, keepdims=True) + EPSILON)
    return values * inverse, inverse


def crms_back(normed, inverse, grad):
    return inverse * (grad - normed * jnp.mean(grad * normed, axis=0, keepdims=True))


def compressed(branch):
    return branch - jnp.mean(branch, axis=0, keepdims=True)


def widened_back(grad):
    return grad - grad[grad.shape[0] - 1 :]


def compressed_back(block):
    values = jnp.where(last_row(block), 0.0, block.astype(FULL))
    return values - jnp.mean(values, axis=0, keepdims=True)


def square_sum(rounded, valid):
    wide = widened(rounded)
    per_token = jnp.sum(wide * wide, axis=0, keepdims=True)
    return jnp.sum(jnp.where(valid, per_token, 0.0), axis=1, keepdims=True)


def prep_kernel(where_ref, x_ref, cot_ref, nt_ref, g_ref):
    normed, _ = crms(widened(x_ref[0]))
    nt_ref[...] = normed.astype(LOW)
    g_ref[...] = compressed_back(cot_ref[0]).astype(LOW)


def tokens_spec(width, block):
    return pl.BlockSpec((width, block), lambda t, *_: (0, t))


def row_spec(width, block):
    return pl.BlockSpec((1, width, block), lambda t, w: (w[0], 0, t))


def prep(where, x, cot):
    width, length = x.shape[1] + 1, x.shape[2]
    spec = tokens_spec(width, length // 4)
    return kernel_call(
        prep_kernel,
        "prep",
        pltpu.PrefetchScalarGridSpec(
            num_scalar_prefetch=1, grid=(4,), in_specs=[row_spec(width, length // 4)] * 2, out_specs=[spec] * 2
        ),
        [jax.ShapeDtypeStruct((width, length), LOW)] * 2,
        0,
        8 * length * width,
        vmem=16,
    )(where, x, cot)


def branch_grad_kernel(g_ref, w_ref, *refs):
    out_ref = refs[-1]
    out_ref[0] = dot(w_ref[...], g_ref[...]).astype(LOW)


def branch_grad(g, down_weight, after=()):
    width, length = g.shape
    blocks = down_weight.shape[0] // width
    return kernel_call(
        branch_grad_kernel,
        "branch_grad",
        pltpu.PrefetchScalarGridSpec(
            num_scalar_prefetch=0,
            grid=(blocks,),
            in_specs=[
                pl.BlockSpec((width, length), lambda b: (0, 0)),
                pl.BlockSpec((width, width), lambda b: (b, 0)),
            ]
            + [pl.BlockSpec(memory_space=pltpu.HBM)] * len(after),
            out_specs=pl.BlockSpec((1, width, length), lambda b: (b, 0, 0)),
        ),
        pltpu.HBM((blocks, width, length), LOW),
        2 * length * width * width * blocks,
        2 * length * width * (blocks + 1),
        vmem=20,
    )(g, down_weight, *after)


def own_column_static(group, piece, section):
    if section == 1 or group == GROUPS:
        return 3 * group + piece
    return group + GROUPS * piece


def piece_kernel(where_ref, w_ref, *out_refs):
    part = out_refs[0].shape[1] // 3
    for section in range(2):

        @pl.when(where_ref[0] == section)
        def _(section=section):
            for group in range(4):
                for piece in range(3):
                    column = own_column_static(group, piece, section) * part
                    out_refs[group][:, piece * part : (piece + 1) * part] = w_ref[0, :, column : column + part]


def weight_piece(where, weights):
    rows, columns = weights.shape[1:]
    shape = (rows // 4, columns // 4)
    return kernel_call(
        piece_kernel,
        "weight_piece",
        pltpu.PrefetchScalarGridSpec(
            num_scalar_prefetch=1,
            grid=(1,),
            in_specs=[pl.BlockSpec((1, rows // 4, columns), lambda i, w: (0, w[1], 0))],
            out_specs=[whole(shape)] * 4,
        ),
        [jax.ShapeDtypeStruct(shape, LOW)] * 4,
        0,
        rows * columns,
        vmem=58,
    )(where, weights)


def weight_copies(group, wanted, where_ref, own_ref, quarters, target, sem, act):
    quarter = target.shape[0] // 4
    part = target.shape[1] // 3

    @pl.when(where_ref[0] == wanted)
    def _():
        for piece in range(3):
            column = own_column_static(group, piece, wanted) * part
            act(pltpu.make_async_copy(own_ref.at[0, :, pl.ds(column, part)], target.at[:, pl.ds(piece * part, part)], sem.at[piece]))

    @pl.when(where_ref[0] != wanted)
    def _():
        for place, source in enumerate(quarters):
            index = where_ref[1] ^ (0, 2, 1, 3)[place]
            act(pltpu.make_async_copy(source, target.at[pl.ds(index * quarter, quarter), :], sem.at[place]))


def segment_rows(segment):
    tokens = segment.shape[1]
    ids = lax.broadcasted_iota(jnp.int32, (16, tokens), 0)
    same = segment == ids
    real = ids < 5
    queries = jnp.where(real & jnp.logical_not(same), MASKED, 0.0).astype(LOW)
    keys = jnp.where(real & same, 1.0, 0.0).astype(LOW)
    return queries, keys


def two_parts(values):
    high = values.astype(LOW)
    return high, (values - high.astype(FULL)).astype(LOW)


def minus_rows(values):
    high = values.astype(LOW)
    rest = values - high.astype(FULL)
    middle = rest.astype(LOW)
    low = rest - middle.astype(FULL)
    row = lax.broadcasted_iota(jnp.int32, (16, values.shape[1]), 0)
    parts = jnp.where(
        row == 0, high.astype(FULL), jnp.where(row == 1, middle.astype(FULL), jnp.where(row == 2, low, 0.0))
    )
    return (-parts).astype(LOW)


def three_ones(tokens):
    return jnp.where(lax.broadcasted_iota(jnp.int32, (16, tokens), 0) < 3, 1.0, 0.0).astype(LOW)


def head_tasks(heads, blocks, block):
    return [
        (head, slice(i * block, (i + 1) * block), slice(0, (i + 1) * block), i * block)
        for head in range(heads)
        for i in range(blocks)
    ]


def in_stages(tasks, stages):
    for step in range(len(tasks) + len(stages) - 1):
        for late, stage in enumerate(stages):
            if 0 <= step - late < len(tasks):
                stage(tasks[step - late])


def attend_kernel(group, where_ref, own_ref, near_ref, beside_ref, core_ref, across_ref, nt_ref, seg_ref, qkv_ref, mixed_ref, total_ref, w_ref, sem):
    copies = functools.partial(
        weight_copies, group, 0, where_ref, own_ref, (near_ref, beside_ref, core_ref, across_ref), w_ref, sem
    )
    copies(lambda c: c.start())
    copies(lambda c: c.wait())
    length = nt_ref.shape[1]
    width = qkv_ref.shape[0] // 3
    heads, blocks = width // HEAD_DIM, 4
    block = length // blocks
    for part in range(3):
        qkv_ref[part * width : (part + 1) * width, :] = dot(
            w_ref[:, part * width : (part + 1) * width], nt_ref[...], 0, 0
        ).astype(LOW)
    seg_queries, seg_keys = segment_rows(seg_ref[0])
    causal = lax.broadcasted_iota(jnp.int32, (block, block), 0) <= lax.broadcasted_iota(jnp.int32, (block, block), 1)
    ones = three_ones(length)
    scored, weighed = {}, {}

    def score(task):
        head, queries, keys, _ = task
        high, low = two_parts(qkv_ref[head * HEAD_DIM : (head + 1) * HEAD_DIM, queries].astype(FULL) * (SCALE * LOG2E))
        key_rows = qkv_ref[width + head * HEAD_DIM : width + (head + 1) * HEAD_DIM, keys]
        scored[task] = dot(
            jnp.concatenate([key_rows, key_rows, seg_keys[:, keys]], axis=0),
            jnp.concatenate([high, low, seg_queries[:, queries]], axis=0),
            0,
            0,
        )

    def weigh(task):
        before = task[3]
        scores = scored.pop(task)
        last = jnp.where(causal, scores[before:], MASKED)
        highest = jnp.max(last, axis=0, keepdims=True)
        if before:
            highest = jnp.maximum(highest, jnp.max(scores[:before], axis=0, keepdims=True))
        exponents = jnp.exp2(last - highest).astype(LOW)
        if before:
            exponents = jnp.concatenate([jnp.exp2(scores[:before] - highest).astype(LOW), exponents], axis=0)
        weighed[task] = (exponents, highest)

    def mix(task):
        head, queries, keys, _ = task
        exponents, highest = weighed.pop(task)
        values = qkv_ref[2 * width + head * HEAD_DIM : 2 * width + (head + 1) * HEAD_DIM, keys]
        mixed = dot(jnp.concatenate([values, ones[:, keys]], axis=0), exponents)
        total = mixed[HEAD_DIM : HEAD_DIM + 1]
        mixed_ref[head * HEAD_DIM : (head + 1) * HEAD_DIM, queries] = (mixed[:HEAD_DIM] / total).astype(LOW)
        total_ref[head : head + 1, queries] = highest + jnp.log2(total)

    in_stages(head_tasks(heads, blocks, block), (score, weigh, mix))


def attend(group, where, own, received, nt, segments):
    width, length = nt.shape
    part = width // GROUPS
    anywhere = pl.BlockSpec(memory_space=pltpu.HBM)
    return kernel_call(
        functools.partial(attend_kernel, group),
        "attend",
        pltpu.PrefetchScalarGridSpec(
            num_scalar_prefetch=1,
            grid=(1,),
            in_specs=[anywhere] * 5
            + [
                pl.BlockSpec((width, length), lambda i, w: (0, 0)),
                pl.BlockSpec((1, 1, length), lambda i, w: (w[0], 0, 0)),
            ],
            out_specs=[
                pl.BlockSpec((3 * part, length), lambda i, w: (0, 0)),
                pl.BlockSpec((part, length), lambda i, w: (0, 0)),
                pl.BlockSpec((part // HEAD_DIM, length), lambda i, w: (0, 0)),
                pl.BlockSpec((width, 3 * part), lambda i, w: (0, 0)),
            ],
            scratch_shapes=[pltpu.SemaphoreType.DMA((4,))],
        ),
        [
            pltpu.HBM((3 * part, length), LOW),
            jax.ShapeDtypeStruct((part, length), LOW),
            pltpu.HBM((part // HEAD_DIM, length), FULL),
            pltpu.HBM((width, 3 * part), LOW),
        ],
        4.5e9,
        8 * width * length,
        vmem=24,
    )(where, own, *received, nt, segments)


def attend_back_kernel(where_ref, qkv_ref, gm_ref, total_ref, delta_ref, seg_ref, nt_ref, *rest):
    keep_ref, send_ref, grads_ref, acc = rest[-4:]
    length = nt_ref.shape[1]
    width = gm_ref.shape[0]
    heads, blocks = width // HEAD_DIM, 4
    block = length // blocks
    seg_queries, seg_keys = segment_rows(seg_ref[0])
    ones = three_ones(length)
    causal = lax.broadcasted_iota(jnp.int32, (block, block), 1) <= lax.broadcasted_iota(jnp.int32, (block, block), 0)
    acc[...] = jnp.zeros_like(acc)
    scored, weighed = {}, {}

    def rows(part, head):
        return slice(part * width + head * HEAD_DIM, part * width + (head + 1) * HEAD_DIM)

    def score(task):
        head, queries, keys, _ = task
        high, low = two_parts(qkv_ref[rows(0, head), queries].astype(FULL) * (SCALE * LOG2E))
        key_rows = qkv_ref[rows(1, head), keys]
        scores = dot(
            jnp.concatenate([high, low, seg_queries[:, queries], minus_rows(total_ref[head : head + 1, queries])], axis=0),
            jnp.concatenate([key_rows, key_rows, seg_keys[:, keys], ones[:, keys]], axis=0),
            0,
            0,
        )
        grads = dot(
            jnp.concatenate([gm_ref[rows(0, head), queries], minus_rows(delta_ref[head : head + 1, queries])], axis=0),
            jnp.concatenate([qkv_ref[rows(2, head), keys], ones[:, keys]], axis=0),
            0,
            0,
        )
        scored[task] = (scores, grads)

    def weigh(task):
        before = task[3]
        scores, grads = scored.pop(task)
        last = jnp.where(causal, scores[:, before:], MASKED)
        if before:
            last = jnp.concatenate([scores[:, :before], last], axis=1)
        probs = jnp.exp2(last)
        weighed[task] = (probs.astype(LOW), (probs * grads).astype(LOW))

    def collect(task):
        head, queries, keys, _ = task
        probs, grads = weighed.pop(task)
        acc[rows(2, head), keys] += dot(gm_ref[rows(0, head), queries], probs)
        acc[rows(1, head), keys] += dot(qkv_ref[rows(0, head), queries] * LOW(SCALE), grads)
        acc[rows(0, head), queries] = dot(qkv_ref[rows(1, head), keys], grads, 1, 1) * SCALE

    in_stages(head_tasks(heads, blocks, block), (score, weigh, collect))
    grads_ref[...] = acc[...].astype(LOW)
    for place, rows_ in halves(where_ref, nt_ref.shape[0]):
        (keep_ref, send_ref)[place][...] = dot(nt_ref[rows_, :], grads_ref[...], 1, 1).astype(LOW)


def halves(where_ref, count):
    half = count // 2
    return [
        (0, pl.ds(pl.multiple_of(where_ref[2] * half, half), half)),
        (1, pl.ds(pl.multiple_of((1 - where_ref[2]) * half, half), half)),
    ]


def whole(shape):
    return pl.BlockSpec(shape, lambda *_: (0,) * len(shape))


def attend_back(where, qkv, gm, total, delta, segments, nt, after=()):
    width, length = nt.shape
    part = gm.shape[0]
    arrays = [qkv, gm, total, delta]
    return kernel_call(
        attend_back_kernel,
        "attend_back",
        pltpu.PrefetchScalarGridSpec(
            num_scalar_prefetch=1,
            grid=(1,),
            in_specs=[whole(a.shape) for a in arrays]
            + [pl.BlockSpec((1, 1, length), lambda i, w: (w[0], 0, 0)), whole(nt.shape)]
            + [pl.BlockSpec(memory_space=pltpu.HBM)] * len(after),
            out_specs=[whole((width // 2, 3 * part))] * 2 + [whole((3 * part, length))],
            scratch_shapes=[pltpu.VMEM((3 * part, length), FULL)],
        ),
        [jax.ShapeDtypeStruct((width // 2, 3 * part), LOW)] * 2 + [pltpu.HBM((3 * part, length), LOW)],
        9e9,
        8 * width * length,
        vmem=28,
    )(where, *arrays, segments, nt, *after)


def middle_kernel(where_ref, own_ref, near_ref, beside_ref, core_ref, across_ref, *refs):
    mixed_refs, (x_ref, seg_ref, mid_ref, nm_ref, sums_ref, w_ref, sem) = refs[:GROUPS], refs[GROUPS:]
    step = pl.program_id(0)

    @pl.when(step == 0)
    def _():
        copies = functools.partial(
            weight_copies, GROUPS, 0, where_ref, own_ref, (near_ref, beside_ref, core_ref, across_ref), w_ref, sem
        )
        copies(lambda c: c.start())
        copies(lambda c: c.wait())
        sums_ref[...] = jnp.zeros_like(sums_ref)

    mixed = jnp.concatenate([ref[...] for ref in mixed_refs], axis=0)
    branch = dot(w_ref[...], mixed, 0, 0)
    middle = (x_ref[0].astype(FULL) + compressed(branch)).astype(LOW)
    mid_ref[...] = middle
    normed, _ = crms(widened(middle))
    nm_ref[...] = normed.astype(LOW)
    valid = seg_ref[0] > 0
    lane = lax.broadcasted_iota(jnp.int32, sums_ref.shape, 1)
    count = jnp.sum(valid.astype(FULL), axis=1, keepdims=True)
    sums_ref[...] += jnp.where(lane == 0, square_sum(middle, valid), 0.0) + jnp.where(lane == 2, count, 0.0)


def middle_of(where, own, received, mixed, x, segments):
    width, length = x.shape[1] + 1, x.shape[2]
    block = length // 4
    anywhere = pl.BlockSpec(memory_space=pltpu.HBM)
    spec = tokens_spec(width, block)
    return kernel_call(
        middle_kernel,
        "middle",
        pltpu.PrefetchScalarGridSpec(
            num_scalar_prefetch=1,
            grid=(4,),
            in_specs=[anywhere] * 5
            + [tokens_spec(width // GROUPS, block)] * GROUPS
            + [row_spec(width, block), pl.BlockSpec((1, 1, block), lambda t, w: (w[0], 0, t))],
            out_specs=[spec, spec, whole((8, 128)), whole((width, width))],
            scratch_shapes=[pltpu.SemaphoreType.DMA((4,))],
        ),
        [pltpu.HBM((width, length), LOW)] * 2
        + [jax.ShapeDtypeStruct((8, 128), FULL), pltpu.HBM((width, width), LOW)],
        2 * length * width * width,
        12 * length * width,
        vmem=20,
    )(where, own, *received, *mixed, x, segments)


def gelu_both(hidden):
    rate = 0.7978845608028654
    square = hidden * hidden
    half = 0.5 + 0.5 * jnp.tanh(hidden * (rate + (rate * 0.044715) * square))
    slope = half + hidden * (2.0 * rate + (6.0 * rate * 0.044715) * square) * (half - half * half)
    return hidden * half, slope


def chunks(length, count):
    return [slice(i * (length // count), (i + 1) * (length // count)) for i in range(count)]


def hidden_kernel(first, where_ref, own_ref, *refs):
    received, refs = refs[:8], refs[8:]
    (nm_hbm, ga_hbm, g_hbm) = refs[:3]
    (act_hbm, grad_hbm, w_hbm, *sums_hbm) = refs[-17:-10]
    (weights, nm_ref, g_ref, ga_ref, act_ref, grad_ref, sums_ref, w_sem, in_sem, out_sem) = refs[-10:]
    length = nm_ref.shape[1]

    def copies(place, do):
        weight_copies(
            first + 2 * place, 1, where_ref, own_ref, received[4 * place : 4 * place + 4], weights.at[place], w_sem.at[place], do
        )

    nm_copy = pltpu.make_async_copy(nm_hbm, nm_ref, in_sem.at[0])
    g_copy = pltpu.make_async_copy(g_hbm, g_ref, in_sem.at[1])
    ga_copies = [pltpu.make_async_copy(ga_hbm.at[first + 2 * i], ga_ref.at[i], in_sem.at[2 + i]) for i in range(2)]
    nm_copy.start()
    copies(0, lambda c: c.start())
    ga_copies[0].start()
    g_copy.start()
    copies(1, lambda c: c.start())
    ga_copies[1].start()
    hidden, sent = {}, []

    def send(source, target):
        copy = pltpu.make_async_copy(source, target, out_sem.at[len(sent)])
        copy.start()
        sent.append(copy)

    def enter(task):
        place, tokens = task
        hidden[task] = dot(weights[place], nm_ref[:, tokens], 0, 0)

    def bend(task):
        place, tokens = task
        value, slope = gelu_both(hidden.pop(task))
        act_ref[place, :, tokens] = value.astype(LOW)
        grad_ref[place, :, tokens] = (ga_ref[place, :, tokens].astype(FULL) * slope).astype(LOW)

    def down(place, which):
        rows = halves(where_ref, nm_ref.shape[0])[which][1]
        sums_ref[2 + which, place] = dot(act_ref[place, rows, :], g_ref[...], 1, 1).astype(LOW)
        send(sums_ref.at[2 + which, place], sums_hbm[2 + which].at[place])

    def up(place, which):
        rows = halves(where_ref, nm_ref.shape[0])[which][1]
        sums_ref[which, place] = dot(nm_ref[rows, :], grad_ref[place], 1, 1).astype(LOW)
        send(sums_ref.at[which, place], sums_hbm[which].at[place])

    def finished(place):
        send(weights.at[place], w_hbm.at[place])
        send(act_ref.at[place], act_hbm.at[place])
        send(grad_ref.at[place], grad_hbm.at[place])

    def tasks(place):
        return [(place, tokens) for tokens in chunks(length, 4)]

    nm_copy.wait()
    copies(0, lambda c: c.wait())
    ga_copies[0].wait()
    in_stages(tasks(0), (enter, bend))
    g_copy.wait()
    copies(1, lambda c: c.wait())
    ga_copies[1].wait()
    finished(0)
    between = [(down, 1), (down, 0), (up, 1), (up, 0)]
    last = None
    for task, (product, which) in zip(tasks(1), between, strict=True):
        enter(task)
        if last is not None:
            bend(last)
        product(0, which)
        last = task
    bend(last)
    finished(1)
    for product, which in between:
        product(1, which)
    for copy in sent:
        copy.wait()


def hidden_of(first, where, own, received, nm, ga, g, after=()):
    width, length = nm.shape
    anywhere = pl.BlockSpec(memory_space=pltpu.HBM)
    out_shape = (
        [pltpu.HBM((2, width, length), LOW)] * 2
        + [pltpu.HBM((2, width, width), LOW)]
        + [pltpu.HBM((2, width // 2, width), LOW)] * 4
    )
    return kernel_call(
        functools.partial(hidden_kernel, first),
        "hidden",
        pltpu.PrefetchScalarGridSpec(
            num_scalar_prefetch=1,
            grid=(1,),
            in_specs=[anywhere] * (12 + len(after)),
            out_specs=[anywhere] * 7,
            scratch_shapes=[
                pltpu.VMEM((2, width, width), LOW),
                pltpu.VMEM((width, length), LOW),
                pltpu.VMEM((width, length), LOW),
                pltpu.VMEM((2, width, length), LOW),
                pltpu.VMEM((2, width, length), LOW),
                pltpu.VMEM((2, width, length), LOW),
                pltpu.VMEM((4, 2, width // 2, width), LOW),
                pltpu.SemaphoreType.DMA((2, 4)),
                pltpu.SemaphoreType.DMA((4,)),
                pltpu.SemaphoreType.DMA((14,)),
            ],
        ),
        out_shape,
        14e9,
        14 * length * width,
        vmem=58,
    )(where, own, *[a for r in received for a in r], nm, ga, g, *after)


def output_kernel(where_ref, *refs):
    (act_a, act_b, grad_a, grad_b, up_a, up_b, down_ref, mid_ref, cot_ref, seg_ref) = refs[:10]
    (keep_out, send_out, gmid_ref, gab_ref, sums_ref) = refs[-5:]
    step = pl.program_id(0)
    width, length = mid_ref.shape

    @pl.when(step == 0)
    def _():
        sums_ref[...] = jnp.zeros_like(sums_ref)

    on_attention = where_ref[0] == 0
    products = {}

    def multiply(tokens):
        out = grad = 0.0
        for group in range(4):
            act = (act_a, act_b)[group % 2][group // 2, :, tokens]
            slope_grad = (grad_a, grad_b)[group % 2][group // 2, :, tokens]
            out = out + dot(down_ref[group * width : (group + 1) * width, :], act, 0, 0)
            grad = grad + dot((up_a, up_b)[group % 2][group // 2], slope_grad)
        products[tokens] = out, grad

    def finish(tokens):
        out, grad = products.pop(tokens)
        middle = mid_ref[:, tokens]
        wide = widened(middle)
        output = (wide + compressed(out)).astype(LOW)
        lane = lax.broadcasted_iota(jnp.int32, sums_ref.shape, 1)
        sums_ref[...] += jnp.where(lane == 1, square_sum(output, seg_ref[0][:, tokens] > 0), 0.0)
        keep_out[:, tokens] = jnp.where(on_attention, middle, output)
        send_out[:, tokens] = jnp.where(on_attention, output, middle)
        normed, inverse = crms(wide)
        grad = (cot_ref[0, :, tokens].astype(FULL) + widened_back(crms_back(normed, inverse, grad))).astype(LOW)
        gmid_ref[:, tokens] = grad
        gab_ref[:, tokens] = compressed_back(grad).astype(LOW)

    in_stages(chunks(length, 2), (multiply, finish))


def output_of(where, acts, grads, ups, down_weight, middle, cot, segments, after=()):
    width, length = middle.shape
    steps = 2
    block = length // steps
    spec = tokens_spec(width, block)
    pair = pl.BlockSpec((2, width, block), lambda t, w: (0, 0, t))
    row = jax.ShapeDtypeStruct((width, length), LOW)
    return kernel_call(
        output_kernel,
        "output",
        pltpu.PrefetchScalarGridSpec(
            num_scalar_prefetch=1,
            grid=(steps,),
            in_specs=[pair] * 4
            + [pl.BlockSpec((2, width, width), lambda t, w: (0, 0, 0), pipeline_mode=pl.Buffered(1))] * 2
            + [pl.BlockSpec(down_weight.shape, lambda t, w: (0, 0), pipeline_mode=pl.Buffered(1))]
            + [spec, row_spec(width, block)]
            + [pl.BlockSpec((1, 1, block), lambda t, w: (w[0], 0, t))]
            + [pl.BlockSpec(memory_space=pltpu.HBM)] * len(after),
            out_specs=[spec] * 4 + [whole((8, 128))],
        ),
        [row] * 4 + [jax.ShapeDtypeStruct((8, 128), FULL)],
        20e9,
        24 * length * width,
        vmem=40,
    )(where, *acts, *grads, *ups, down_weight, middle, cot, segments, *after)


def mixed_grad_kernel(where_ref, gab_ref, w_ref, *refs):
    mixed_refs, gm_refs, (delta_ref, keep_ref, send_ref, mixed_all) = refs[:GROUPS], refs[-GROUPS - 4 : -4], refs[-4:]
    gab = gab_ref[...]
    part = gm_refs[0].shape[0]
    heads = part // HEAD_DIM
    for group in range(GROUPS):
        rows = slice(group * part, (group + 1) * part)
        grads = dot(w_ref[rows, :], gab).astype(LOW)
        gm_refs[group][...] = grads
        mixed = mixed_refs[group][...]
        mixed_all[rows, :] = mixed
        product = grads.astype(FULL) * mixed.astype(FULL)
        for head in range(heads):
            delta_ref[group, head : head + 1, :] = jnp.sum(
                product[head * HEAD_DIM : (head + 1) * HEAD_DIM], axis=0, keepdims=True
            )
    for place, rows in halves(where_ref, mixed_all.shape[0]):
        (keep_ref, send_ref)[place][...] = dot(mixed_all[rows, :], gab, 1, 1).astype(LOW)


def mixed_grad(where, gab, w, mixed, after=()):
    width, length = gab.shape
    part = width // GROUPS
    heads = part // HEAD_DIM
    outs = kernel_call(
        mixed_grad_kernel,
        "mixed_grad",
        pltpu.PrefetchScalarGridSpec(
            num_scalar_prefetch=1,
            grid=(1,),
            in_specs=[whole((width, length)), whole((width, width))]
            + [whole((part, length))] * GROUPS
            + [pl.BlockSpec(memory_space=pltpu.HBM)] * len(after),
            out_specs=[whole((part, length))] * GROUPS
            + [whole((GROUPS, heads, length))]
            + [whole((width // 2, width))] * 2,
            scratch_shapes=[pltpu.VMEM((width, length), LOW)],
        ),
        [jax.ShapeDtypeStruct((part, length), LOW)] * GROUPS
        + [jax.ShapeDtypeStruct((GROUPS, heads, length), FULL)]
        + [jax.ShapeDtypeStruct((width // 2, width), LOW)] * 2,
        4 * length * width * width,
        8 * length * width,
        vmem=28,
    )(where, gab, w, *mixed, *after)
    return outs[:GROUPS], outs[GROUPS], outs[GROUPS + 1], outs[GROUPS + 2]


def input_grad_kernel(where_ref, x_ref, gmid_ref, *refs):
    grad_refs, w_refs, (keep_ref, *send_refs) = refs[:GROUPS], refs[GROUPS : 2 * GROUPS], refs[-3:]
    on_attention = where_ref[0] == 0
    grad_normed = dot(w_refs[0][...], grad_refs[0][...])
    for group in range(1, GROUPS):
        grad_normed = grad_normed + dot(w_refs[group][...], grad_refs[group][...])
    normed, inverse = crms(widened(x_ref[0]))
    middle = gmid_ref[...]
    grad = (middle.astype(FULL) + widened_back(crms_back(normed, inverse, grad_normed))).astype(LOW)
    keep_ref[...] = jnp.where(on_attention, grad, middle)
    sent = jnp.where(on_attention, middle, grad)
    for part, send_ref in enumerate(send_refs):

        @pl.when((pl.program_id(0) > 0) == (part == 1))
        def _(send_ref=send_ref):
            send_ref[...] = sent


def input_grad(where, x, grad_middle, grads, weights, after=()):
    width, length = grad_middle.shape
    spec = tokens_spec(width, length // 4)
    return kernel_call(
        input_grad_kernel,
        "input_grad",
        pltpu.PrefetchScalarGridSpec(
            num_scalar_prefetch=1,
            grid=(4,),
            in_specs=[row_spec(width, length // 4), spec]
            + [spec] * GROUPS
            + [whole((width, width))] * GROUPS
            + [pl.BlockSpec(memory_space=pltpu.HBM)] * len(after),
            out_specs=[
                spec,
                pl.BlockSpec((width, length // 4), lambda t, w: (0, 0)),
                pl.BlockSpec((width, length // 4), lambda t, w: (0, jnp.maximum(t - 1, 0))),
            ],
        ),
        [jax.ShapeDtypeStruct((width, tokens), LOW) for tokens in (length, length // 4, length - length // 4)],
        6 * length * width * width,
        12 * length * width,
        vmem=30,
    )(where, x, grad_middle, *grads, *weights, *after)


def rows_kernel(where_ref, kept_ref, *refs):
    other_refs, out_ref = refs[:-1], refs[-1]
    kept = kept_ref[...].astype(FULL)
    other = other_refs[0][...].astype(FULL)
    if len(other_refs) > 1:
        other = jnp.where(pl.program_id(0) == 0, other, other_refs[1][...].astype(FULL))
    mine = where_ref[0] == 0
    out_ref[...] = jnp.stack([jnp.where(mine, kept, other), jnp.where(mine, other, kept)], axis=1).astype(LOW)


def rows_of(where, kept, others, after=()):
    width, length = kept.shape
    block = length // 4
    places = [lambda t, w: (0, t)] if len(others) == 1 else [lambda t, w: (0, 0), lambda t, w: (0, jnp.maximum(t - 1, 0))]

    def body(where_ref, *refs):
        rows_kernel(where_ref, *refs[: 1 + len(others)], refs[-1])

    out = kernel_call(
        body,
        "rows",
        pltpu.PrefetchScalarGridSpec(
            num_scalar_prefetch=1,
            grid=(4,),
            in_specs=[tokens_spec(width, block)]
            + [pl.BlockSpec((width, block), place) for place in places]
            + [pl.BlockSpec(memory_space=pltpu.HBM)] * len(after),
            out_specs=pl.BlockSpec((width, 2, block), lambda t, w: (0, 0, t)),
        ),
        pltpu.HBM((width - 1, 2, length), LOW),
        2e10,
        length,
        vmem=40,
    )(where, kept, *others, *after)
    return jnp.transpose(out, (1, 2, 0))[None]


def partner(block, distance):
    size = lax.axis_size("dp")
    return lax.ppermute(block, "dp", [(i, i ^ distance) for i in range(size)])


def across(block):
    return lax.ppermute(block, "section", [(0, 1), (1, 0)])


def split(left, right, distance):
    bit = (lax.axis_index("dp") & distance) // distance
    half = left.shape[1] // 2
    part = lambda a, at: lax.dynamic_slice_in_dim(a, at * half, half, 1)
    return add_low(part(left, bit), part(right, bit)), add_low(part(left, 1 - bit), part(right, 1 - bit))


def add_low(left, right):
    return (left.astype(FULL) + right.astype(FULL)).astype(LOW)


class Scatter:
    def __init__(self, keep, got, order):
        self.order = order
        self.keep, self.got = keep, got
        self.at = 0

    def step(self, *others):
        self.at += 1
        self.got = later(self.got, *others)
        self.keep, self.sent = split(self.keep, self.got, self.order[self.at])
        self.got = partner(self.sent, self.order[self.at])

    def total(self, *others):
        while self.at < len(self.order) - 1:
            self.step(*others)
        return add_low(self.keep, later(self.got, *others))


class Gather:
    def __init__(self, shard, order, *others):
        self.left = list(reversed(order))
        self.held = later(shard, *others)[None] if others else shard[None]
        self.got = partner(self.held, self.left.pop(0))

    def step(self, *others):
        self.held = jnp.concatenate([self.held, later(self.got, *others)], axis=0)
        self.got = partner(self.held, self.left.pop(0))

    def all(self, *others):
        while self.left:
            self.step(*others)
        return self.held, self.got


def number_of(order):
    me = lax.axis_index("dp").astype(jnp.int32)
    number = jnp.int32(0)
    for distance in order:
        number = number * 2 + (me // distance) % 2
    return number


def later(value, *others):
    return lax.optimization_barrier((value, *others))[0]


def gathered_specs(array, per_step):
    half_steps = array.shape[0] // per_step
    block = (per_step, *array.shape[1:])
    return [
        pl.BlockSpec(block, lambda e, w: (jnp.minimum(e, half_steps - 1), 0, 0)),
        pl.BlockSpec(block, lambda e, w: (jnp.maximum(e - half_steps, 0), 0, 0)),
    ]


def each_entry(number_ref, halves_refs, do):
    steps = pl.num_programs(0)
    per_step = halves_refs[0].shape[0]
    for place, ref in enumerate(halves_refs):

        @pl.when((pl.program_id(0) * 2 >= steps) == (place == 1))
        def _(ref=ref):
            for entry in range(per_step):
                do((number_ref[1] % per_step) ^ entry, ref, entry)


def down_sum_kernel(number_ref, near_ref, far_ref, out_ref):
    rows = out_ref.shape[2]

    def write(place, ref, entry):
        for block in range(2):
            out_ref[block, place] = ref[entry, block * rows : (block + 1) * rows, :].astype(FULL)

    each_entry(number_ref, (near_ref, far_ref), write)


def down_sum(number, near, far, width):
    entries = 2 * near.shape[0]
    rows = width // entries
    per_step = entries // 4
    out = kernel_call(
        down_sum_kernel,
        "down_sum",
        pltpu.PrefetchScalarGridSpec(
            num_scalar_prefetch=1,
            grid=(4,),
            in_specs=gathered_specs(near, per_step),
            out_specs=pl.BlockSpec((2, per_step, rows, width), lambda e, w: (0, (w[1] // per_step) ^ e, 0, 0)),
        ),
        jax.ShapeDtypeStruct((2, entries, rows, width), FULL),
        2e10,
        width,
        vmem=58,
    )(number, near, far)
    return out.reshape(2 * width, width)


def columns_of(numbers):
    if numbers[0] < 0:
        return [[(0, 3 * block, 3)] for block in (-numbers[0] - 1, -numbers[1] - 1)]
    return [
        [(0, 9, 3)] if block == 0 else [(piece, own_column_static(block - 1, piece, 0), 1) for piece in range(3)]
        for block in numbers
    ]


def counts_of(section, slots, width, near_ref, far_ref):
    rows = sum(ref[entry, :16, :128].astype(FULL) for ref in (near_ref, far_ref) for entry in range(ref.shape[0]))
    lane = lax.broadcasted_iota(jnp.int32, (1, 128), 1)
    total = [
        jnp.sum(jnp.where((lane % 3 == which) & (lane < 9), rows[:1], 0.0), axis=1, keepdims=True) for which in range(3)
    ]
    square = jnp.where(section == 0, total[0], total[1])
    count = jnp.where(section == 0, total[2], slots - total[2])
    root = jnp.sqrt(square / (total[2] * width))
    return jnp.broadcast_to(jnp.where(lane == 0, root, jnp.where(lane == 1, count, 0.0)), (8, 128))


def first_sum_kernel(skip, blocks, slots, number_ref, near_ref, far_ref, *refs):
    buffer, sem = refs[-2:]
    out_ref = refs[-4] if slots else refs[-3]
    entries, rows, columns = out_ref.shape
    width = columns // 4
    part = width // 3
    half = entries // 2
    if slots:
        refs[-3][...] = counts_of(number_ref[0], slots, width, near_ref, far_ref)
    for section in range(2):

        @pl.when(number_ref[0] == section)
        def _(section=section):
            pieces = columns_of(blocks[section])

            def copies(place, do):
                first = pl.multiple_of(jnp.where(number_ref[1] < half, place, 1 - place) * half, half)
                for at in range(2):
                    for order, (start, column, size) in enumerate(pieces[at]):
                        do(
                            pltpu.make_async_copy(
                                buffer.at[at, pl.ds(first, half), :, pl.ds(start * part, size * part)],
                                out_ref.at[pl.ds(first, half), :, pl.ds(column * part, size * part)],
                                sem.at[place, at, order],
                            )
                        )

            for place, ref in enumerate((near_ref, far_ref)):
                for entry in range(half):
                    for at in range(2):
                        values = ref[entry, skip + at * rows : skip + (at + 1) * rows, :]
                        buffer[at, number_ref[1] ^ (entry + place * half)] = values.astype(FULL)
                copies(place, lambda c: c.start())
            for place in range(2):
                copies(place, lambda c: c.wait())


def first_sum(number, skip, blocks, gathered, width, before=None, slots=None):
    near, far = gathered
    entries = 2 * near.shape[0]
    rows = width // entries
    held = [] if before is None else [before]
    anywhere = pl.BlockSpec(memory_space=pl.ANY)
    return pl.pallas_call(
        functools.partial(first_sum_kernel, skip, blocks, slots),
        grid_spec=pltpu.PrefetchScalarGridSpec(
            num_scalar_prefetch=1,
            grid=(1,),
            in_specs=[whole(near.shape), whole(far.shape)] + [anywhere] * len(held),
            out_specs=[anywhere] + [whole((8, 128))] * bool(slots),
            scratch_shapes=[pltpu.VMEM((2, entries, rows, width), FULL), pltpu.SemaphoreType.DMA((2, 2, 3))],
        ),
        out_shape=[jax.ShapeDtypeStruct((entries, rows, 4 * width), FULL)]
        + [jax.ShapeDtypeStruct((8, 128), FULL)] * bool(slots),
        input_output_aliases={3: 0} if held else {},
        compiler_params=pltpu.CompilerParams(vmem_limit_bytes=24 * 2**20),
        cost_estimate=pl.CostEstimate(flops=1000, bytes_accessed=1000, transcendentals=0),
        name="first_sum",
    )(number, near, far, *held)


def on_device(stream_in, cotangent, weights_first, down_weight, segments):
    rows_dev, length, compact_width = stream_in.shape
    width = compact_width + 1
    section = lax.axis_index("section").astype(jnp.int32)
    index = lax.axis_index("dp").astype(jnp.int32)
    size = lax.axis_size("dp")
    on_attention = section == 0
    where = jnp.stack([section, index & 3, index & 1])
    segments3 = segments.reshape(rows_dev, 1, length)
    order = [1 << i for i in range(size.bit_length() - 1)]
    flat = lambda a: a.reshape(-1, width)

    near = [across(piece) for piece in weight_piece(where, weights_first)]
    x, cot = jnp.transpose(stream_in, (0, 2, 1)), jnp.transpose(cotangent, (0, 2, 1))
    nt, g = prep(where, x, cot)
    ga = branch_grad(g, down_weight, after=(near[0],))
    attended, received, besides = [], [], [partner(later(near[0], nt), 2), partner(later(near[1], ga), 2)]
    for group in range(4):
        quarter, beside = near[group], besides[group]
        done = [attended[group - 1][1] if group else ga]
        received.append((quarter, beside, partner(quarter, 1), partner(later(beside, *done), 1)))
        if group < 2:
            besides.append(partner(later(near[group + 2], *done), 2))
        if group < GROUPS:
            attended.append(attend(group, where, weights_first, received[group], nt, segments3))
    mixed = [a[1] for a in attended]
    middle, nm, sums_mid, out_weights = middle_of(where, weights_first, received[GROUPS], mixed, x, segments3)

    act_a, grad_a, weights_a, keep_a, send_a, *down_a = hidden_of(0, where, weights_first, received[0::2], nm, ga, g)
    up_a, got_a = partner(send_a, 1), partner(down_a[1], 1)
    act_b, grad_b, weights_b, keep_b, send_b, *down_b = hidden_of(
        1, where, weights_first, received[1::2], nm, ga, g, after=(act_a,)
    )
    up_b, got_b = partner(send_b, 1), partner(down_b[1], 1)
    halves_a, halves_b = split(keep_a, up_a, order[1]), split(keep_b, up_b, order[1])
    up = Scatter(keep_a, up_a, order)
    up.keep, up.sent = (jnp.concatenate(both) for both in zip(halves_a, halves_b, strict=True))
    up.at, up.got = 1, partner(up.sent, order[1])
    kept, sent = [], []
    for keep, got in ((down_a[0], got_a), (down_b[0], got_b)):
        lower, upper = add_low(keep[0], got[0]), add_low(keep[1], got[1])
        kept.append(jnp.where(on_attention, lower, upper))
        sent.append(jnp.where(on_attention, upper, lower))
    kept, sent = jnp.stack(kept), later(jnp.stack(sent), up.sent)
    down = Scatter(kept, across(sent), order)
    keep_out, send_out, grad_mid, gab, sums_out = output_of(
        where, (act_a, act_b), (grad_a, grad_b), (weights_a, weights_b), down_weight, middle, cot, segments3, after=(sent,)
    )
    up.step(gab)
    gm, delta, keep_w, send_w = mixed_grad(where, gab, out_weights, mixed, after=(up.sent,))
    keeps, sends, grads = [keep_w], [send_w], []

    def backward(group, *after):
        qkv, _, total, _ = attended[group]
        keep_w, send_w, grad = attend_back(where, qkv, gm[group], total, delta[group], segments3, nt, after=after)
        keeps.append(keep_w)
        sends.append(send_w)
        grads.append(grad)

    down.step(delta)
    backward(0, down.sent)
    up.step(grads[0])
    down.step(up.sent)
    sent_a = later(jnp.stack(sends), down.sent)
    attn_a = Scatter(jnp.stack(keeps), partner(sent_a, 1), order)
    backward(1, sent_a)
    attn_a.step(grads[1])
    down.step(attn_a.sent)
    received_out = across(send_out)
    backward(2, down.sent)
    down = down.total(grads[2])
    sum_dn = Gather(flat(down), order)
    up = up.total(sum_dn.held)
    up_a, up_b, rows = up[:2], up[2:], up.shape[1]
    attn_a.step(up)
    attn_b = Scatter(jnp.stack(keeps[2:]), partner(later(jnp.stack(sends[2:]), attn_a.sent), 1), order)
    attn_b.step()
    keep_grad, *send_grad = input_grad(
        where, x, grad_mid, grads, [a[3] for a in attended], after=(attn_b.sent, received_out)
    )
    attn_a.step(keep_grad)
    attn_b.step(attn_a.sent)
    sum_dn.step(attn_b.sent)
    attn_a = attn_a.total(sum_dn.held)

    scalars = (sums_mid + sums_out)[0, :3]

    def scalar_rows(values):
        high = values.astype(LOW)
        rest = values - high.astype(FULL)
        middle_part = rest.astype(LOW)
        low = (rest - middle_part.astype(FULL)).astype(LOW)
        packed = jnp.concatenate([high, middle_part, low])
        return jnp.zeros((16, width), LOW).at[0, :9].set(packed)

    def scalars_of(block):
        parts = block[..., 0, :9].astype(FULL)
        return parts[..., :3] + parts[..., 3:6] + parts[..., 6:9]

    mine_a, theirs_a = jnp.where(on_attention, attn_a, up_a), jnp.where(on_attention, up_a, attn_a)
    sent_a = jnp.concatenate([scalar_rows(scalars), flat(theirs_a)])
    swapped = across(sent_a)
    attn_b.step(sent_a)
    swapped = later(swapped, attn_b.sent)
    pair = scalars + scalars_of(swapped[:16])
    shard_a = add_low(flat(mine_a), swapped[16:])
    sum_a = Gather(jnp.concatenate([scalar_rows(pair), shard_a]), order)
    received_grad = [across(later(send_grad[0], sum_a.held))]
    sum_dn.step(sum_a.held)
    received_grad[0] = later(received_grad[0], sum_dn.held)
    attn_b = attn_b.total(received_grad[0])
    mine_b, theirs_b = jnp.where(on_attention, attn_b, up_b), jnp.where(on_attention, up_b, attn_b)
    swapped_b = across(flat(theirs_b))
    received_grad.append(across(later(send_grad[1], theirs_b)))
    sum_a.step(theirs_b)
    stream_out = rows_of(where, keep_out, [received_out], after=(sum_a.held,))
    sum_b = Gather(add_low(flat(mine_b), later(swapped_b, stream_out)), order)
    sum_a.step(sum_b.held)
    sum_dn.step(sum_a.held)
    number = jnp.stack([section, number_of(order)])
    grad_down = down_sum(later(number, sum_dn.held), *sum_dn.all(), width)
    sum_b.step(grad_down)
    sum_b.step(sum_a.got)
    sum_a.step(sum_b.held)
    stream_grad = rows_of(where, keep_grad, received_grad, after=(sum_a.held,))
    sum_b.step(stream_grad)
    sum_a, sum_b = sum_a.all(), sum_b.all()
    slots = float(rows_dev * length * size)
    grad_first, counts = first_sum(later(number, sum_b[0]), 16, ((0, 1), (-1, -3)), sum_a, width, slots=slots)
    (grad_first,) = first_sum(number, 0, ((2, 3), (-2, -4)), sum_b, width, before=grad_first)
    grad_first = grad_first.reshape(width, 4 * width)
    residual_rms, token_count = counts[0, :1], counts[0, 1:2].astype(jnp.int32)
    return (
        stream_out,
        stream_grad,
        grad_first[None],
        grad_down,
        residual_rms,
        token_count,
    )


def solution(mesh):
    placed = (
        P("dp", None, None),
        P("dp", None, None),
        P("section", None, None),
        P(),
        P("dp", None),
    )
    return jax.shard_map(
        on_device,
        mesh=mesh,
        in_specs=placed,
        out_specs=(
            P("section", "dp", None, None),
            P("section", "dp", None, None),
            P("section", None, None),
            P("section", None),
            P("section"),
            P("section"),
        ),
        check_vma=False,
    )
```

```python
import functools

import jax
import jax.numpy as jnp
from jax import lax
from jax.experimental import pallas as pl
from jax.experimental.pallas import tpu as pltpu
from jax.sharding import PartitionSpec as P

HEADS = 12
HEAD_DIM = 64
GROUPS = 3
EPSILON = 1e-06
MASKED = -1e30
SCALE = HEAD_DIM ** (-0.5)
LOG2E = 1.4426950408889634
LOW = jnp.bfloat16
FULL = jnp.float32


def dot(left, right, left_dim=1, right_dim=0):
    return lax.dot_general(
        left, right, (((left_dim,), (right_dim,)), ((), ())), preferred_element_type=FULL
    )


def kernel_call(body, name, grid_spec, out_shape, flops, moved, vmem=32):
    return pl.pallas_call(
        body,
        grid_spec=grid_spec,
        out_shape=out_shape,
        compiler_params=pltpu.CompilerParams(vmem_limit_bytes=vmem * 2**20),
        cost_estimate=pl.CostEstimate(flops=int(flops * 1.5), bytes_accessed=int(moved * 1.5), transcendentals=0),
        name=name,
    )


def last_row(block):
    return lax.broadcasted_iota(jnp.int32, block.shape, 0) == block.shape[0] - 1


def widened(block):
    values = jnp.where(last_row(block), 0.0, block.astype(FULL))
    return jnp.where(last_row(block), -jnp.sum(values, axis=0, keepdims=True), values)


def crms(values):
    inverse = lax.rsqrt(jnp.mean(values * values, axis=0, keepdims=True) + EPSILON)
    return values * inverse, inverse


def crms_back(normed, inverse, grad):
    return inverse * (grad - normed * jnp.mean(grad * normed, axis=0, keepdims=True))


def compressed(branch):
    return branch - jnp.mean(branch, axis=0, keepdims=True)


def widened_back(grad):
    return grad - grad[grad.shape[0] - 1 :]


def compressed_back(block):
    values = jnp.where(last_row(block), 0.0, block.astype(FULL))
    return values - jnp.mean(values, axis=0, keepdims=True)


def square_sum(rounded, valid):
    wide = widened(rounded)
    per_token = jnp.sum(wide * wide, axis=0, keepdims=True)
    return jnp.sum(jnp.where(valid, per_token, 0.0), axis=1, keepdims=True)


def prep_kernel(where_ref, x_ref, cot_ref, nt_ref, g_ref):
    normed, _ = crms(widened(x_ref[0]))
    nt_ref[...] = normed.astype(LOW)
    g_ref[...] = compressed_back(cot_ref[0]).astype(LOW)


def tokens_spec(width, block):
    return pl.BlockSpec((width, block), lambda t, *_: (0, t))


def row_spec(width, block):
    return pl.BlockSpec((1, width, block), lambda t, w: (w[0], 0, t))


def prep(where, x, cot):
    width, length = x.shape[1] + 1, x.shape[2]
    spec = tokens_spec(width, length // 4)
    return kernel_call(
        prep_kernel,
        "prep",
        pltpu.PrefetchScalarGridSpec(
            num_scalar_prefetch=1, grid=(4,), in_specs=[row_spec(width, length // 4)] * 2, out_specs=[spec] * 2
        ),
        [jax.ShapeDtypeStruct((width, length), LOW)] * 2,
        0,
        8 * length * width,
        vmem=16,
    )(where, x, cot)


def branch_grad_kernel(g_ref, w_ref, *refs):
    out_ref = refs[-1]
    out_ref[0] = dot(w_ref[...], g_ref[...]).astype(LOW)


def branch_grad(g, down_weight, after=()):
    width, length = g.shape
    blocks = down_weight.shape[0] // width
    return kernel_call(
        branch_grad_kernel,
        "branch_grad",
        pltpu.PrefetchScalarGridSpec(
            num_scalar_prefetch=0,
            grid=(blocks,),
            in_specs=[
                pl.BlockSpec((width, length), lambda b: (0, 0)),
                pl.BlockSpec((width, width), lambda b: (b, 0)),
            ]
            + [pl.BlockSpec(memory_space=pltpu.HBM)] * len(after),
            out_specs=pl.BlockSpec((1, width, length), lambda b: (b, 0, 0)),
        ),
        pltpu.HBM((blocks, width, length), LOW),
        2 * length * width * width * blocks,
        2 * length * width * (blocks + 1),
        vmem=20,
    )(g, down_weight, *after)


def own_column_static(group, piece, section):
    if section == 1 or group == GROUPS:
        return 3 * group + piece
    return group + GROUPS * piece


def piece_kernel(where_ref, w_ref, *out_refs):
    part = out_refs[0].shape[1] // 3
    for section in range(2):

        @pl.when(where_ref[0] == section)
        def _(section=section):
            for group in range(4):
                for piece in range(3):
                    column = own_column_static(group, piece, section) * part
                    out_refs[group][:, piece * part : (piece + 1) * part] = w_ref[0, :, column : column + part]


def weight_piece(where, weights):
    rows, columns = weights.shape[1:]
    shape = (rows // 4, columns // 4)
    return kernel_call(
        piece_kernel,
        "weight_piece",
        pltpu.PrefetchScalarGridSpec(
            num_scalar_prefetch=1,
            grid=(1,),
            in_specs=[pl.BlockSpec((1, rows // 4, columns), lambda i, w: (0, w[1], 0))],
            out_specs=[whole(shape)] * 4,
        ),
        [jax.ShapeDtypeStruct(shape, LOW)] * 4,
        0,
        rows * columns,
        vmem=58,
    )(where, weights)


def weight_copies(group, wanted, where_ref, own_ref, quarters, target, sem, act):
    quarter = target.shape[0] // 4
    part = target.shape[1] // 3

    @pl.when(where_ref[0] == wanted)
    def _():
        for piece in range(3):
            column = own_column_static(group, piece, wanted) * part
            act(pltpu.make_async_copy(own_ref.at[0, :, pl.ds(column, part)], target.at[:, pl.ds(piece * part, part)], sem.at[piece]))

    @pl.when(where_ref[0] != wanted)
    def _():
        for place, source in enumerate(quarters):
            index = where_ref[1] ^ (0, 2, 1, 3)[place]
            act(pltpu.make_async_copy(source, target.at[pl.ds(index * quarter, quarter), :], sem.at[place]))


def segment_rows(segment):
    tokens = segment.shape[1]
    ids = lax.broadcasted_iota(jnp.int32, (16, tokens), 0)
    same = segment == ids
    real = ids < 5
    queries = jnp.where(real & jnp.logical_not(same), MASKED, 0.0).astype(LOW)
    keys = jnp.where(real & same, 1.0, 0.0).astype(LOW)
    return queries, keys


def two_parts(values):
    high = values.astype(LOW)
    return high, (values - high.astype(FULL)).astype(LOW)


def minus_rows(values):
    high = values.astype(LOW)
    rest = values - high.astype(FULL)
    middle = rest.astype(LOW)
    low = rest - middle.astype(FULL)
    row = lax.broadcasted_iota(jnp.int32, (16, values.shape[1]), 0)
    parts = jnp.where(
        row == 0, high.astype(FULL), jnp.where(row == 1, middle.astype(FULL), jnp.where(row == 2, low, 0.0))
    )
    return (-parts).astype(LOW)


def three_ones(tokens):
    return jnp.where(lax.broadcasted_iota(jnp.int32, (16, tokens), 0) < 3, 1.0, 0.0).astype(LOW)


def head_tasks(heads, blocks, block):
    return [
        (head, slice(i * block, (i + 1) * block), slice(0, (i + 1) * block), i * block)
        for head in range(heads)
        for i in range(blocks)
    ]


def in_stages(tasks, stages):
    for step in range(len(tasks) + len(stages) - 1):
        for late, stage in enumerate(stages):
            if 0 <= step - late < len(tasks):
                stage(tasks[step - late])


def attend_kernel(group, where_ref, own_ref, near_ref, beside_ref, core_ref, across_ref, nt_ref, seg_ref, qkv_ref, mixed_ref, total_ref, w_ref, sem):
    copies = functools.partial(
        weight_copies, group, 0, where_ref, own_ref, (near_ref, beside_ref, core_ref, across_ref), w_ref, sem
    )
    copies(lambda c: c.start())
    copies(lambda c: c.wait())
    length = nt_ref.shape[1]
    width = qkv_ref.shape[0] // 3
    heads, blocks = width // HEAD_DIM, 4
    block = length // blocks
    for part in range(3):
        qkv_ref[part * width : (part + 1) * width, :] = dot(
            w_ref[:, part * width : (part + 1) * width], nt_ref[...], 0, 0
        ).astype(LOW)
    seg_queries, seg_keys = segment_rows(seg_ref[0])
    causal = lax.broadcasted_iota(jnp.int32, (block, block), 0) <= lax.broadcasted_iota(jnp.int32, (block, block), 1)
    ones = three_ones(length)
    scored, weighed = {}, {}

    def score(task):
        head, queries, keys, _ = task
        high, low = two_parts(qkv_ref[head * HEAD_DIM : (head + 1) * HEAD_DIM, queries].astype(FULL) * (SCALE * LOG2E))
        key_rows = qkv_ref[width + head * HEAD_DIM : width + (head + 1) * HEAD_DIM, keys]
        scored[task] = dot(
            jnp.concatenate([key_rows, key_rows, seg_keys[:, keys]], axis=0),
            jnp.concatenate([high, low, seg_queries[:, queries]], axis=0),
            0,
            0,
        )

    def weigh(task):
        before = task[3]
        scores = scored.pop(task)
        last = jnp.where(causal, scores[before:], MASKED)
        highest = jnp.max(last, axis=0, keepdims=True)
        if before:
            highest = jnp.maximum(highest, jnp.max(scores[:before], axis=0, keepdims=True))
        exponents = jnp.exp2(last - highest).astype(LOW)
        if before:
            exponents = jnp.concatenate([jnp.exp2(scores[:before] - highest).astype(LOW), exponents], axis=0)
        weighed[task] = (exponents, highest)

    def mix(task):
        head, queries, keys, _ = task
        exponents, highest = weighed.pop(task)
        values = qkv_ref[2 * width + head * HEAD_DIM : 2 * width + (head + 1) * HEAD_DIM, keys]
        mixed = dot(jnp.concatenate([values, ones[:, keys]], axis=0), exponents)
        total = mixed[HEAD_DIM : HEAD_DIM + 1]
        mixed_ref[head * HEAD_DIM : (head + 1) * HEAD_DIM, queries] = (mixed[:HEAD_DIM] / total).astype(LOW)
        total_ref[head : head + 1, queries] = highest + jnp.log2(total)

    in_stages(head_tasks(heads, blocks, block), (score, weigh, mix))


def attend(group, where, own, received, nt, segments):
    width, length = nt.shape
    part = width // GROUPS
    anywhere = pl.BlockSpec(memory_space=pltpu.HBM)
    return kernel_call(
        functools.partial(attend_kernel, group),
        "attend",
        pltpu.PrefetchScalarGridSpec(
            num_scalar_prefetch=1,
            grid=(1,),
            in_specs=[anywhere] * 5
            + [
                pl.BlockSpec((width, length), lambda i, w: (0, 0)),
                pl.BlockSpec((1, 1, length), lambda i, w: (w[0], 0, 0)),
            ],
            out_specs=[
                pl.BlockSpec((3 * part, length), lambda i, w: (0, 0)),
                pl.BlockSpec((part, length), lambda i, w: (0, 0)),
                pl.BlockSpec((part // HEAD_DIM, length), lambda i, w: (0, 0)),
                pl.BlockSpec((width, 3 * part), lambda i, w: (0, 0)),
            ],
            scratch_shapes=[pltpu.SemaphoreType.DMA((4,))],
        ),
        [
            pltpu.HBM((3 * part, length), LOW),
            jax.ShapeDtypeStruct((part, length), LOW),
            pltpu.HBM((part // HEAD_DIM, length), FULL),
            pltpu.HBM((width, 3 * part), LOW),
        ],
        4.5e9,
        8 * width * length,
        vmem=24,
    )(where, own, *received, nt, segments)


def attend_back_kernel(where_ref, qkv_ref, gm_ref, total_ref, delta_ref, seg_ref, nt_ref, *rest):
    keep_ref, send_ref, grads_ref, acc = rest[-4:]
    length = nt_ref.shape[1]
    width = gm_ref.shape[0]
    heads, blocks = width // HEAD_DIM, 4
    block = length // blocks
    seg_queries, seg_keys = segment_rows(seg_ref[0])
    ones = three_ones(length)
    causal = lax.broadcasted_iota(jnp.int32, (block, block), 1) <= lax.broadcasted_iota(jnp.int32, (block, block), 0)
    acc[...] = jnp.zeros_like(acc)
    scored, weighed = {}, {}

    def rows(part, head):
        return slice(part * width + head * HEAD_DIM, part * width + (head + 1) * HEAD_DIM)

    def score(task):
        head, queries, keys, _ = task
        high, low = two_parts(qkv_ref[rows(0, head), queries].astype(FULL) * (SCALE * LOG2E))
        key_rows = qkv_ref[rows(1, head), keys]
        scores = dot(
            jnp.concatenate([high, low, seg_queries[:, queries], minus_rows(total_ref[head : head + 1, queries])], axis=0),
            jnp.concatenate([key_rows, key_rows, seg_keys[:, keys], ones[:, keys]], axis=0),
            0,
            0,
        )
        grads = dot(
            jnp.concatenate([gm_ref[rows(0, head), queries], minus_rows(delta_ref[head : head + 1, queries])], axis=0),
            jnp.concatenate([qkv_ref[rows(2, head), keys], ones[:, keys]], axis=0),
            0,
            0,
        )
        scored[task] = (scores, grads)

    def weigh(task):
        before = task[3]
        scores, grads = scored.pop(task)
        last = jnp.where(causal, scores[:, before:], MASKED)
        if before:
            last = jnp.concatenate([scores[:, :before], last], axis=1)
        probs = jnp.exp2(last)
        weighed[task] = (probs.astype(LOW), (probs * grads).astype(LOW))

    def collect(task):
        head, queries, keys, _ = task
        probs, grads = weighed.pop(task)
        acc[rows(2, head), keys] += dot(gm_ref[rows(0, head), queries], probs)
        acc[rows(1, head), keys] += dot(qkv_ref[rows(0, head), queries] * LOW(SCALE), grads)
        acc[rows(0, head), queries] = dot(qkv_ref[rows(1, head), keys], grads, 1, 1) * SCALE

    in_stages(head_tasks(heads, blocks, block), (score, weigh, collect))
    grads_ref[...] = acc[...].astype(LOW)
    for place, rows_ in halves(where_ref, nt_ref.shape[0]):
        (keep_ref, send_ref)[place][...] = dot(nt_ref[rows_, :], grads_ref[...], 1, 1).astype(LOW)


def halves(where_ref, count):
    half = count // 2
    return [
        (0, pl.ds(pl.multiple_of(where_ref[2] * half, half), half)),
        (1, pl.ds(pl.multiple_of((1 - where_ref[2]) * half, half), half)),
    ]


def whole(shape):
    return pl.BlockSpec(shape, lambda *_: (0,) * len(shape))


def attend_back(where, qkv, gm, total, delta, segments, nt, after=()):
    width, length = nt.shape
    part = gm.shape[0]
    arrays = [qkv, gm, total, delta]
    return kernel_call(
        attend_back_kernel,
        "attend_back",
        pltpu.PrefetchScalarGridSpec(
            num_scalar_prefetch=1,
            grid=(1,),
            in_specs=[whole(a.shape) for a in arrays]
            + [pl.BlockSpec((1, 1, length), lambda i, w: (w[0], 0, 0)), whole(nt.shape)]
            + [pl.BlockSpec(memory_space=pltpu.HBM)] * len(after),
            out_specs=[whole((width // 2, 3 * part))] * 2 + [whole((3 * part, length))],
            scratch_shapes=[pltpu.VMEM((3 * part, length), FULL)],
        ),
        [jax.ShapeDtypeStruct((width // 2, 3 * part), LOW)] * 2 + [pltpu.HBM((3 * part, length), LOW)],
        9e9,
        8 * width * length,
        vmem=28,
    )(where, *arrays, segments, nt, *after)


def middle_kernel(where_ref, own_ref, near_ref, beside_ref, core_ref, across_ref, *refs):
    mixed_refs, (x_ref, seg_ref, mid_ref, nm_ref, sums_ref, w_ref, sem) = refs[:GROUPS], refs[GROUPS:]
    step = pl.program_id(0)

    @pl.when(step == 0)
    def _():
        copies = functools.partial(
            weight_copies, GROUPS, 0, where_ref, own_ref, (near_ref, beside_ref, core_ref, across_ref), w_ref, sem
        )
        copies(lambda c: c.start())
        copies(lambda c: c.wait())
        sums_ref[...] = jnp.zeros_like(sums_ref)

    mixed = jnp.concatenate([ref[...] for ref in mixed_refs], axis=0)
    branch = dot(w_ref[...], mixed, 0, 0)
    middle = (x_ref[0].astype(FULL) + compressed(branch)).astype(LOW)
    mid_ref[...] = middle
    normed, _ = crms(widened(middle))
    nm_ref[...] = normed.astype(LOW)
    valid = seg_ref[0] > 0
    lane = lax.broadcasted_iota(jnp.int32, sums_ref.shape, 1)
    count = jnp.sum(valid.astype(FULL), axis=1, keepdims=True)
    sums_ref[...] += jnp.where(lane == 0, square_sum(middle, valid), 0.0) + jnp.where(lane == 2, count, 0.0)


def middle_of(where, own, received, mixed, x, segments):
    width, length = x.shape[1] + 1, x.shape[2]
    block = length // 4
    anywhere = pl.BlockSpec(memory_space=pltpu.HBM)
    spec = tokens_spec(width, block)
    return kernel_call(
        middle_kernel,
        "middle",
        pltpu.PrefetchScalarGridSpec(
            num_scalar_prefetch=1,
            grid=(4,),
            in_specs=[anywhere] * 5
            + [tokens_spec(width // GROUPS, block)] * GROUPS
            + [row_spec(width, block), pl.BlockSpec((1, 1, block), lambda t, w: (w[0], 0, t))],
            out_specs=[spec, spec, whole((8, 128)), whole((width, width))],
            scratch_shapes=[pltpu.SemaphoreType.DMA((4,))],
        ),
        [pltpu.HBM((width, length), LOW)] * 2
        + [jax.ShapeDtypeStruct((8, 128), FULL), pltpu.HBM((width, width), LOW)],
        2 * length * width * width,
        12 * length * width,
        vmem=20,
    )(where, own, *received, *mixed, x, segments)


def gelu_both(hidden):
    rate = 0.7978845608028654
    square = hidden * hidden
    half = 0.5 + 0.5 * jnp.tanh(hidden * (rate + (rate * 0.044715) * square))
    slope = half + hidden * (2.0 * rate + (6.0 * rate * 0.044715) * square) * (half - half * half)
    return hidden * half, slope


def chunks(length, count):
    return [slice(i * (length // count), (i + 1) * (length // count)) for i in range(count)]


def hidden_kernel(first, where_ref, own_ref, *refs):
    received, refs = refs[:8], refs[8:]
    (nm_hbm, ga_hbm, g_hbm) = refs[:3]
    (act_hbm, grad_hbm, w_hbm, *sums_hbm) = refs[-17:-10]
    (weights, nm_ref, g_ref, ga_ref, act_ref, grad_ref, sums_ref, w_sem, in_sem, out_sem) = refs[-10:]
    length = nm_ref.shape[1]

    def copies(place, do):
        weight_copies(
            first + 2 * place, 1, where_ref, own_ref, received[4 * place : 4 * place + 4], weights.at[place], w_sem.at[place], do
        )

    nm_copy = pltpu.make_async_copy(nm_hbm, nm_ref, in_sem.at[0])
    g_copy = pltpu.make_async_copy(g_hbm, g_ref, in_sem.at[1])
    ga_copies = [pltpu.make_async_copy(ga_hbm.at[first + 2 * i], ga_ref.at[i], in_sem.at[2 + i]) for i in range(2)]
    nm_copy.start()
    copies(0, lambda c: c.start())
    ga_copies[0].start()
    g_copy.start()
    copies(1, lambda c: c.start())
    ga_copies[1].start()
    hidden, sent = {}, []

    def send(source, target):
        copy = pltpu.make_async_copy(source, target, out_sem.at[len(sent)])
        copy.start()
        sent.append(copy)

    def enter(task):
        place, tokens = task
        hidden[task] = dot(weights[place], nm_ref[:, tokens], 0, 0)

    def bend(task):
        place, tokens = task
        value, slope = gelu_both(hidden.pop(task))
        act_ref[place, :, tokens] = value.astype(LOW)
        grad_ref[place, :, tokens] = (ga_ref[place, :, tokens].astype(FULL) * slope).astype(LOW)

    def down(place, which):
        rows = halves(where_ref, nm_ref.shape[0])[which][1]
        sums_ref[2 + which, place] = dot(act_ref[place, rows, :], g_ref[...], 1, 1).astype(LOW)
        send(sums_ref.at[2 + which, place], sums_hbm[2 + which].at[place])

    def up(place, which):
        rows = halves(where_ref, nm_ref.shape[0])[which][1]
        sums_ref[which, place] = dot(nm_ref[rows, :], grad_ref[place], 1, 1).astype(LOW)
        send(sums_ref.at[which, place], sums_hbm[which].at[place])

    def finished(place):
        send(weights.at[place], w_hbm.at[place])
        send(act_ref.at[place], act_hbm.at[place])
        send(grad_ref.at[place], grad_hbm.at[place])

    def tasks(place):
        return [(place, tokens) for tokens in chunks(length, 4)]

    nm_copy.wait()
    copies(0, lambda c: c.wait())
    ga_copies[0].wait()
    in_stages(tasks(0), (enter, bend))
    g_copy.wait()
    copies(1, lambda c: c.wait())
    ga_copies[1].wait()
    finished(0)
    between = [(down, 1), (down, 0), (up, 1), (up, 0)]
    last = None
    for task, (product, which) in zip(tasks(1), between, strict=True):
        enter(task)
        if last is not None:
            bend(last)
        product(0, which)
        last = task
    bend(last)
    finished(1)
    for product, which in between:
        product(1, which)
    for copy in sent:
        copy.wait()


def hidden_of(first, where, own, received, nm, ga, g, after=()):
    width, length = nm.shape
    anywhere = pl.BlockSpec(memory_space=pltpu.HBM)
    out_shape = (
        [pltpu.HBM((2, width, length), LOW)] * 2
        + [pltpu.HBM((2, width, width), LOW)]
        + [pltpu.HBM((2, width // 2, width), LOW)] * 4
    )
    return kernel_call(
        functools.partial(hidden_kernel, first),
        "hidden",
        pltpu.PrefetchScalarGridSpec(
            num_scalar_prefetch=1,
            grid=(1,),
            in_specs=[anywhere] * (12 + len(after)),
            out_specs=[anywhere] * 7,
            scratch_shapes=[
                pltpu.VMEM((2, width, width), LOW),
                pltpu.VMEM((width, length), LOW),
                pltpu.VMEM((width, length), LOW),
                pltpu.VMEM((2, width, length), LOW),
                pltpu.VMEM((2, width, length), LOW),
                pltpu.VMEM((2, width, length), LOW),
                pltpu.VMEM((4, 2, width // 2, width), LOW),
                pltpu.SemaphoreType.DMA((2, 4)),
                pltpu.SemaphoreType.DMA((4,)),
                pltpu.SemaphoreType.DMA((14,)),
            ],
        ),
        out_shape,
        14e9,
        14 * length * width,
        vmem=58,
    )(where, own, *[a for r in received for a in r], nm, ga, g, *after)


def output_kernel(where_ref, *refs):
    (act_a, act_b, grad_a, grad_b, up_a, up_b, down_ref, mid_ref, cot_ref, seg_ref) = refs[:10]
    (keep_out, send_out, gmid_ref, gab_ref, sums_ref) = refs[-5:]
    step = pl.program_id(0)
    width, length = mid_ref.shape

    @pl.when(step == 0)
    def _():
        sums_ref[...] = jnp.zeros_like(sums_ref)

    on_attention = where_ref[0] == 0
    products = {}

    def multiply(tokens):
        out = grad = 0.0
        for group in range(4):
            act = (act_a, act_b)[group % 2][group // 2, :, tokens]
            slope_grad = (grad_a, grad_b)[group % 2][group // 2, :, tokens]
            out = out + dot(down_ref[group * width : (group + 1) * width, :], act, 0, 0)
            grad = grad + dot((up_a, up_b)[group % 2][group // 2], slope_grad)
        products[tokens] = out, grad

    def finish(tokens):
        out, grad = products.pop(tokens)
        middle = mid_ref[:, tokens]
        wide = widened(middle)
        output = (wide + compressed(out)).astype(LOW)
        lane = lax.broadcasted_iota(jnp.int32, sums_ref.shape, 1)
        sums_ref[...] += jnp.where(lane == 1, square_sum(output, seg_ref[0][:, tokens] > 0), 0.0)
        keep_out[:, tokens] = jnp.where(on_attention, middle, output)
        send_out[:, tokens] = jnp.where(on_attention, output, middle)
        normed, inverse = crms(wide)
        grad = (cot_ref[0, :, tokens].astype(FULL) + widened_back(crms_back(normed, inverse, grad))).astype(LOW)
        gmid_ref[:, tokens] = grad
        gab_ref[:, tokens] = compressed_back(grad).astype(LOW)

    in_stages(chunks(length, 2), (multiply, finish))


def output_of(where, acts, grads, ups, down_weight, middle, cot, segments, after=()):
    width, length = middle.shape
    steps = 2
    block = length // steps
    spec = tokens_spec(width, block)
    pair = pl.BlockSpec((2, width, block), lambda t, w: (0, 0, t))
    row = jax.ShapeDtypeStruct((width, length), LOW)
    return kernel_call(
        output_kernel,
        "output",
        pltpu.PrefetchScalarGridSpec(
            num_scalar_prefetch=1,
            grid=(steps,),
            in_specs=[pair] * 4
            + [pl.BlockSpec((2, width, width), lambda t, w: (0, 0, 0), pipeline_mode=pl.Buffered(1))] * 2
            + [pl.BlockSpec(down_weight.shape, lambda t, w: (0, 0), pipeline_mode=pl.Buffered(1))]
            + [spec, row_spec(width, block)]
            + [pl.BlockSpec((1, 1, block), lambda t, w: (w[0], 0, t))]
            + [pl.BlockSpec(memory_space=pltpu.HBM)] * len(after),
            out_specs=[spec] * 4 + [whole((8, 128))],
        ),
        [row] * 4 + [jax.ShapeDtypeStruct((8, 128), FULL)],
        20e9,
        24 * length * width,
        vmem=40,
    )(where, *acts, *grads, *ups, down_weight, middle, cot, segments, *after)


def mixed_grad_kernel(where_ref, gab_ref, w_ref, *refs):
    mixed_refs, gm_refs, (delta_ref, keep_ref, send_ref, mixed_all) = refs[:GROUPS], refs[-GROUPS - 4 : -4], refs[-4:]
    gab = gab_ref[...]
    part = gm_refs[0].shape[0]
    heads = part // HEAD_DIM
    for group in range(GROUPS):
        rows = slice(group * part, (group + 1) * part)
        grads = dot(w_ref[rows, :], gab).astype(LOW)
        gm_refs[group][...] = grads
        mixed = mixed_refs[group][...]
        mixed_all[rows, :] = mixed
        product = grads.astype(FULL) * mixed.astype(FULL)
        for head in range(heads):
            delta_ref[group, head : head + 1, :] = jnp.sum(
                product[head * HEAD_DIM : (head + 1) * HEAD_DIM], axis=0, keepdims=True
            )
    for place, rows in halves(where_ref, mixed_all.shape[0]):
        (keep_ref, send_ref)[place][...] = dot(mixed_all[rows, :], gab, 1, 1).astype(LOW)


def mixed_grad(where, gab, w, mixed, after=()):
    width, length = gab.shape
    part = width // GROUPS
    heads = part // HEAD_DIM
    outs = kernel_call(
        mixed_grad_kernel,
        "mixed_grad",
        pltpu.PrefetchScalarGridSpec(
            num_scalar_prefetch=1,
            grid=(1,),
            in_specs=[whole((width, length)), whole((width, width))]
            + [whole((part, length))] * GROUPS
            + [pl.BlockSpec(memory_space=pltpu.HBM)] * len(after),
            out_specs=[whole((part, length))] * GROUPS
            + [whole((GROUPS, heads, length))]
            + [whole((width // 2, width))] * 2,
            scratch_shapes=[pltpu.VMEM((width, length), LOW)],
        ),
        [jax.ShapeDtypeStruct((part, length), LOW)] * GROUPS
        + [jax.ShapeDtypeStruct((GROUPS, heads, length), FULL)]
        + [jax.ShapeDtypeStruct((width // 2, width), LOW)] * 2,
        4 * length * width * width,
        8 * length * width,
        vmem=28,
    )(where, gab, w, *mixed, *after)
    return outs[:GROUPS], outs[GROUPS], outs[GROUPS + 1], outs[GROUPS + 2]


def input_grad_kernel(where_ref, x_ref, gmid_ref, *refs):
    grad_refs, w_refs, (keep_ref, *send_refs) = refs[:GROUPS], refs[GROUPS : 2 * GROUPS], refs[-3:]
    on_attention = where_ref[0] == 0
    grad_normed = dot(w_refs[0][...], grad_refs[0][...])
    for group in range(1, GROUPS):
        grad_normed = grad_normed + dot(w_refs[group][...], grad_refs[group][...])
    normed, inverse = crms(widened(x_ref[0]))
    middle = gmid_ref[...]
    grad = (middle.astype(FULL) + widened_back(crms_back(normed, inverse, grad_normed))).astype(LOW)
    keep_ref[...] = jnp.where(on_attention, grad, middle)
    sent = jnp.where(on_attention, middle, grad)
    for part, send_ref in enumerate(send_refs):

        @pl.when((pl.program_id(0) > 0) == (part == 1))
        def _(send_ref=send_ref):
            send_ref[...] = sent


def input_grad(where, x, grad_middle, grads, weights, after=()):
    width, length = grad_middle.shape
    spec = tokens_spec(width, length // 4)
    return kernel_call(
        input_grad_kernel,
        "input_grad",
        pltpu.PrefetchScalarGridSpec(
            num_scalar_prefetch=1,
            grid=(4,),
            in_specs=[row_spec(width, length // 4), spec]
            + [spec] * GROUPS
            + [whole((width, width))] * GROUPS
            + [pl.BlockSpec(memory_space=pltpu.HBM)] * len(after),
            out_specs=[
                spec,
                pl.BlockSpec((width, length // 4), lambda t, w: (0, 0)),
                pl.BlockSpec((width, length // 4), lambda t, w: (0, jnp.maximum(t - 1, 0))),
            ],
        ),
        [jax.ShapeDtypeStruct((width, tokens), LOW) for tokens in (length, length // 4, length - length // 4)],
        6 * length * width * width,
        12 * length * width,
        vmem=30,
    )(where, x, grad_middle, *grads, *weights, *after)


def rows_kernel(where_ref, kept_ref, *refs):
    other_refs, out_ref = refs[:-1], refs[-1]
    kept = kept_ref[...].astype(FULL)
    other = other_refs[0][...].astype(FULL)
    if len(other_refs) > 1:
        other = jnp.where(pl.program_id(0) == 0, other, other_refs[1][...].astype(FULL))
    mine = where_ref[0] == 0
    out_ref[...] = jnp.stack([jnp.where(mine, kept, other), jnp.where(mine, other, kept)], axis=1).astype(LOW)


def rows_of(where, kept, others, after=()):
    width, length = kept.shape
    block = length // 4
    places = [lambda t, w: (0, t)] if len(others) == 1 else [lambda t, w: (0, 0), lambda t, w: (0, jnp.maximum(t - 1, 0))]

    def body(where_ref, *refs):
        rows_kernel(where_ref, *refs[: 1 + len(others)], refs[-1])

    out = kernel_call(
        body,
        "rows",
        pltpu.PrefetchScalarGridSpec(
            num_scalar_prefetch=1,
            grid=(4,),
            in_specs=[tokens_spec(width, block)]
            + [pl.BlockSpec((width, block), place) for place in places]
            + [pl.BlockSpec(memory_space=pltpu.HBM)] * len(after),
            out_specs=pl.BlockSpec((width, 2, block), lambda t, w: (0, 0, t)),
        ),
        pltpu.HBM((width - 1, 2, length), LOW),
        2e10,
        length,
        vmem=40,
    )(where, kept, *others, *after)
    return jnp.transpose(out, (1, 2, 0))[None]


def partner(block, distance):
    size = lax.axis_size("dp")
    return lax.ppermute(block, "dp", [(i, i ^ distance) for i in range(size)])


def across(block):
    return lax.ppermute(block, "section", [(0, 1), (1, 0)])


def split(left, right, distance):
    bit = (lax.axis_index("dp") & distance) // distance
    half = left.shape[1] // 2
    part = lambda a, at: lax.dynamic_slice_in_dim(a, at * half, half, 1)
    return add_low(part(left, bit), part(right, bit)), add_low(part(left, 1 - bit), part(right, 1 - bit))


def add_low(left, right):
    return (left.astype(FULL) + right.astype(FULL)).astype(LOW)


class Scatter:
    def __init__(self, keep, got, order):
        self.order = order
        self.keep, self.got = keep, got
        self.at = 0

    def step(self, *others):
        self.at += 1
        self.got = later(self.got, *others)
        self.keep, self.sent = split(self.keep, self.got, self.order[self.at])
        self.got = partner(self.sent, self.order[self.at])

    def total(self, *others):
        while self.at < len(self.order) - 1:
            self.step(*others)
        return add_low(self.keep, later(self.got, *others))


class Gather:
    def __init__(self, shard, order, *others):
        self.left = list(reversed(order))
        self.held = later(shard, *others)[None] if others else shard[None]
        self.got = partner(self.held, self.left.pop(0))

    def step(self, *others):
        self.held = jnp.concatenate([self.held, later(self.got, *others)], axis=0)
        self.got = partner(self.held, self.left.pop(0))

    def all(self, *others):
        while self.left:
            self.step(*others)
        return self.held, self.got


def number_of(order):
    me = lax.axis_index("dp").astype(jnp.int32)
    number = jnp.int32(0)
    for distance in order:
        number = number * 2 + (me // distance) % 2
    return number


def later(value, *others):
    return lax.optimization_barrier((value, *others))[0]


def gathered_specs(array, per_step):
    half_steps = array.shape[0] // per_step
    block = (per_step, *array.shape[1:])
    return [
        pl.BlockSpec(block, lambda e, w: (jnp.minimum(e, half_steps - 1), 0, 0)),
        pl.BlockSpec(block, lambda e, w: (jnp.maximum(e - half_steps, 0), 0, 0)),
    ]


def each_entry(number_ref, halves_refs, do):
    steps = pl.num_programs(0)
    per_step = halves_refs[0].shape[0]
    for place, ref in enumerate(halves_refs):

        @pl.when((pl.program_id(0) * 2 >= steps) == (place == 1))
        def _(ref=ref):
            for entry in range(per_step):
                do((number_ref[1] % per_step) ^ entry, ref, entry)


def down_sum_kernel(number_ref, near_ref, far_ref, out_ref):
    rows = out_ref.shape[2]

    def write(place, ref, entry):
        for block in range(2):
            out_ref[block, place] = ref[entry, block * rows : (block + 1) * rows, :].astype(FULL)

    each_entry(number_ref, (near_ref, far_ref), write)


def down_sum(number, near, far, width):
    entries = 2 * near.shape[0]
    rows = width // entries
    per_step = entries // 4
    out = kernel_call(
        down_sum_kernel,
        "down_sum",
        pltpu.PrefetchScalarGridSpec(
            num_scalar_prefetch=1,
            grid=(4,),
            in_specs=gathered_specs(near, per_step),
            out_specs=pl.BlockSpec((2, per_step, rows, width), lambda e, w: (0, (w[1] // per_step) ^ e, 0, 0)),
        ),
        jax.ShapeDtypeStruct((2, entries, rows, width), FULL),
        2e10,
        width,
        vmem=58,
    )(number, near, far)
    return out.reshape(2 * width, width)


def columns_of(numbers):
    if numbers[0] < 0:
        return [[(0, 3 * block, 3)] for block in (-numbers[0] - 1, -numbers[1] - 1)]
    return [
        [(0, 9, 3)] if block == 0 else [(piece, own_column_static(block - 1, piece, 0), 1) for piece in range(3)]
        for block in numbers
    ]


def counts_of(section, slots, width, near_ref, far_ref):
    rows = sum(ref[entry, :16, :128].astype(FULL) for ref in (near_ref, far_ref) for entry in range(ref.shape[0]))
    lane = lax.broadcasted_iota(jnp.int32, (1, 128), 1)
    total = [
        jnp.sum(jnp.where((lane % 3 == which) & (lane < 9), rows[:1], 0.0), axis=1, keepdims=True) for which in range(3)
    ]
    square = jnp.where(section == 0, total[0], total[1])
    count = jnp.where(section == 0, total[2], slots - total[2])
    root = jnp.sqrt(square / (total[2] * width))
    return jnp.broadcast_to(jnp.where(lane == 0, root, jnp.where(lane == 1, count, 0.0)), (8, 128))


def first_sum_kernel(skip, blocks, slots, number_ref, near_ref, far_ref, *refs):
    buffer, sem = refs[-2:]
    out_ref = refs[-4] if slots else refs[-3]
    entries, rows, columns = out_ref.shape
    width = columns // 4
    part = width // 3
    half = entries // 2
    if slots:
        refs[-3][...] = counts_of(number_ref[0], slots, width, near_ref, far_ref)
    for section in range(2):

        @pl.when(number_ref[0] == section)
        def _(section=section):
            pieces = columns_of(blocks[section])

            def copies(place, do):
                first = pl.multiple_of(jnp.where(number_ref[1] < half, place, 1 - place) * half, half)
                for at in range(2):
                    for order, (start, column, size) in enumerate(pieces[at]):
                        do(
                            pltpu.make_async_copy(
                                buffer.at[at, pl.ds(first, half), :, pl.ds(start * part, size * part)],
                                out_ref.at[pl.ds(first, half), :, pl.ds(column * part, size * part)],
                                sem.at[place, at, order],
                            )
                        )

            for place, ref in enumerate((near_ref, far_ref)):
                for entry in range(half):
                    for at in range(2):
                        values = ref[entry, skip + at * rows : skip + (at + 1) * rows, :]
                        buffer[at, number_ref[1] ^ (entry + place * half)] = values.astype(FULL)
                copies(place, lambda c: c.start())
            for place in range(2):
                copies(place, lambda c: c.wait())


def first_sum(number, skip, blocks, gathered, width, before=None, slots=None):
    near, far = gathered
    entries = 2 * near.shape[0]
    rows = width // entries
    held = [] if before is None else [before]
    anywhere = pl.BlockSpec(memory_space=pl.ANY)
    return pl.pallas_call(
        functools.partial(first_sum_kernel, skip, blocks, slots),
        grid_spec=pltpu.PrefetchScalarGridSpec(
            num_scalar_prefetch=1,
            grid=(1,),
            in_specs=[whole(near.shape), whole(far.shape)] + [anywhere] * len(held),
            out_specs=[anywhere] + [whole((8, 128))] * bool(slots),
            scratch_shapes=[pltpu.VMEM((2, entries, rows, width), FULL), pltpu.SemaphoreType.DMA((2, 2, 3))],
        ),
        out_shape=[jax.ShapeDtypeStruct((entries, rows, 4 * width), FULL)]
        + [jax.ShapeDtypeStruct((8, 128), FULL)] * bool(slots),
        input_output_aliases={3: 0} if held else {},
        compiler_params=pltpu.CompilerParams(vmem_limit_bytes=24 * 2**20),
        cost_estimate=pl.CostEstimate(flops=1000, bytes_accessed=1000, transcendentals=0),
        name="first_sum",
    )(number, near, far, *held)


def on_device(stream_in, cotangent, weights_first, down_weight, segments):
    rows_dev, length, compact_width = stream_in.shape
    width = compact_width + 1
    section = lax.axis_index("section").astype(jnp.int32)
    index = lax.axis_index("dp").astype(jnp.int32)
    size = lax.axis_size("dp")
    on_attention = section == 0
    where = jnp.stack([section, index & 3, index & 1])
    segments3 = segments.reshape(rows_dev, 1, length)
    order = [1 << i for i in range(size.bit_length() - 1)]
    flat = lambda a: a.reshape(-1, width)

    near = [across(piece) for piece in weight_piece(where, weights_first)]
    x, cot = jnp.transpose(stream_in, (0, 2, 1)), jnp.transpose(cotangent, (0, 2, 1))
    nt, g = prep(where, x, cot)
    ga = branch_grad(g, down_weight, after=(near[0],))
    attended, received, besides = [], [], [partner(later(near[0], nt), 2), partner(later(near[1], ga), 2)]
    for group in range(4):
        quarter, beside = near[group], besides[group]
        done = [attended[group - 1][1] if group else ga]
        received.append((quarter, beside, partner(quarter, 1), partner(later(beside, *done), 1)))
        if group < 2:
            besides.append(partner(later(near[group + 2], *done), 2))
        if group < GROUPS:
            attended.append(attend(group, where, weights_first, received[group], nt, segments3))
    mixed = [a[1] for a in attended]
    middle, nm, sums_mid, out_weights = middle_of(where, weights_first, received[GROUPS], mixed, x, segments3)

    act_a, grad_a, weights_a, keep_a, send_a, *down_a = hidden_of(0, where, weights_first, received[0::2], nm, ga, g)
    up_a, got_a = partner(send_a, 1), partner(down_a[1], 1)
    act_b, grad_b, weights_b, keep_b, send_b, *down_b = hidden_of(
        1, where, weights_first, received[1::2], nm, ga, g, after=(act_a,)
    )
    up_b, got_b = partner(send_b, 1), partner(down_b[1], 1)
    halves_a, halves_b = split(keep_a, up_a, order[1]), split(keep_b, up_b, order[1])
    up = Scatter(keep_a, up_a, order)
    up.keep, up.sent = (jnp.concatenate(both) for both in zip(halves_a, halves_b, strict=True))
    up.at, up.got = 1, partner(up.sent, order[1])
    kept, sent = [], []
    for keep, got in ((down_a[0], got_a), (down_b[0], got_b)):
        lower, upper = add_low(keep[0], got[0]), add_low(keep[1], got[1])
        kept.append(jnp.where(on_attention, lower, upper))
        sent.append(jnp.where(on_attention, upper, lower))
    kept, sent = jnp.stack(kept), later(jnp.stack(sent), up.sent)
    down = Scatter(kept, across(sent), order)
    keep_out, send_out, grad_mid, gab, sums_out = output_of(
        where, (act_a, act_b), (grad_a, grad_b), (weights_a, weights_b), down_weight, middle, cot, segments3, after=(sent,)
    )
    up.step(gab)
    gm, delta, keep_w, send_w = mixed_grad(where, gab, out_weights, mixed, after=(up.sent,))
    keeps, sends, grads = [keep_w], [send_w], []

    def backward(group, *after):
        qkv, _, total, _ = attended[group]
        keep_w, send_w, grad = attend_back(where, qkv, gm[group], total, delta[group], segments3, nt, after=after)
        keeps.append(keep_w)
        sends.append(send_w)
        grads.append(grad)

    down.step(delta)
    backward(0, down.sent)
    up.step(grads[0])
    down.step(up.sent)
    sent_a = later(jnp.stack(sends), down.sent)
    attn_a = Scatter(jnp.stack(keeps), partner(sent_a, 1), order)
    backward(1, sent_a)
    attn_a.step(grads[1])
    down.step(attn_a.sent)
    received_out = across(send_out)
    backward(2, down.sent)
    down = down.total(grads[2])
    sum_dn = Gather(flat(down), order)
    up = up.total(sum_dn.held)
    up_a, up_b, rows = up[:2], up[2:], up.shape[1]
    attn_a.step(up)
    attn_b = Scatter(jnp.stack(keeps[2:]), partner(later(jnp.stack(sends[2:]), attn_a.sent), 1), order)
    attn_b.step()
    keep_grad, *send_grad = input_grad(
        where, x, grad_mid, grads, [a[3] for a in attended], after=(attn_b.sent, received_out)
    )
    attn_a.step(keep_grad)
    attn_b.step(attn_a.sent)
    sum_dn.step(attn_b.sent)
    attn_a = attn_a.total(sum_dn.held)

    scalars = (sums_mid + sums_out)[0, :3]

    def scalar_rows(values):
        high = values.astype(LOW)
        rest = values - high.astype(FULL)
        middle_part = rest.astype(LOW)
        low = (rest - middle_part.astype(FULL)).astype(LOW)
        packed = jnp.concatenate([high, middle_part, low])
        return jnp.zeros((16, width), LOW).at[0, :9].set(packed)

    def scalars_of(block):
        parts = block[..., 0, :9].astype(FULL)
        return parts[..., :3] + parts[..., 3:6] + parts[..., 6:9]

    mine_a, theirs_a = jnp.where(on_attention, attn_a, up_a), jnp.where(on_attention, up_a, attn_a)
    sent_a = jnp.concatenate([scalar_rows(scalars), flat(theirs_a)])
    swapped = across(sent_a)
    attn_b.step(sent_a)
    swapped = later(swapped, attn_b.sent)
    pair = scalars + scalars_of(swapped[:16])
    shard_a = add_low(flat(mine_a), swapped[16:])
    sum_a = Gather(jnp.concatenate([scalar_rows(pair), shard_a]), order)
    received_grad = [across(later(send_grad[0], sum_a.held))]
    sum_dn.step(sum_a.held)
    received_grad[0] = later(received_grad[0], sum_dn.held)
    attn_b = attn_b.total(received_grad[0])
    mine_b, theirs_b = jnp.where(on_attention, attn_b, up_b), jnp.where(on_attention, up_b, attn_b)
    swapped_b = across(flat(theirs_b))
    received_grad.append(across(later(send_grad[1], theirs_b)))
    sum_a.step(theirs_b)
    stream_out = rows_of(where, keep_out, [received_out], after=(sum_a.held,))
    sum_b = Gather(add_low(flat(mine_b), later(swapped_b, stream_out)), order)
    sum_a.step(sum_b.held)
    sum_dn.step(sum_a.held)
    number = jnp.stack([section, number_of(order)])
    grad_down = down_sum(later(number, sum_dn.held), *sum_dn.all(), width)
    sum_b.step(grad_down)
    sum_b.step(sum_a.got)
    sum_a.step(sum_b.held)
    stream_grad = rows_of(where, keep_grad, received_grad, after=(sum_a.held,))
    sum_b.step(stream_grad)
    sum_a, sum_b = sum_a.all(), sum_b.all()
    slots = float(rows_dev * length * size)
    grad_first, counts = first_sum(later(number, sum_b[0]), 16, ((0, 1), (-1, -3)), sum_a, width, slots=slots)
    (grad_first,) = first_sum(number, 0, ((2, 3), (-2, -4)), sum_b, width, before=grad_first)
    grad_first = grad_first.reshape(width, 4 * width)
    residual_rms, token_count = counts[0, :1], counts[0, 1:2].astype(jnp.int32)
    return (
        stream_out,
        stream_grad,
        grad_first[None],
        grad_down,
        residual_rms,
        token_count,
    )


def solution(mesh):
    placed = (
        P("dp", None, None),
        P("dp", None, None),
        P("section", None, None),
        P(),
        P("dp", None),
    )
    return jax.shard_map(
        on_device,
        mesh=mesh,
        in_specs=placed,
        out_specs=(
            P("section", "dp", None, None),
            P("section", "dp", None, None),
            P("section", None, None),
            P("section", None),
            P("section"),
            P("section"),
        ),
        check_vma=False,
    )
```

```python
import functools

import jax
import jax.numpy as jnp
from jax import lax
from jax.experimental import pallas as pl
from jax.experimental.pallas import tpu as pltpu
from jax.sharding import PartitionSpec as P

HEADS = 12
HEAD_DIM = 64
GROUPS = 3
EPSILON = 1e-06
MASKED = -1e30
SCALE = HEAD_DIM ** (-0.5)
LOG2E = 1.4426950408889634
LOW = jnp.bfloat16
FULL = jnp.float32


def dot(left, right, left_dim=1, right_dim=0):
    return lax.dot_general(
        left, right, (((left_dim,), (right_dim,)), ((), ())), preferred_element_type=FULL
    )


def kernel_call(body, name, grid_spec, out_shape, flops, moved, vmem=32):
    return pl.pallas_call(
        body,
        grid_spec=grid_spec,
        out_shape=out_shape,
        compiler_params=pltpu.CompilerParams(vmem_limit_bytes=vmem * 2**20),
        cost_estimate=pl.CostEstimate(flops=int(flops * 1.5), bytes_accessed=int(moved * 1.5), transcendentals=0),
        name=name,
    )


def last_row(block):
    return lax.broadcasted_iota(jnp.int32, block.shape, 0) == block.shape[0] - 1


def widened(block):
    values = jnp.where(last_row(block), 0.0, block.astype(FULL))
    return jnp.where(last_row(block), -jnp.sum(values, axis=0, keepdims=True), values)


def crms(values):
    inverse = lax.rsqrt(jnp.mean(values * values, axis=0, keepdims=True) + EPSILON)
    return values * inverse, inverse


def crms_back(normed, inverse, grad):
    return inverse * (grad - normed * jnp.mean(grad * normed, axis=0, keepdims=True))


def compressed(branch):
    return branch - jnp.mean(branch, axis=0, keepdims=True)


def widened_back(grad):
    return grad - grad[grad.shape[0] - 1 :]


def compressed_back(block):
    values = jnp.where(last_row(block), 0.0, block.astype(FULL))
    return values - jnp.mean(values, axis=0, keepdims=True)


def square_sum(rounded, valid):
    wide = widened(rounded)
    per_token = jnp.sum(wide * wide, axis=0, keepdims=True)
    return jnp.sum(jnp.where(valid, per_token, 0.0), axis=1, keepdims=True)


def prep_kernel(where_ref, x_ref, cot_ref, nt_ref, g_ref):
    normed, _ = crms(widened(x_ref[0]))
    nt_ref[...] = normed.astype(LOW)
    g_ref[...] = compressed_back(cot_ref[0]).astype(LOW)


def tokens_spec(width, block):
    return pl.BlockSpec((width, block), lambda t, *_: (0, t))


def row_spec(width, block):
    return pl.BlockSpec((1, width, block), lambda t, w: (w[0], 0, t))


def prep(where, x, cot):
    width, length = x.shape[1] + 1, x.shape[2]
    spec = tokens_spec(width, length // 4)
    return kernel_call(
        prep_kernel,
        "prep",
        pltpu.PrefetchScalarGridSpec(
            num_scalar_prefetch=1, grid=(4,), in_specs=[row_spec(width, length // 4)] * 2, out_specs=[spec] * 2
        ),
        [jax.ShapeDtypeStruct((width, length), LOW)] * 2,
        0,
        8 * length * width,
        vmem=16,
    )(where, x, cot)


def branch_grad_kernel(g_ref, w_ref, *refs):
    out_ref = refs[-1]
    out_ref[0] = dot(w_ref[...], g_ref[...]).astype(LOW)


def branch_grad(g, down_weight, after=()):
    width, length = g.shape
    blocks = down_weight.shape[0] // width
    return kernel_call(
        branch_grad_kernel,
        "branch_grad",
        pltpu.PrefetchScalarGridSpec(
            num_scalar_prefetch=0,
            grid=(blocks,),
            in_specs=[
                pl.BlockSpec((width, length), lambda b: (0, 0)),
                pl.BlockSpec((width, width), lambda b: (b, 0)),
            ]
            + [pl.BlockSpec(memory_space=pltpu.HBM)] * len(after),
            out_specs=pl.BlockSpec((1, width, length), lambda b: (b, 0, 0)),
        ),
        pltpu.HBM((blocks, width, length), LOW),
        2 * length * width * width * blocks,
        2 * length * width * (blocks + 1),
        vmem=20,
    )(g, down_weight, *after)


def own_column_static(group, piece, section):
    if section == 1 or group == GROUPS:
        return 3 * group + piece
    return group + GROUPS * piece


def piece_kernel(where_ref, w_ref, *out_refs):
    part = out_refs[0].shape[1] // 3
    for section in range(2):

        @pl.when(where_ref[0] == section)
        def _(section=section):
            for group in range(4):
                for piece in range(3):
                    column = own_column_static(group, piece, section) * part
                    out_refs[group][:, piece * part : (piece + 1) * part] = w_ref[0, :, column : column + part]


def weight_piece(where, weights):
    rows, columns = weights.shape[1:]
    shape = (rows // 4, columns // 4)
    return kernel_call(
        piece_kernel,
        "weight_piece",
        pltpu.PrefetchScalarGridSpec(
            num_scalar_prefetch=1,
            grid=(1,),
            in_specs=[pl.BlockSpec((1, rows // 4, columns), lambda i, w: (0, w[1], 0))],
            out_specs=[whole(shape)] * 4,
        ),
        [jax.ShapeDtypeStruct(shape, LOW)] * 4,
        0,
        rows * columns,
        vmem=58,
    )(where, weights)


def weight_copies(group, wanted, where_ref, own_ref, quarters, target, sem, act):
    quarter = target.shape[0] // 4
    part = target.shape[1] // 3

    @pl.when(where_ref[0] == wanted)
    def _():
        for piece in range(3):
            column = own_column_static(group, piece, wanted) * part
            act(pltpu.make_async_copy(own_ref.at[0, :, pl.ds(column, part)], target.at[:, pl.ds(piece * part, part)], sem.at[piece]))

    @pl.when(where_ref[0] != wanted)
    def _():
        for place, source in enumerate(quarters):
            index = where_ref[1] ^ (0, 2, 1, 3)[place]
            act(pltpu.make_async_copy(source, target.at[pl.ds(index * quarter, quarter), :], sem.at[place]))


def segment_rows(segment):
    tokens = segment.shape[1]
    ids = lax.broadcasted_iota(jnp.int32, (16, tokens), 0)
    same = segment == ids
    real = ids < 5
    queries = jnp.where(real & jnp.logical_not(same), MASKED, 0.0).astype(LOW)
    keys = jnp.where(real & same, 1.0, 0.0).astype(LOW)
    return queries, keys


def two_parts(values):
    high = values.astype(LOW)
    return high, (values - high.astype(FULL)).astype(LOW)


def minus_rows(values):
    high = values.astype(LOW)
    rest = values - high.astype(FULL)
    middle = rest.astype(LOW)
    low = rest - middle.astype(FULL)
    row = lax.broadcasted_iota(jnp.int32, (16, values.shape[1]), 0)
    parts = jnp.where(
        row == 0, high.astype(FULL), jnp.where(row == 1, middle.astype(FULL), jnp.where(row == 2, low, 0.0))
    )
    return (-parts).astype(LOW)


def three_ones(tokens):
    return jnp.where(lax.broadcasted_iota(jnp.int32, (16, tokens), 0) < 3, 1.0, 0.0).astype(LOW)


def head_tasks(heads, blocks, block):
    return [
        (head, slice(i * block, (i + 1) * block), slice(0, (i + 1) * block), i * block)
        for head in range(heads)
        for i in range(blocks)
    ]


def in_stages(tasks, stages):
    for step in range(len(tasks) + len(stages) - 1):
        for late, stage in enumerate(stages):
            if 0 <= step - late < len(tasks):
                stage(tasks[step - late])


def attend_kernel(group, where_ref, own_ref, near_ref, beside_ref, core_ref, across_ref, nt_ref, seg_ref, qkv_ref, mixed_ref, total_ref, w_ref, sem):
    copies = functools.partial(
        weight_copies, group, 0, where_ref, own_ref, (near_ref, beside_ref, core_ref, across_ref), w_ref, sem
    )
    copies(lambda c: c.start())
    copies(lambda c: c.wait())
    length = nt_ref.shape[1]
    width = qkv_ref.shape[0] // 3
    heads, blocks = width // HEAD_DIM, 4
    block = length // blocks
    for part in range(3):
        qkv_ref[part * width : (part + 1) * width, :] = dot(
            w_ref[:, part * width : (part + 1) * width], nt_ref[...], 0, 0
        ).astype(LOW)
    seg_queries, seg_keys = segment_rows(seg_ref[0])
    causal = lax.broadcasted_iota(jnp.int32, (block, block), 0) <= lax.broadcasted_iota(jnp.int32, (block, block), 1)
    ones = three_ones(length)
    scored, weighed = {}, {}

    def score(task):
        head, queries, keys, _ = task
        high, low = two_parts(qkv_ref[head * HEAD_DIM : (head + 1) * HEAD_DIM, queries].astype(FULL) * (SCALE * LOG2E))
        key_rows = qkv_ref[width + head * HEAD_DIM : width + (head + 1) * HEAD_DIM, keys]
        scored[task] = dot(
            jnp.concatenate([key_rows, key_rows, seg_keys[:, keys]], axis=0),
            jnp.concatenate([high, low, seg_queries[:, queries]], axis=0),
            0,
            0,
        )

    def weigh(task):
        before = task[3]
        scores = scored.pop(task)
        last = jnp.where(causal, scores[before:], MASKED)
        highest = jnp.max(last, axis=0, keepdims=True)
        if before:
            highest = jnp.maximum(highest, jnp.max(scores[:before], axis=0, keepdims=True))
        exponents = jnp.exp2(last - highest).astype(LOW)
        if before:
            exponents = jnp.concatenate([jnp.exp2(scores[:before] - highest).astype(LOW), exponents], axis=0)
        weighed[task] = (exponents, highest)

    def mix(task):
        head, queries, keys, _ = task
        exponents, highest = weighed.pop(task)
        values = qkv_ref[2 * width + head * HEAD_DIM : 2 * width + (head + 1) * HEAD_DIM, keys]
        mixed = dot(jnp.concatenate([values, ones[:, keys]], axis=0), exponents)
        total = mixed[HEAD_DIM : HEAD_DIM + 1]
        mixed_ref[head * HEAD_DIM : (head + 1) * HEAD_DIM, queries] = (mixed[:HEAD_DIM] / total).astype(LOW)
        total_ref[head : head + 1, queries] = highest + jnp.log2(total)

    in_stages(head_tasks(heads, blocks, block), (score, weigh, mix))


def attend(group, where, own, received, nt, segments):
    width, length = nt.shape
    part = width // GROUPS
    anywhere = pl.BlockSpec(memory_space=pltpu.HBM)
    return kernel_call(
        functools.partial(attend_kernel, group),
        "attend",
        pltpu.PrefetchScalarGridSpec(
            num_scalar_prefetch=1,
            grid=(1,),
            in_specs=[anywhere] * 5
            + [
                pl.BlockSpec((width, length), lambda i, w: (0, 0)),
                pl.BlockSpec((1, 1, length), lambda i, w: (w[0], 0, 0)),
            ],
            out_specs=[
                pl.BlockSpec((3 * part, length), lambda i, w: (0, 0)),
                pl.BlockSpec((part, length), lambda i, w: (0, 0)),
                pl.BlockSpec((part // HEAD_DIM, length), lambda i, w: (0, 0)),
                pl.BlockSpec((width, 3 * part), lambda i, w: (0, 0)),
            ],
            scratch_shapes=[pltpu.SemaphoreType.DMA((4,))],
        ),
        [
            pltpu.HBM((3 * part, length), LOW),
            jax.ShapeDtypeStruct((part, length), LOW),
            pltpu.HBM((part // HEAD_DIM, length), FULL),
            pltpu.HBM((width, 3 * part), LOW),
        ],
        4.5e9,
        8 * width * length,
        vmem=24,
    )(where, own, *received, nt, segments)


def attend_back_kernel(where_ref, qkv_ref, gm_ref, total_ref, delta_ref, seg_ref, nt_ref, *rest):
    keep_ref, send_ref, grads_ref, acc = rest[-4:]
    length = nt_ref.shape[1]
    width = gm_ref.shape[0]
    heads, blocks = width // HEAD_DIM, 4
    block = length // blocks
    seg_queries, seg_keys = segment_rows(seg_ref[0])
    ones = three_ones(length)
    causal = lax.broadcasted_iota(jnp.int32, (block, block), 1) <= lax.broadcasted_iota(jnp.int32, (block, block), 0)
    acc[...] = jnp.zeros_like(acc)
    scored, weighed = {}, {}

    def rows(part, head):
        return slice(part * width + head * HEAD_DIM, part * width + (head + 1) * HEAD_DIM)

    def score(task):
        head, queries, keys, _ = task
        high, low = two_parts(qkv_ref[rows(0, head), queries].astype(FULL) * (SCALE * LOG2E))
        key_rows = qkv_ref[rows(1, head), keys]
        scores = dot(
            jnp.concatenate([high, low, seg_queries[:, queries], minus_rows(total_ref[head : head + 1, queries])], axis=0),
            jnp.concatenate([key_rows, key_rows, seg_keys[:, keys], ones[:, keys]], axis=0),
            0,
            0,
        )
        grads = dot(
            jnp.concatenate([gm_ref[rows(0, head), queries], minus_rows(delta_ref[head : head + 1, queries])], axis=0),
            jnp.concatenate([qkv_ref[rows(2, head), keys], ones[:, keys]], axis=0),
            0,
            0,
        )
        scored[task] = (scores, grads)

    def weigh(task):
        before = task[3]
        scores, grads = scored.pop(task)
        last = jnp.where(causal, scores[:, before:], MASKED)
        if before:
            last = jnp.concatenate([scores[:, :before], last], axis=1)
        probs = jnp.exp2(last)
        weighed[task] = (probs.astype(LOW), (probs * grads).astype(LOW))

    def collect(task):
        head, queries, keys, _ = task
        probs, grads = weighed.pop(task)
        acc[rows(2, head), keys] += dot(gm_ref[rows(0, head), queries], probs)
        acc[rows(1, head), keys] += dot(qkv_ref[rows(0, head), queries] * LOW(SCALE), grads)
        acc[rows(0, head), queries] = dot(qkv_ref[rows(1, head), keys], grads, 1, 1) * SCALE

    in_stages(head_tasks(heads, blocks, block), (score, weigh, collect))
    grads_ref[...] = acc[...].astype(LOW)
    for place, rows_ in halves(where_ref, nt_ref.shape[0]):
        (keep_ref, send_ref)[place][...] = dot(nt_ref[rows_, :], grads_ref[...], 1, 1).astype(LOW)


def halves(where_ref, count):
    half = count // 2
    return [
        (0, pl.ds(pl.multiple_of(where_ref[2] * half, half), half)),
        (1, pl.ds(pl.multiple_of((1 - where_ref[2]) * half, half), half)),
    ]


def whole(shape):
    return pl.BlockSpec(shape, lambda *_: (0,) * len(shape))


def attend_back(where, qkv, gm, total, delta, segments, nt, after=()):
    width, length = nt.shape
    part = gm.shape[0]
    arrays = [qkv, gm, total, delta]
    return kernel_call(
        attend_back_kernel,
        "attend_back",
        pltpu.PrefetchScalarGridSpec(
            num_scalar_prefetch=1,
            grid=(1,),
            in_specs=[whole(a.shape) for a in arrays]
            + [pl.BlockSpec((1, 1, length), lambda i, w: (w[0], 0, 0)), whole(nt.shape)]
            + [pl.BlockSpec(memory_space=pltpu.HBM)] * len(after),
            out_specs=[whole((width // 2, 3 * part))] * 2 + [whole((3 * part, length))],
            scratch_shapes=[pltpu.VMEM((3 * part, length), FULL)],
        ),
        [jax.ShapeDtypeStruct((width // 2, 3 * part), LOW)] * 2 + [pltpu.HBM((3 * part, length), LOW)],
        9e9,
        8 * width * length,
        vmem=28,
    )(where, *arrays, segments, nt, *after)


def middle_kernel(where_ref, own_ref, near_ref, beside_ref, core_ref, across_ref, *refs):
    mixed_refs, (x_ref, seg_ref, mid_ref, nm_ref, sums_ref, w_ref, sem) = refs[:GROUPS], refs[GROUPS:]
    step = pl.program_id(0)

    @pl.when(step == 0)
    def _():
        copies = functools.partial(
            weight_copies, GROUPS, 0, where_ref, own_ref, (near_ref, beside_ref, core_ref, across_ref), w_ref, sem
        )
        copies(lambda c: c.start())
        copies(lambda c: c.wait())
        sums_ref[...] = jnp.zeros_like(sums_ref)

    mixed = jnp.concatenate([ref[...] for ref in mixed_refs], axis=0)
    branch = dot(w_ref[...], mixed, 0, 0)
    middle = (x_ref[0].astype(FULL) + compressed(branch)).astype(LOW)
    mid_ref[...] = middle
    normed, _ = crms(widened(middle))
    nm_ref[...] = normed.astype(LOW)
    valid = seg_ref[0] > 0
    lane = lax.broadcasted_iota(jnp.int32, sums_ref.shape, 1)
    count = jnp.sum(valid.astype(FULL), axis=1, keepdims=True)
    sums_ref[...] += jnp.where(lane == 0, square_sum(middle, valid), 0.0) + jnp.where(lane == 2, count, 0.0)


def middle_of(where, own, received, mixed, x, segments):
    width, length = x.shape[1] + 1, x.shape[2]
    block = length // 4
    anywhere = pl.BlockSpec(memory_space=pltpu.HBM)
    spec = tokens_spec(width, block)
    return kernel_call(
        middle_kernel,
        "middle",
        pltpu.PrefetchScalarGridSpec(
            num_scalar_prefetch=1,
            grid=(4,),
            in_specs=[anywhere] * 5
            + [tokens_spec(width // GROUPS, block)] * GROUPS
            + [row_spec(width, block), pl.BlockSpec((1, 1, block), lambda t, w: (w[0], 0, t))],
            out_specs=[spec, spec, whole((8, 128)), whole((width, width))],
            scratch_shapes=[pltpu.SemaphoreType.DMA((4,))],
        ),
        [pltpu.HBM((width, length), LOW)] * 2
        + [jax.ShapeDtypeStruct((8, 128), FULL), pltpu.HBM((width, width), LOW)],
        2 * length * width * width,
        12 * length * width,
        vmem=20,
    )(where, own, *received, *mixed, x, segments)


def gelu_both(hidden):
    rate = 0.7978845608028654
    square = hidden * hidden
    half = 0.5 + 0.5 * jnp.tanh(hidden * (rate + (rate * 0.044715) * square))
    slope = half + hidden * (2.0 * rate + (6.0 * rate * 0.044715) * square) * (half - half * half)
    return hidden * half, slope


def chunks(length, count):
    return [slice(i * (length // count), (i + 1) * (length // count)) for i in range(count)]


def hidden_kernel(first, where_ref, own_ref, *refs):
    received, refs = refs[:8], refs[8:]
    (nm_hbm, ga_hbm, g_hbm) = refs[:3]
    (act_hbm, grad_hbm, w_hbm, *sums_hbm) = refs[-17:-10]
    (weights, nm_ref, g_ref, ga_ref, act_ref, grad_ref, sums_ref, w_sem, in_sem, out_sem) = refs[-10:]
    length = nm_ref.shape[1]

    def copies(place, do):
        weight_copies(
            first + 2 * place, 1, where_ref, own_ref, received[4 * place : 4 * place + 4], weights.at[place], w_sem.at[place], do
        )

    nm_copy = pltpu.make_async_copy(nm_hbm, nm_ref, in_sem.at[0])
    g_copy = pltpu.make_async_copy(g_hbm, g_ref, in_sem.at[1])
    ga_copies = [pltpu.make_async_copy(ga_hbm.at[first + 2 * i], ga_ref.at[i], in_sem.at[2 + i]) for i in range(2)]
    nm_copy.start()
    copies(0, lambda c: c.start())
    ga_copies[0].start()
    g_copy.start()
    copies(1, lambda c: c.start())
    ga_copies[1].start()
    hidden, sent = {}, []

    def send(source, target):
        copy = pltpu.make_async_copy(source, target, out_sem.at[len(sent)])
        copy.start()
        sent.append(copy)

    def enter(task):
        place, tokens = task
        hidden[task] = dot(weights[place], nm_ref[:, tokens], 0, 0)

    def bend(task):
        place, tokens = task
        value, slope = gelu_both(hidden.pop(task))
        act_ref[place, :, tokens] = value.astype(LOW)
        grad_ref[place, :, tokens] = (ga_ref[place, :, tokens].astype(FULL) * slope).astype(LOW)

    def down(place, which):
        rows = halves(where_ref, nm_ref.shape[0])[which][1]
        sums_ref[2 + which, place] = dot(act_ref[place, rows, :], g_ref[...], 1, 1).astype(LOW)
        send(sums_ref.at[2 + which, place], sums_hbm[2 + which].at[place])

    def up(place, which):
        rows = halves(where_ref, nm_ref.shape[0])[which][1]
        sums_ref[which, place] = dot(nm_ref[rows, :], grad_ref[place], 1, 1).astype(LOW)
        send(sums_ref.at[which, place], sums_hbm[which].at[place])

    def finished(place):
        send(weights.at[place], w_hbm.at[place])
        send(act_ref.at[place], act_hbm.at[place])
        send(grad_ref.at[place], grad_hbm.at[place])

    def tasks(place):
        return [(place, tokens) for tokens in chunks(length, 4)]

    nm_copy.wait()
    copies(0, lambda c: c.wait())
    ga_copies[0].wait()
    in_stages(tasks(0), (enter, bend))
    g_copy.wait()
    copies(1, lambda c: c.wait())
    ga_copies[1].wait()
    finished(0)
    between = [(down, 1), (down, 0), (up, 1), (up, 0)]
    last = None
    for task, (product, which) in zip(tasks(1), between, strict=True):
        enter(task)
        if last is not None:
            bend(last)
        product(0, which)
        last = task
    bend(last)
    finished(1)
    for product, which in between:
        product(1, which)
    for copy in sent:
        copy.wait()


def hidden_of(first, where, own, received, nm, ga, g, after=()):
    width, length = nm.shape
    anywhere = pl.BlockSpec(memory_space=pltpu.HBM)
    out_shape = (
        [pltpu.HBM((2, width, length), LOW)] * 2
        + [pltpu.HBM((2, width, width), LOW)]
        + [pltpu.HBM((2, width // 2, width), LOW)] * 4
    )
    return kernel_call(
        functools.partial(hidden_kernel, first),
        "hidden",
        pltpu.PrefetchScalarGridSpec(
            num_scalar_prefetch=1,
            grid=(1,),
            in_specs=[anywhere] * (12 + len(after)),
            out_specs=[anywhere] * 7,
            scratch_shapes=[
                pltpu.VMEM((2, width, width), LOW),
                pltpu.VMEM((width, length), LOW),
                pltpu.VMEM((width, length), LOW),
                pltpu.VMEM((2, width, length), LOW),
                pltpu.VMEM((2, width, length), LOW),
                pltpu.VMEM((2, width, length), LOW),
                pltpu.VMEM((4, 2, width // 2, width), LOW),
                pltpu.SemaphoreType.DMA((2, 4)),
                pltpu.SemaphoreType.DMA((4,)),
                pltpu.SemaphoreType.DMA((14,)),
            ],
        ),
        out_shape,
        14e9,
        14 * length * width,
        vmem=58,
    )(where, own, *[a for r in received for a in r], nm, ga, g, *after)


def output_kernel(where_ref, *refs):
    (act_a, act_b, grad_a, grad_b, up_a, up_b, down_ref, mid_ref, cot_ref, seg_ref) = refs[:10]
    (keep_out, send_out, gmid_ref, gab_ref, sums_ref) = refs[-5:]
    step = pl.program_id(0)
    width, length = mid_ref.shape

    @pl.when(step == 0)
    def _():
        sums_ref[...] = jnp.zeros_like(sums_ref)

    on_attention = where_ref[0] == 0
    products = {}

    def multiply(tokens):
        out = grad = 0.0
        for group in range(4):
            act = (act_a, act_b)[group % 2][group // 2, :, tokens]
            slope_grad = (grad_a, grad_b)[group % 2][group // 2, :, tokens]
            out = out + dot(down_ref[group * width : (group + 1) * width, :], act, 0, 0)
            grad = grad + dot((up_a, up_b)[group % 2][group // 2], slope_grad)
        products[tokens] = out, grad

    def finish(tokens):
        out, grad = products.pop(tokens)
        middle = mid_ref[:, tokens]
        wide = widened(middle)
        output = (wide + compressed(out)).astype(LOW)
        lane = lax.broadcasted_iota(jnp.int32, sums_ref.shape, 1)
        sums_ref[...] += jnp.where(lane == 1, square_sum(output, seg_ref[0][:, tokens] > 0), 0.0)
        keep_out[:, tokens] = jnp.where(on_attention, middle, output)
        send_out[:, tokens] = jnp.where(on_attention, output, middle)
        normed, inverse = crms(wide)
        grad = (cot_ref[0, :, tokens].astype(FULL) + widened_back(crms_back(normed, inverse, grad))).astype(LOW)
        gmid_ref[:, tokens] = grad
        gab_ref[:, tokens] = compressed_back(grad).astype(LOW)

    in_stages(chunks(length, 2), (multiply, finish))


def output_of(where, acts, grads, ups, down_weight, middle, cot, segments, after=()):
    width, length = middle.shape
    steps = 2
    block = length // steps
    spec = tokens_spec(width, block)
    pair = pl.BlockSpec((2, width, block), lambda t, w: (0, 0, t))
    row = jax.ShapeDtypeStruct((width, length), LOW)
    return kernel_call(
        output_kernel,
        "output",
        pltpu.PrefetchScalarGridSpec(
            num_scalar_prefetch=1,
            grid=(steps,),
            in_specs=[pair] * 4
            + [pl.BlockSpec((2, width, width), lambda t, w: (0, 0, 0), pipeline_mode=pl.Buffered(1))] * 2
            + [pl.BlockSpec(down_weight.shape, lambda t, w: (0, 0), pipeline_mode=pl.Buffered(1))]
            + [spec, row_spec(width, block)]
            + [pl.BlockSpec((1, 1, block), lambda t, w: (w[0], 0, t))]
            + [pl.BlockSpec(memory_space=pltpu.HBM)] * len(after),
            out_specs=[spec] * 4 + [whole((8, 128))],
        ),
        [row] * 4 + [jax.ShapeDtypeStruct((8, 128), FULL)],
        20e9,
        24 * length * width,
        vmem=40,
    )(where, *acts, *grads, *ups, down_weight, middle, cot, segments, *after)


def mixed_grad_kernel(where_ref, gab_ref, w_ref, *refs):
    mixed_refs, gm_refs, (delta_ref, keep_ref, send_ref, mixed_all) = refs[:GROUPS], refs[-GROUPS - 4 : -4], refs[-4:]
    gab = gab_ref[...]
    part = gm_refs[0].shape[0]
    heads = part // HEAD_DIM
    for group in range(GROUPS):
        rows = slice(group * part, (group + 1) * part)
        grads = dot(w_ref[rows, :], gab).astype(LOW)
        gm_refs[group][...] = grads
        mixed = mixed_refs[group][...]
        mixed_all[rows, :] = mixed
        product = grads.astype(FULL) * mixed.astype(FULL)
        for head in range(heads):
            delta_ref[group, head : head + 1, :] = jnp.sum(
                product[head * HEAD_DIM : (head + 1) * HEAD_DIM], axis=0, keepdims=True
            )
    for place, rows in halves(where_ref, mixed_all.shape[0]):
        (keep_ref, send_ref)[place][...] = dot(mixed_all[rows, :], gab, 1, 1).astype(LOW)


def mixed_grad(where, gab, w, mixed, after=()):
    width, length = gab.shape
    part = width // GROUPS
    heads = part // HEAD_DIM
    outs = kernel_call(
        mixed_grad_kernel,
        "mixed_grad",
        pltpu.PrefetchScalarGridSpec(
            num_scalar_prefetch=1,
            grid=(1,),
            in_specs=[whole((width, length)), whole((width, width))]
            + [whole((part, length))] * GROUPS
            + [pl.BlockSpec(memory_space=pltpu.HBM)] * len(after),
            out_specs=[whole((part, length))] * GROUPS
            + [whole((GROUPS, heads, length))]
            + [whole((width // 2, width))] * 2,
            scratch_shapes=[pltpu.VMEM((width, length), LOW)],
        ),
        [jax.ShapeDtypeStruct((part, length), LOW)] * GROUPS
        + [jax.ShapeDtypeStruct((GROUPS, heads, length), FULL)]
        + [jax.ShapeDtypeStruct((width // 2, width), LOW)] * 2,
        4 * length * width * width,
        8 * length * width,
        vmem=28,
    )(where, gab, w, *mixed, *after)
    return outs[:GROUPS], outs[GROUPS], outs[GROUPS + 1], outs[GROUPS + 2]


def input_grad_kernel(where_ref, x_ref, gmid_ref, *refs):
    grad_refs, w_refs, (keep_ref, *send_refs) = refs[:GROUPS], refs[GROUPS : 2 * GROUPS], refs[-3:]
    on_attention = where_ref[0] == 0
    grad_normed = dot(w_refs[0][...], grad_refs[0][...])
    for group in range(1, GROUPS):
        grad_normed = grad_normed + dot(w_refs[group][...], grad_refs[group][...])
    normed, inverse = crms(widened(x_ref[0]))
    middle = gmid_ref[...]
    grad = (middle.astype(FULL) + widened_back(crms_back(normed, inverse, grad_normed))).astype(LOW)
    keep_ref[...] = jnp.where(on_attention, grad, middle)
    sent = jnp.where(on_attention, middle, grad)
    for part, send_ref in enumerate(send_refs):

        @pl.when((pl.program_id(0) > 0) == (part == 1))
        def _(send_ref=send_ref):
            send_ref[...] = sent


def input_grad(where, x, grad_middle, grads, weights, after=()):
    width, length = grad_middle.shape
    spec = tokens_spec(width, length // 4)
    return kernel_call(
        input_grad_kernel,
        "input_grad",
        pltpu.PrefetchScalarGridSpec(
            num_scalar_prefetch=1,
            grid=(4,),
            in_specs=[row_spec(width, length // 4), spec]
            + [spec] * GROUPS
            + [whole((width, width))] * GROUPS
            + [pl.BlockSpec(memory_space=pltpu.HBM)] * len(after),
            out_specs=[
                spec,
                pl.BlockSpec((width, length // 4), lambda t, w: (0, 0)),
                pl.BlockSpec((width, length // 4), lambda t, w: (0, jnp.maximum(t - 1, 0))),
            ],
        ),
        [jax.ShapeDtypeStruct((width, tokens), LOW) for tokens in (length, length // 4, length - length // 4)],
        6 * length * width * width,
        12 * length * width,
        vmem=30,
    )(where, x, grad_middle, *grads, *weights, *after)


def rows_kernel(where_ref, kept_ref, *refs):
    other_refs, out_ref = refs[:-1], refs[-1]
    kept = kept_ref[...].astype(FULL)
    other = other_refs[0][...].astype(FULL)
    if len(other_refs) > 1:
        other = jnp.where(pl.program_id(0) == 0, other, other_refs[1][...].astype(FULL))
    mine = where_ref[0] == 0
    both = jnp.stack([jnp.where(mine, kept, other), jnp.where(mine, other, kept)], axis=1).astype(LOW)
    out_ref[...] = both[: out_ref.shape[0]]


def rows_of(where, kept, others, after=()):
    width, length = kept.shape
    block = length // 4
    places = [lambda t, w: (0, t)] if len(others) == 1 else [lambda t, w: (0, 0), lambda t, w: (0, jnp.maximum(t - 1, 0))]

    def body(where_ref, *refs):
        rows_kernel(where_ref, *refs[: 1 + len(others)], refs[-1])

    out = kernel_call(
        body,
        "rows",
        pltpu.PrefetchScalarGridSpec(
            num_scalar_prefetch=1,
            grid=(4,),
            in_specs=[tokens_spec(width, block)]
            + [pl.BlockSpec((width, block), place) for place in places]
            + [pl.BlockSpec(memory_space=pltpu.HBM)] * len(after),
            out_specs=pl.BlockSpec((width - 1, 2, block), lambda t, w: (0, 0, t)),
        ),
        pltpu.HBM((width - 1, 2, length), LOW),
        2e10,
        length,
        vmem=40,
    )(where, kept, *others, *after)
    return jnp.transpose(out, (1, 2, 0))[None]


def partner(block, distance):
    size = lax.axis_size("dp")
    return lax.ppermute(block, "dp", [(i, i ^ distance) for i in range(size)])


def across(block):
    return lax.ppermute(block, "section", [(0, 1), (1, 0)])


def split(left, right, distance):
    bit = (lax.axis_index("dp") & distance) // distance
    half = left.shape[1] // 2
    part = lambda a, at: lax.dynamic_slice_in_dim(a, at * half, half, 1)
    return add_low(part(left, bit), part(right, bit)), add_low(part(left, 1 - bit), part(right, 1 - bit))


def add_low(left, right):
    return (left.astype(FULL) + right.astype(FULL)).astype(LOW)


class Scatter:
    def __init__(self, keep, got, order):
        self.order = order
        self.keep, self.got = keep, got
        self.at = 0

    def step(self, *others):
        self.at += 1
        self.got = later(self.got, *others)
        self.keep, self.sent = split(self.keep, self.got, self.order[self.at])
        self.got = partner(self.sent, self.order[self.at])

    def total(self, *others):
        while self.at < len(self.order) - 1:
            self.step(*others)
        return add_low(self.keep, later(self.got, *others))


class Gather:
    def __init__(self, shard, order, *others):
        self.left = list(reversed(order))
        self.held = later(shard, *others)[None] if others else shard[None]
        self.got = partner(self.held, self.left.pop(0))

    def step(self, *others):
        self.held = jnp.concatenate([self.held, later(self.got, *others)], axis=0)
        self.got = partner(self.held, self.left.pop(0))

    def all(self, *others):
        while self.left:
            self.step(*others)
        return self.held, self.got


def number_of(order):
    me = lax.axis_index("dp").astype(jnp.int32)
    number = jnp.int32(0)
    for distance in order:
        number = number * 2 + (me // distance) % 2
    return number


def later(value, *others):
    return lax.optimization_barrier((value, *others))[0]


def gathered_specs(array, per_step):
    half_steps = array.shape[0] // per_step
    block = (per_step, *array.shape[1:])
    return [
        pl.BlockSpec(block, lambda e, w: (jnp.minimum(e, half_steps - 1), 0, 0)),
        pl.BlockSpec(block, lambda e, w: (jnp.maximum(e - half_steps, 0), 0, 0)),
    ]


def each_entry(number_ref, halves_refs, do):
    steps = pl.num_programs(0)
    per_step = halves_refs[0].shape[0]
    for place, ref in enumerate(halves_refs):

        @pl.when((pl.program_id(0) * 2 >= steps) == (place == 1))
        def _(ref=ref):
            for entry in range(per_step):
                do((number_ref[1] % per_step) ^ entry, ref, entry)


def down_sum_kernel(number_ref, near_ref, far_ref, out_ref):
    rows = out_ref.shape[2]

    def write(place, ref, entry):
        for block in range(2):
            out_ref[block, place] = ref[entry, block * rows : (block + 1) * rows, :].astype(FULL)

    each_entry(number_ref, (near_ref, far_ref), write)


def down_sum(number, near, far, width):
    entries = 2 * near.shape[0]
    rows = width // entries
    per_step = entries // 4
    out = kernel_call(
        down_sum_kernel,
        "down_sum",
        pltpu.PrefetchScalarGridSpec(
            num_scalar_prefetch=1,
            grid=(4,),
            in_specs=gathered_specs(near, per_step),
            out_specs=pl.BlockSpec((2, per_step, rows, width), lambda e, w: (0, (w[1] // per_step) ^ e, 0, 0)),
        ),
        jax.ShapeDtypeStruct((2, entries, rows, width), FULL),
        2e10,
        width,
        vmem=58,
    )(number, near, far)
    return out.reshape(2 * width, width)


def columns_of(numbers):
    if numbers[0] < 0:
        return [[(0, 3 * block, 3)] for block in (-numbers[0] - 1, -numbers[1] - 1)]
    return [
        [(0, 9, 3)] if block == 0 else [(piece, own_column_static(block - 1, piece, 0), 1) for piece in range(3)]
        for block in numbers
    ]


def counts_of(section, slots, width, near_ref, far_ref):
    rows = sum(ref[entry, :16, :128].astype(FULL) for ref in (near_ref, far_ref) for entry in range(ref.shape[0]))
    lane = lax.broadcasted_iota(jnp.int32, (1, 128), 1)
    total = [
        jnp.sum(jnp.where((lane % 3 == which) & (lane < 9), rows[:1], 0.0), axis=1, keepdims=True) for which in range(3)
    ]
    square = jnp.where(section == 0, total[0], total[1])
    count = jnp.where(section == 0, total[2], slots - total[2])
    root = jnp.sqrt(square / (total[2] * width))
    return jnp.broadcast_to(jnp.where(lane == 0, root, jnp.where(lane == 1, count, 0.0)), (8, 128))


def first_sum_kernel(skip, blocks, slots, number_ref, near_ref, far_ref, *refs):
    buffer, sem = refs[-2:]
    out_ref = refs[-4] if slots else refs[-3]
    entries, rows, columns = out_ref.shape
    width = columns // 4
    part = width // 3
    half = entries // 2
    if slots:
        refs[-3][...] = counts_of(number_ref[0], slots, width, near_ref, far_ref)
    for section in range(2):

        @pl.when(number_ref[0] == section)
        def _(section=section):
            pieces = columns_of(blocks[section])

            def copies(place, do):
                first = pl.multiple_of(jnp.where(number_ref[1] < half, place, 1 - place) * half, half)
                for at in range(2):
                    for order, (start, column, size) in enumerate(pieces[at]):
                        do(
                            pltpu.make_async_copy(
                                buffer.at[at, pl.ds(first, half), :, pl.ds(start * part, size * part)],
                                out_ref.at[pl.ds(first, half), :, pl.ds(column * part, size * part)],
                                sem.at[place, at, order],
                            )
                        )

            for place, ref in enumerate((near_ref, far_ref)):
                for entry in range(half):
                    for at in range(2):
                        values = ref[entry, skip + at * rows : skip + (at + 1) * rows, :]
                        buffer[at, number_ref[1] ^ (entry + place * half)] = values.astype(FULL)
                copies(place, lambda c: c.start())
            for place in range(2):
                copies(place, lambda c: c.wait())


def first_sum(number, skip, blocks, gathered, width, before=None, slots=None):
    near, far = gathered
    entries = 2 * near.shape[0]
    rows = width // entries
    held = [] if before is None else [before]
    anywhere = pl.BlockSpec(memory_space=pl.ANY)
    return pl.pallas_call(
        functools.partial(first_sum_kernel, skip, blocks, slots),
        grid_spec=pltpu.PrefetchScalarGridSpec(
            num_scalar_prefetch=1,
            grid=(1,),
            in_specs=[whole(near.shape), whole(far.shape)] + [anywhere] * len(held),
            out_specs=[anywhere] + [whole((8, 128))] * bool(slots),
            scratch_shapes=[pltpu.VMEM((2, entries, rows, width), FULL), pltpu.SemaphoreType.DMA((2, 2, 3))],
        ),
        out_shape=[jax.ShapeDtypeStruct((entries, rows, 4 * width), FULL)]
        + [jax.ShapeDtypeStruct((8, 128), FULL)] * bool(slots),
        input_output_aliases={3: 0} if held else {},
        compiler_params=pltpu.CompilerParams(vmem_limit_bytes=24 * 2**20),
        cost_estimate=pl.CostEstimate(flops=1000, bytes_accessed=1000, transcendentals=0),
        name="first_sum",
    )(number, near, far, *held)


def on_device(stream_in, cotangent, weights_first, down_weight, segments):
    rows_dev, length, compact_width = stream_in.shape
    width = compact_width + 1
    section = lax.axis_index("section").astype(jnp.int32)
    index = lax.axis_index("dp").astype(jnp.int32)
    size = lax.axis_size("dp")
    on_attention = section == 0
    where = jnp.stack([section, index & 3, index & 1])
    segments3 = segments.reshape(rows_dev, 1, length)
    order = [1 << i for i in range(size.bit_length() - 1)]
    flat = lambda a: a.reshape(-1, width)

    near = [across(piece) for piece in weight_piece(where, weights_first)]
    x, cot = jnp.transpose(stream_in, (0, 2, 1)), jnp.transpose(cotangent, (0, 2, 1))
    nt, g = prep(where, x, cot)
    ga = branch_grad(g, down_weight, after=(near[0],))
    attended, received, besides = [], [], [partner(later(near[0], nt), 2), partner(later(near[1], ga), 2)]
    for group in range(4):
        quarter, beside = near[group], besides[group]
        done = [attended[group - 1][1] if group else ga]
        received.append((quarter, beside, partner(quarter, 1), partner(later(beside, *done), 1)))
        if group < 2:
            besides.append(partner(later(near[group + 2], *done), 2))
        if group < GROUPS:
            attended.append(attend(group, where, weights_first, received[group], nt, segments3))
    mixed = [a[1] for a in attended]
    middle, nm, sums_mid, out_weights = middle_of(where, weights_first, received[GROUPS], mixed, x, segments3)

    act_a, grad_a, weights_a, keep_a, send_a, *down_a = hidden_of(0, where, weights_first, received[0::2], nm, ga, g)
    up_a, got_a = partner(send_a, 1), partner(down_a[1], 1)
    act_b, grad_b, weights_b, keep_b, send_b, *down_b = hidden_of(
        1, where, weights_first, received[1::2], nm, ga, g, after=(act_a,)
    )
    up_b, got_b = partner(send_b, 1), partner(down_b[1], 1)
    halves_a, halves_b = split(keep_a, up_a, order[1]), split(keep_b, up_b, order[1])
    up = Scatter(keep_a, up_a, order)
    up.keep, up.sent = (jnp.concatenate(both) for both in zip(halves_a, halves_b, strict=True))
    up.at, up.got = 1, partner(up.sent, order[1])
    kept, sent = [], []
    for keep, got in ((down_a[0], got_a), (down_b[0], got_b)):
        lower, upper = add_low(keep[0], got[0]), add_low(keep[1], got[1])
        kept.append(jnp.where(on_attention, lower, upper))
        sent.append(jnp.where(on_attention, upper, lower))
    kept, sent = jnp.stack(kept), later(jnp.stack(sent), up.sent)
    down = Scatter(kept, across(sent), order)
    keep_out, send_out, grad_mid, gab, sums_out = output_of(
        where, (act_a, act_b), (grad_a, grad_b), (weights_a, weights_b), down_weight, middle, cot, segments3, after=(sent,)
    )
    up.step(gab)
    gm, delta, keep_w, send_w = mixed_grad(where, gab, out_weights, mixed, after=(up.sent,))
    keeps, sends, grads = [keep_w], [send_w], []

    def backward(group, *after):
        qkv, _, total, _ = attended[group]
        keep_w, send_w, grad = attend_back(where, qkv, gm[group], total, delta[group], segments3, nt, after=after)
        keeps.append(keep_w)
        sends.append(send_w)
        grads.append(grad)

    down.step(delta)
    backward(0, down.sent)
    up.step(grads[0])
    down.step(up.sent)
    sent_a = later(jnp.stack(sends), down.sent)
    attn_a = Scatter(jnp.stack(keeps), partner(sent_a, 1), order)
    backward(1, sent_a)
    attn_a.step(grads[1])
    down.step(attn_a.sent)
    received_out = across(send_out)
    backward(2, down.sent)
    down = down.total(grads[2])
    sum_dn = Gather(flat(down), order)
    up = up.total(sum_dn.held)
    up_a, up_b, rows = up[:2], up[2:], up.shape[1]
    attn_a.step(up)
    attn_b = Scatter(jnp.stack(keeps[2:]), partner(later(jnp.stack(sends[2:]), attn_a.sent), 1), order)
    attn_b.step()
    keep_grad, *send_grad = input_grad(
        where, x, grad_mid, grads, [a[3] for a in attended], after=(attn_b.sent, received_out)
    )
    attn_a.step(keep_grad)
    attn_b.step(attn_a.sent)
    sum_dn.step(attn_b.sent)
    attn_a = attn_a.total(sum_dn.held)

    scalars = (sums_mid + sums_out)[0, :3]

    def scalar_rows(values):
        high = values.astype(LOW)
        rest = values - high.astype(FULL)
        middle_part = rest.astype(LOW)
        low = (rest - middle_part.astype(FULL)).astype(LOW)
        packed = jnp.concatenate([high, middle_part, low])
        return jnp.zeros((16, width), LOW).at[0, :9].set(packed)

    def scalars_of(block):
        parts = block[..., 0, :9].astype(FULL)
        return parts[..., :3] + parts[..., 3:6] + parts[..., 6:9]

    mine_a, theirs_a = jnp.where(on_attention, attn_a, up_a), jnp.where(on_attention, up_a, attn_a)
    sent_a = jnp.concatenate([scalar_rows(scalars), flat(theirs_a)])
    swapped = across(sent_a)
    attn_b.step(sent_a)
    swapped = later(swapped, attn_b.sent)
    pair = scalars + scalars_of(swapped[:16])
    shard_a = add_low(flat(mine_a), swapped[16:])
    sum_a = Gather(jnp.concatenate([scalar_rows(pair), shard_a]), order)
    received_grad = [across(later(send_grad[0], sum_a.held))]
    sum_dn.step(sum_a.held)
    received_grad[0] = later(received_grad[0], sum_dn.held)
    attn_b = attn_b.total(received_grad[0])
    mine_b, theirs_b = jnp.where(on_attention, attn_b, up_b), jnp.where(on_attention, up_b, attn_b)
    swapped_b = across(flat(theirs_b))
    received_grad.append(across(later(send_grad[1], theirs_b)))
    sum_a.step(theirs_b)
    stream_out = rows_of(where, keep_out, [received_out], after=(sum_a.held,))
    sum_b = Gather(add_low(flat(mine_b), later(swapped_b, stream_out)), order)
    sum_a.step(sum_b.held)
    sum_dn.step(sum_a.held)
    number = jnp.stack([section, number_of(order)])
    grad_down = down_sum(later(number, sum_dn.held), *sum_dn.all(), width)
    sum_b.step(grad_down)
    sum_b.step(sum_a.got)
    sum_a.step(sum_b.held)
    stream_grad = rows_of(where, keep_grad, received_grad, after=(sum_a.held,))
    sum_b.step(stream_grad)
    sum_a, sum_b = sum_a.all(), sum_b.all()
    slots = float(rows_dev * length * size)
    grad_first, counts = first_sum(later(number, sum_b[0]), 16, ((0, 1), (-1, -3)), sum_a, width, slots=slots)
    (grad_first,) = first_sum(number, 0, ((2, 3), (-2, -4)), sum_b, width, before=grad_first)
    grad_first = grad_first.reshape(width, 4 * width)
    residual_rms, token_count = counts[0, :1], counts[0, 1:2].astype(jnp.int32)
    return (
        stream_out,
        stream_grad,
        grad_first[None],
        grad_down,
        residual_rms,
        token_count,
    )


def solution(mesh):
    placed = (
        P("dp", None, None),
        P("dp", None, None),
        P("section", None, None),
        P(),
        P("dp", None),
    )
    return jax.shard_map(
        on_device,
        mesh=mesh,
        in_specs=placed,
        out_specs=(
            P("section", "dp", None, None),
            P("section", "dp", None, None),
            P("section", None, None),
            P("section", None),
            P("section"),
            P("section"),
        ),
        check_vma=False,
    )
```
